32 devices in a mesh: groups: 2 (over x), tiles: 16 (over z, y, core).
Axes of the slice: x: 2, y: 2, z: 4, core: 2. Of those that a mesh axis runs over, the one named last changes fastest.
Arguments:
- video_q: bfloat16 [8192, 3072], P(('groups', 'tiles')), parts along dimension 0, may hold values from -88 to 88, as said below
- video_k: bfloat16 [8192, 3072], P(('groups', 'tiles')), parts along dimension 0, may hold values from -4 to 4, as said below
- video_v: bfloat16 [8192, 3072], P(('groups', 'tiles')), parts along dimension 0, may hold values from -5 to 5
- text_q: bfloat16 [512, 3072], P('groups'), parts along dimension 0, may hold values from -88 to 88
- text_k: bfloat16 [512, 3072], P('groups'), parts along dimension 0, may hold values from -5 to 5
- text_v: bfloat16 [512, 3072], P('groups'), parts along dimension 0, may hold values from -5 to 5
- window: int32 [32, 6], P('tiles'), may hold values from 0 to 13, as said below
- counts: int32 [64], P(('groups', 'tiles')), parts along dimension 0, may hold values from 1 to 128, as said below
- text_count: int32 [2], P('groups'), parts along dimension 0, may hold values from 64 to 256
Outputs:
- video_out: bfloat16 [8192, 3072], P(('groups', 'tiles')), parts along dimension 0
- text_out: bfloat16 [512, 3072], P(('groups', 'tiles')), parts along dimension 0
The draws below stay inside these ranges and needn't reach their ends.
There are 2 independent parts, one for each index of `groups`. The reference program is written for one: setup_inputs(seed, part) draws one part's arguments, and reference() takes and returns one part's arrays. A program takes and returns all parts, laid end to end along the dimension named above; an argument that names none is the same for every part. Nothing has to cross between parts.
Inputs may be any that keep to these rules, and one draw needn't show every extreme that they name: `video_q`: queries drawn for the problem. `video_k`: keys drawn for the problem. `window`: each row names 6 different codes, among them always 3, 6, 9 and 12. `counts`: valid tokens are the first slots of a tile.
All inputs are finite; a program needn't handle non-finite values.
Results may differ from the reference program's by a relative error of at most 0.003.
Values may be sent and summed in bfloat16 or wider, within the bound.
A program may use at most 192 MiB of HBM per device.

```python
import math
import jax
import jax.numpy as jnp
from jax import lax

HEADS = 24
HD = 128
D = 3072
TOK = 128
CT = 2
NR = 4
WIN = 6
TEXT = 256
TILES_ALL = 32
VIDEO = 4096
N_TILES = 16


def base_keys(key):
    keys_drawn = jnp.clip(jax.random.normal(jax.random.fold_in(key, 11), (VIDEO, D), jnp.float32), -4.0, 4.0)
    return keys_drawn


def draw_video_k(key, part):
    return base_keys(key).astype(jnp.bfloat16)


def draw_video_q(key, part):
    drawn = 2.5 * jnp.clip(jax.random.normal(jax.random.fold_in(key, 23), (VIDEO, D), jnp.float32), -4.0, 4.0)
    return drawn.astype(jnp.bfloat16)


def draw_text_q(key, part):
    drawn = 3.5 * jnp.clip(jax.random.normal(jax.random.fold_in(key, 37), (TEXT, D), jnp.float32), -4.0, 4.0)
    return drawn.astype(jnp.bfloat16)


def draw_window(key, part):
    fixed_codes = jnp.broadcast_to(jnp.array([3, 6, 9, 12], jnp.int32), (TILES_ALL, 4))
    other_codes = jnp.array([0, 1, 2, 4, 5, 7, 8, 10, 11, 13], jnp.int32)
    scores = jax.random.randint(jax.random.fold_in(key, 61), (TILES_ALL, 10), 0, 1 << 20, dtype=jnp.int32)
    scores = scores * 16 + jnp.arange(10, dtype=jnp.int32)[None, :]
    _, picked = lax_top(-scores)
    extra = other_codes[picked]
    return jnp.concatenate([fixed_codes, extra], axis=1)[:, :WIN].astype(jnp.int32)


def lax_top(values):
    return jax.lax.top_k(values, WIN - 4)


def draw_counts(key, part):
    tile_ids = jnp.arange(TILES_ALL, dtype=jnp.int32)
    device = tile_ids // CT
    column = tile_ids % CT
    tiles_devices = TILES_ALL // CT
    row_block = (device + tiles_devices // 2 + NR + NR // 2) % tiles_devices % NR
    edge = (row_block == NR - 1) | (column == CT - 1)
    drawn = jax.random.randint(jax.random.fold_in(key, 5), (TILES_ALL,), 1, TOK + 1, dtype=jnp.int32)
    return jnp.where(edge, drawn, TOK).astype(jnp.int32)


def draw_text_count(key, part):
    drawn = jax.random.randint(jax.random.fold_in(key, 41), (1,), TEXT // 4, TEXT, dtype=jnp.int32)
    return jnp.where(part % 2 == 1, TEXT, drawn).astype(jnp.int32)


def level_of(own_key, dims, pieces, smallest, top_value):
    factor_of = 1.0
    for position, shards_of in pieces:
        heights = jax.random.uniform(jax.random.fold_in(jax.random.fold_in(own_key, 6), position), (shards_of,), jnp.float32, smallest / len(pieces), top_value / len(pieces))
        factor_of = factor_of * jnp.repeat(jnp.exp(heights), dims[position] // shards_of).reshape((-1,) + (1,) * (len(dims) - 1 - position))
    return factor_of


def normal_values(rng, extent, scale, limit, split=(), kind=jnp.bfloat16):
    values = scale * jax.random.normal(rng, extent, jnp.float32)
    if split:
        values = values * level_of(rng, extent, split, -0.22, 0.18)
    return jnp.clip(values, -limit, limit).astype(kind)


def setup_inputs(seed: int = 0, part: int = 0) -> dict:
    key_of = jax.random.split(jax.random.key(seed), 10)
    part_splits = jax.random.split(jax.random.fold_in(key_of[9], part), 10)
    video_q = draw_video_q(jax.random.fold_in(jax.random.fold_in(key_of[9], part), 71), part)
    video_k = draw_video_k(jax.random.fold_in(jax.random.fold_in(key_of[9], part), 71), part)
    video_v = normal_values(part_splits[2], (VIDEO, D), 1.0, 5.0, ((0, 16),))
    text_q = draw_text_q(jax.random.fold_in(jax.random.fold_in(key_of[9], part), 71), part)
    text_k = normal_values(part_splits[4], (TEXT, D), 1.0, 5.0)
    text_v = normal_values(part_splits[5], (TEXT, D), 1.0, 5.0)
    window = draw_window(jax.random.fold_in(key_of[9], 71), part)
    counts = draw_counts(jax.random.fold_in(jax.random.fold_in(key_of[9], part), 71), part)
    text_count = draw_text_count(jax.random.fold_in(jax.random.fold_in(key_of[9], part), 71), part)
    return dict(video_q=video_q, video_k=video_k, video_v=video_v, text_q=text_q, text_k=text_k, text_v=text_v, window=window, counts=counts, text_count=text_count)


def reference(video_q, video_k, video_v, text_q, text_k, text_v, window, counts, text_count):
    score_scale = 1.0 / math.sqrt(HD)
    devices_all = N_TILES
    blocks_time = devices_all // NR
    layout_shift = devices_all // 2 + NR + NR // 2
    spread = ((1, 1), (1, 1), (1, 1), (0, 0), (0, 0), (0, 0))
    key_rolled = jnp.roll(video_k.reshape(devices_all, CT, TOK, HEADS, HD), layout_shift, axis=0)
    value_rolled = jnp.roll(video_v.reshape(devices_all, CT, TOK, HEADS, HD), layout_shift, axis=0)
    count_rolled = jnp.roll(counts.reshape(devices_all, CT), layout_shift, axis=0)
    key_grid = jnp.pad(key_rolled.reshape(blocks_time, NR, CT, TOK, HEADS, HD), spread)
    value_grid = jnp.pad(value_rolled.reshape(blocks_time, NR, CT, TOK, HEADS, HD), spread)
    count_grid = jnp.pad(count_rolled.reshape(blocks_time, NR, CT), ((1, 1), (1, 1), (1, 1)))
    query_tiles = video_q.reshape(devices_all, CT, TOK, HEADS, HD)
    window_rows = window.reshape(devices_all, CT, WIN)
    count_rows = counts.reshape(devices_all, CT)
    text_valid = jnp.arange(TEXT, dtype=jnp.int32) < text_count[0]
    time_step = jnp.array([0, -1, 1, 0, 0], jnp.int32)
    row_step = jnp.array([0, 0, 0, -1, 1], jnp.int32)
    text_keys = text_k.reshape(TEXT, HEADS, HD).astype(jnp.float32)
    text_values = text_v.reshape(TEXT, HEADS, HD).astype(jnp.float32)
    slot_ids = jnp.arange(TOK, dtype=jnp.int32)

    def one_device(device):
        spot = ((device + layout_shift) % devices_all).astype(jnp.int32)
        tblock = (spot // NR).astype(jnp.int32)
        rblock = (spot % NR).astype(jnp.int32)
        zero_at = jnp.zeros((), jnp.int32)
        key_near = lax.dynamic_slice(key_grid, (tblock, rblock, zero_at, zero_at, zero_at, zero_at), (3, 3, CT + 2, TOK, HEADS, HD))
        value_near = lax.dynamic_slice(value_grid, (tblock, rblock, zero_at, zero_at, zero_at, zero_at), (3, 3, CT + 2, TOK, HEADS, HD))
        count_near = lax.dynamic_slice(count_grid, (tblock, rblock, zero_at), (3, 3, CT + 2))
        window_codes = window_rows[device]
        cell_codes = jnp.concatenate([jnp.ones((CT, 1), jnp.int32), (window_codes + (window_codes >= 1)).astype(jnp.int32)], axis=1)
        block_of = cell_codes // 3
        column_at = jnp.arange(CT, dtype=jnp.int32)[:, None] + cell_codes % 3
        time_at = 1 + time_step[block_of]
        row_at = 1 + row_step[block_of]
        keys_chosen = key_near[time_at, row_at, column_at].reshape(CT, (WIN + 1) * TOK, HEADS, HD).astype(jnp.float32)
        values_chosen = value_near[time_at, row_at, column_at].reshape(CT, (WIN + 1) * TOK, HEADS, HD).astype(jnp.float32)
        counts_chosen = count_near[time_at, row_at, column_at]
        key_valid = (slot_ids[None, None, :] < counts_chosen[:, :, None]).reshape(CT, (WIN + 1) * TOK)
        queries = query_tiles[device].astype(jnp.float32)
        video_scores = jnp.einsum('cqhd,ckhd->chqk', queries, keys_chosen) * score_scale
        video_scores = jnp.where(key_valid[:, None, None, :], video_scores, -jnp.inf)
        text_scores = jnp.einsum('cqhd,khd->chqk', queries, text_keys) * score_scale
        text_scores = jnp.where(text_valid[None, None, None, :], text_scores, -jnp.inf)
        row_top = jnp.maximum(lax.optimization_barrier(jnp.max(video_scores, axis=-1)), lax.optimization_barrier(jnp.max(text_scores, axis=-1)))[..., None]
        video_probs = jnp.exp(video_scores - row_top)
        text_probs = jnp.exp(text_scores - row_top)
        denom = lax.optimization_barrier(jnp.sum(video_probs, axis=-1)) + lax.optimization_barrier(jnp.sum(text_probs, axis=-1))
        video_round = lax.optimization_barrier(video_probs.astype(jnp.bfloat16)).astype(jnp.float32)
        text_round = lax.optimization_barrier(text_probs.astype(jnp.bfloat16)).astype(jnp.float32)
        numer = jnp.einsum('chqk,ckhd->cqhd', video_round, values_chosen) + jnp.einsum('chqk,khd->cqhd', text_round, text_values)
        result = numer / jnp.transpose(denom, (0, 2, 1))[..., None]
        query_valid = slot_ids[None, :] < count_rows[device][:, None]
        return jnp.where(query_valid[:, :, None, None], result, 0.0).astype(jnp.bfloat16)
    device_ids = jnp.arange(devices_all, dtype=jnp.int32)
    video_out = lax.map(one_device, device_ids).reshape(VIDEO, D)
    key_blocks = video_k.reshape(devices_all, CT * TOK, HEADS, HD)
    value_blocks = video_v.reshape(devices_all, CT * TOK, HEADS, HD)
    valid_blocks = (slot_ids[None, None, :] < count_rows[:, :, None]).reshape(devices_all, CT * TOK)
    text_queries = text_q.reshape(TEXT, HEADS, HD).astype(jnp.float32)

    def block_scores(device):
        scores = jnp.einsum('qhd,khd->hqk', text_queries, key_blocks[device].astype(jnp.float32)) * score_scale
        return jnp.where(valid_blocks[device][None, None, :], scores, -jnp.inf)

    def block_top(device):
        return lax.optimization_barrier(jnp.max(block_scores(device), axis=-1))
    global_top = lax.optimization_barrier(jnp.max(lax.map(block_top, device_ids), axis=0))

    def accumulate(carry, device):
        weights = jnp.exp(block_scores(device) - global_top[..., None])
        denom_part = lax.optimization_barrier(jnp.sum(weights, axis=-1))
        weights_round = lax.optimization_barrier(weights.astype(jnp.bfloat16)).astype(jnp.float32)
        numer_part = jnp.einsum('hqk,khd->qhd', weights_round, value_blocks[device].astype(jnp.float32))
        return ((carry[0] + numer_part, carry[1] + denom_part.T), None)
    start_sums = (jnp.zeros((TEXT, HEADS, HD), jnp.float32), jnp.zeros((TEXT, HEADS), jnp.float32))
    (numer_all, denom_all), _ = lax.scan(accumulate, start_sums, device_ids)
    text_result = numer_all / denom_all[..., None]
    text_out = jnp.where(text_valid[:, None, None], text_result, 0.0).astype(jnp.bfloat16).reshape(TEXT, D)
    return (video_out, text_out)
```

```python
import functools
import math

import jax
import jax.numpy as jnp
from jax import lax
from jax.experimental import pallas as pl
from jax.experimental.pallas import tpu as pltpu
from jax.sharding import PartitionSpec as P

HD = 128
NR = 4
WIDTH = 256
PER = WIDTH // HD
AHEAD = 4
LOG2E_SCALE = math.log2(math.e) / math.sqrt(HD)
MESH = pl.DeviceIdType.MESH
NT = (((1,), (1,)), ((), ()))
NEG = -jnp.inf


def softmax_block(q, blocks, half):
    scores = []
    for key, _, bias in blocks:
        s = lax.dot_general(q, key, NT, preferred_element_type=jnp.float32)
        scores.append(
            jnp.concatenate([s[:half] + bias[0:1, :], s[half:] + bias[1:2, :]], axis=0)
        )
    top = functools.reduce(jnp.maximum, scores)
    top = jnp.max(top, axis=1, keepdims=True)
    total, num = None, None
    for s, (_, value, _) in zip(scores, blocks):
        p = jnp.exp2((s - top) * LOG2E_SCALE)
        total = p if total is None else total + p
        term = jnp.dot(p.astype(jnp.bfloat16), value, preferred_element_type=jnp.float32)
        num = term if num is None else num + term
    return num / jnp.sum(total, axis=1, keepdims=True)


def main_kernel(
    n, fold,
    q_hbm, k_hbm, v_hbm, tq_hbm, tk_hbm, tv_hbm, window_ref, counts_ref, tcount_ref,
    out_ref, tout_ref,
    q_ref, k_ref, v_ref, tq_ref, tk_ref, tv_ref,
    own_ref, bias_ref, qv_ref, near, near_bias,
    relay, far_bias, far_q, side, far_out, back,
    tnum, tstat, ynum, ystat, snum, sstat, rnum, rstat,
    load_sem, send_sem, recv_sem, bsend_sem, brecv_sem, fsend_sem, rsend_sem, rrecv_sem,
    qsend_sem, qrecv_sem, xsend_sem, xrecv_sem, osend_sem, orecv_sem,
    ysend_sem, yrecv_sem, zsend_sem, zrecv_sem,
):
    group = lax.axis_index("groups")
    me = lax.axis_index("tiles")
    last = n // NR - 1
    tokens, width = q_hbm.shape
    chunks = width // WIDTH
    pairs = chunks // 2
    tiles = counts_ref.shape[0]
    tok = tokens // tiles
    half = tokens // 2
    share = tout_ref.shape[0]
    text = tq_hbm.shape[0]
    ahead = min(AHEAD, pairs)

    def at(offset):
        return lax.rem(me + offset + n, n)

    spot = lax.rem(me + n // 2 + NR + NR // 2, n)
    row = lax.rem(spot, NR)
    time = lax.div(spot, NR)
    core = lax.rem(me, 2)
    line = lax.rem(lax.div(me, 2), 2)
    has = (time > 0, time < last, row > 0, row < NR - 1)
    offs = (-NR, NR, -1, 1)
    even = lax.rem(row, 2) == 0
    odd = lax.rem(row, 2) == 1
    is_a = (me == 0) if fold else None
    is_b = (me == 1) if fold else None
    is_c = (me == n - 4) if fold else None
    is_d = (me == n - 3) if fold else None
    is_e = (me == n - 1) if fold else None

    barrier = pltpu.get_barrier_semaphore()

    def greet(i, _):
        pl.semaphore_signal(barrier, inc=1, device_id=(group, at(i)), device_id_type=MESH)
        return 0

    lax.fori_loop(1, n, greet, 0)

    loads = [
        pltpu.make_async_copy(source, target, load_sem.at[i])
        for i, (source, target) in enumerate((
            (k_hbm, k_ref), (tq_hbm, tq_ref), (v_hbm, v_ref),
            (q_hbm, q_ref), (tk_hbm, tk_ref), (tv_hbm, tv_ref),
        ))
    ]
    for copy in loads:
        copy.start()

    lane = lax.broadcasted_iota(jnp.int32, (8, tokens), 1)
    slot = lax.rem(lane, tok)
    count = jnp.full((8, tokens), counts_ref[0], jnp.int32)
    for s in range(1, tiles):
        count = jnp.where(lane >= s * tok, counts_ref[s], count)
    own_ref[...] = jnp.where(slot < count, 0.0, NEG)

    pl.semaphore_wait(barrier, n - 1)

    def remote(source, target, sent, got, to):
        return pltpu.make_async_remote_copy(
            src_ref=source, dst_ref=target, send_sem=sent, recv_sem=got,
            device_id=(group, to), device_id_type=MESH,
        )

    def columns(c):
        return pl.ds(pl.multiple_of(c * WIDTH, WIDTH), WIDTH)

    def block(kv, c):
        return (k_hbm, v_hbm)[kv].at[:, columns(c)]

    def bias_copy(d):
        return remote(own_ref, near_bias.at[d], bsend_sem.at[d], brecv_sem.at[d], at(-offs[d]))

    def direct(d, kv, c):
        return remote(
            block(kv, c), near.at[d, kv, c], send_sem.at[d, kv, c], recv_sem.at[d, kv, c], at(-offs[d])
        )

    def to_relay(d, kv, c):
        return remote(
            block(kv, c), relay.at[kv, c], send_sem.at[d, kv, c], rrecv_sem.at[kv, c], at(1 + kv)
        )

    def from_relay(d, kv, c):
        return remote(
            relay.at[kv, c], near.at[d, kv, c], rsend_sem.at[kv, c], recv_sem.at[d, kv, c],
            at(-1 - kv - offs[d]),
        )

    def forward(d, kv, c):
        slot, to = (2, at(1 - NR)) if d == 0 else (3, at(NR - 1))
        return remote(
            near.at[d, kv, c], near.at[slot, kv, c], fsend_sem.at[kv, c], recv_sem.at[slot, kv, c], to
        )

    def q_direct(j):
        return remote(
            q_hbm.at[:, columns(2 * j)], far_q.at[j], qsend_sem.at[j], qrecv_sem.at[j], at(-NR)
        )

    def q_to_relay(j):
        return remote(
            q_hbm.at[:, columns(2 * j)], relay.at[1, j], qsend_sem.at[j], rrecv_sem.at[1, j], at(2)
        )

    def q_from_relay(j):
        return remote(relay.at[1, j], far_q.at[j], rsend_sem.at[1, j], qrecv_sem.at[j], at(-2 - NR))

    def out_direct(j):
        return remote(far_out.at[j], back.at[j], osend_sem.at[j], orecv_sem.at[j], at(NR))

    def out_to_relay(j):
        return remote(far_out.at[j], relay.at[1, j], osend_sem.at[j], rrecv_sem.at[1, j], at(2))

    def out_from_relay(j):
        return remote(relay.at[1, j], back.at[j], rsend_sem.at[1, j], orecv_sem.at[j], at(2))

    def beside(kv, j):
        return remote(
            near.at[1, kv, 2 * j], side.at[0, kv, j], xsend_sem.at[kv, j], xrecv_sem.at[0, kv, j], at(-1)
        )

    def above(kv, j):
        return remote(
            block(kv, 2 * j), side.at[1, kv, j], xsend_sem.at[kv, j], xrecv_sem.at[1, kv, j], at(-3)
        )

    def far_bias_copy():
        return remote(bias_ref, far_bias, bsend_sem.at[4], brecv_sem.at[4], at(-NR))

    off = jnp.logical_not
    plain_next, plain_prev = time < last, time > 0
    plain_down = (row == 1) & (time == last)
    both = (0, 1)
    early, far, handed, slow, onward = [], [], [], [], []
    if fold:
        relays = ((me == 2) | (me == 3), me == n - 2)
        plain_next = plain_next & (me < n - NR) & off(relays[0])
        plain_prev = plain_prev & (me >= NR) & off(relays[1])
        plain_down = plain_down & off(is_e)
        early = [
            (direct, 0, is_c, both, False),
            (to_relay, 0, is_d, (0,), True),
            (direct, 0, is_d, (1,), True),
            (direct, 2, is_e, both, False),
        ]
        far = [(direct, 1, is_a, both, True)]
        handed = [(to_relay, 1, is_b, both, True)]
        slow = [(direct, 0, relays[0], both, True), (direct, 1, relays[1], both, True)]
        onward = [(me == 2, 1, (0,)), (me == 3, 1, (1,)), (me == n - 2, 0, (0,))]
    early = early + [
        (direct, 0, plain_next, both, True),
        (direct, 1, plain_prev, both, True),
        (direct, 2, plain_down, both, True),
        (direct, 3, (row == 2) & (time == 0), both, True),
    ]
    forwards = [(0, (row == 1) & (time > 0)), (1, (row == 2) & (time < last))]

    def when(condition, act):
        pl.when(condition)(act)

    def send_pair(sends, j, act):
        for o in range(2):
            c = 2 * j + o
            for make, d, condition, kinds, moved in sends:
                if o == 0 and not moved:
                    continue

                def go(make=make, d=d, kinds=kinds, c=c):
                    for kv in kinds:
                        act(make(d, kv, c))

                when(condition, go)
            if sends is far and fold and o == 0:
                @pl.when(is_a & (lax.rem(j, 2) == 0))
                def _():
                    act(q_direct(j))

                @pl.when(is_a & (lax.rem(j, 2) == 1))
                def _():
                    act(q_to_relay(j))

            if sends is early and fold and o == 0:
                @pl.when(is_e)
                def _():
                    act(above(0, j))
                    act(above(1, j))

    def pass_on(j):
        for o in range(2):
            c = 2 * j + o
            for condition, d, kinds in onward:
                @pl.when(condition)
                def _(d=d, kinds=kinds, c=c):
                    for kv in kinds:
                        to_relay(d, kv, c).wait_recv()
                        from_relay(d, kv, c).start()
        if fold:
            @pl.when((me == 2) & (lax.rem(j, 2) == 1))
            def _():
                q_to_relay(j).wait_recv()
                q_from_relay(j).start()

    def pass_pair(j):
        if fold:
            @pl.when(j < pairs)
            def _():
                pass_on(j)

            @pl.when(j + 1 < pairs)
            def _():
                send_pair(slow, j + 1, start)

    def pass_out(j):
        @pl.when((me == n - 2) & (lax.rem(j, 2) == 0))
        def _():
            out_to_relay(j).wait_recv()
            out_from_relay(j).start()

    def start(copy):
        copy.start()

    def wait_send(copy):
        copy.wait_send()

    bias_sends = (has[1], has[0], has[3], has[2])
    for d in range(4):
        @pl.when(bias_sends[d])
        def _(d=d):
            bias_copy(d).start()

    text_chunks = chunks // 2
    first = core * text_chunks

    def start_sibling(i, _):
        c = lax.rem((1 - core) * text_chunks + i, chunks)
        for d, condition in ((2, even), (3, odd)):
            @pl.when(condition)
            def _(d=d):
                direct(d, 0, c).start()
                direct(d, 1, c).start()
        return 0

    def start_pairs(sends, low, high):
        def go(j, _):
            send_pair(sends, j, start)
            return 0

        if sends and high > low:
            lax.fori_loop(low, high, go, 0)

    far_ahead, handed_ahead, passed = min(2, pairs), min(3, pairs), text_chunks // 2
    start_pairs(early, 0, 1)
    start_pairs(far, 0, 1)
    start_pairs(handed, 0, 1)
    start_pairs(slow, 0, 1)
    lax.fori_loop(0, chunks, start_sibling, 0)
    start_pairs(early, 1, ahead)
    start_pairs(far, 1, far_ahead)
    start_pairs(handed, 1, handed_ahead)

    def missing(d):
        near_bias[d] = jnp.full(near_bias.shape[1:], NEG, jnp.float32)

        def clear(c, _):
            near[d, 0, c] = jnp.zeros(near.shape[3:], jnp.bfloat16)
            near[d, 1, c] = jnp.zeros(near.shape[3:], jnp.bfloat16)
            return 0

        lax.fori_loop(0, chunks, clear, 0)

    for d in range(4):
        @pl.when(off(has[d]))
        def _(d=d):
            missing(d)

        @pl.when(has[d])
        def _(d=d):
            bias_copy(d).wait_recv()

    codes = []
    for t in range(tiles):
        found = []
        for i in range(window_ref.shape[1]):
            w = window_ref[t, i]
            found.append(w + jnp.where(w >= 1, 1, 0))
        codes.append(found)
    for b in range(5):
        for t in range(tiles):
            pick = jnp.zeros((8, tokens), jnp.int32)
            for s in range(tiles):
                want = 3 * b + s - t + 1
                if want == 1:
                    hits = jnp.int32(1)
                elif 3 * b <= want < 3 * b + 3:
                    hits = functools.reduce(
                        jnp.add, [jnp.where(e == want, 1, 0) for e in codes[t]]
                    )
                else:
                    hits = jnp.int32(0)
                pick = jnp.where((lane >= s * tok) & (lane < (s + 1) * tok), hits, pick)
            extra = own_ref[...] if b == 0 else near_bias[b - 1]
            total = jnp.where(pick > 0, 0.0, NEG) + extra
            bias_ref[b, t:t + 1, :] = total[0:1]
    text_lane = lax.broadcasted_iota(jnp.int32, (8, text), 1)
    bias_ref[5] = jnp.where(text_lane < tcount_ref[0], 0.0, NEG)
    if fold:
        @pl.when(is_a)
        def _():
            far_bias_copy().start()
    rows = lax.broadcasted_iota(jnp.int32, (tokens, HD), 0)
    limit = jnp.full((tokens, HD), counts_ref[0], jnp.int32)
    for s in range(1, tiles):
        limit = jnp.where(rows >= s * tok, counts_ref[s], limit)
    qv_ref[...] = jnp.where(lax.rem(rows, tok) < limit, 1.0, 0.0)

    lanes = lax.broadcasted_iota(jnp.int32, (share, 128), 1)
    tstat[...] = jnp.zeros_like(tstat)
    pair_slot = 3 - lax.rem(row, 2)

    def sibling_arrived(c):
        for d, condition in ((3, even), (2, odd)):
            @pl.when(condition)
            def _(d=d):
                direct(d, 0, c).wait_recv()
                direct(d, 1, c).wait_recv()

    for copy in loads[:3]:
        copy.wait()

    def text_part(j, _):
        c = first + j
        sibling_arrived(c)
        for h in range(PER):
            cols = pl.ds(pl.multiple_of(c * WIDTH + h * HD, HD), HD)
            here = slice(h * HD, (h + 1) * HD)
            to = pl.ds(pl.multiple_of(j * WIDTH + h * HD, HD), HD)
            q = tq_ref[:, cols]
            s0 = lax.dot_general(q, k_ref[:, cols], NT, preferred_element_type=jnp.float32)
            s1 = lax.dot_general(
                q, near[pair_slot, 0, c, :, here], NT, preferred_element_type=jnp.float32
            )
            s0 = s0 + own_ref[0:1, :]
            s1 = s1 + near_bias[pair_slot, 0:1, :]
            top = jnp.max(jnp.maximum(s0, s1), axis=1, keepdims=True)
            p0 = jnp.exp2((s0 - top) * LOG2E_SCALE)
            p1 = jnp.exp2((s1 - top) * LOG2E_SCALE)
            total = jnp.sum(p0 + p1, axis=1, keepdims=True)
            num = None
            for p, value in ((p0, v_ref[:, cols]), (p1, near[pair_slot, 1, c, :, here])):
                wide = p * 65537.0
                high = wide - (wide - p)
                for part in (high, p - high):
                    term = jnp.dot(
                        part.astype(jnp.bfloat16), value, preferred_element_type=jnp.float32
                    )
                    num = term if num is None else num + term
            head = j * PER + h
            for b in range(n):
                y, k = (b // 2) % 2, (b // 4) * 2 + b % 2
                part = slice(b * share, (b + 1) * share)
                tnum[y, k, :, to] = num[part]
                stat = jnp.where(lanes == head, top[part], tstat[y, k])
                tstat[y, k] = jnp.where(lanes == head + 64, total[part], stat)

        if fold:
            @pl.when(lax.rem(j, 2) == 1)
            def _():
                pass_pair(lax.div(j, 2))
        return 0

    lax.fori_loop(0, text_chunks, text_part, 0)

    partner = at(2 - 4 * line)

    def y_copies(there):
        return (
            remote(tnum.at[there], ynum, ysend_sem.at[0], yrecv_sem.at[0], partner),
            remote(tstat.at[there], ystat, ysend_sem.at[1], yrecv_sem.at[1], partner),
        )

    for copy in y_copies(1 - line):
        copy.start()
    start_pairs(handed, handed_ahead, pairs)

    peers = n // 2
    my_peer = lax.div(me, 4) * 2 + core
    heads = snum.shape[2] // HD

    def z_copies(i, there, here):
        k = lax.rem(my_peer + i, peers)
        to = lax.div(k, 2) * 4 + 2 * line + lax.rem(k, 2)
        source = k if there is None else there
        target = my_peer if here is None else here
        return (
            remote(snum.at[source], rnum.at[target], zsend_sem.at[0, i], zrecv_sem.at[0, i], to),
            remote(sstat.at[source], rstat.at[target], zsend_sem.at[1, i], zrecv_sem.at[1, i], to),
        )

    def text_exchange():
        for copy in y_copies(1 - line):
            copy.wait_recv()

        def combine(k, _):
            mine, theirs = tstat[line, k], ystat[k]
            top = jnp.maximum(mine, theirs)
            one = jnp.exp2((mine - top) * LOG2E_SCALE)
            two = jnp.exp2((theirs - top) * LOG2E_SCALE)
            den = one * jnp.roll(mine, 64, axis=1) + two * jnp.roll(theirs, 64, axis=1)
            sstat[k] = jnp.where(lanes < 64, top, jnp.roll(den, 64, axis=1))
            for h in range(heads):
                cols = slice(h * HD, (h + 1) * HD)
                num = tnum[line, k, :, cols] * one[:, h:h + 1] + ynum[k, :, cols] * two[:, h:h + 1]
                snum[k, :, cols] = num.astype(jnp.bfloat16)
            return 0

        lax.fori_loop(0, peers, combine, 0)

        def start_z(i, _):
            for copy in z_copies(i, None, None):
                copy.start()
            return 0

        lax.fori_loop(1, peers, start_z, 0)
        start_pairs(early, ahead, pairs)
        rnum[my_peer] = snum[my_peer]
        rstat[my_peer] = sstat[my_peer]

    row_ids = me * share + lax.broadcasted_iota(jnp.int32, (share, HD), 0)
    row_valid = row_ids < jnp.full((share, HD), tcount_ref[0], jnp.int32)

    def text_finish():
        def arrived(i, _):
            for copy in z_copies(i, None, None):
                copy.wait_send()
                copy.wait_recv()
            return 0

        lax.fori_loop(1, peers, arrived, 0)
        for e in range(2):
            top = lax.fori_loop(
                1, peers // 2, lambda i, m: jnp.maximum(m, rstat[2 * i + e]), rstat[e]
            )

            def add(i, carry):
                den, nums = carry
                stat = rstat[2 * i + e]
                scale = jnp.exp2((stat - top) * LOG2E_SCALE)
                den = den + scale * jnp.roll(stat, 64, axis=1)
                nums = tuple(
                    nums[j]
                    + rnum[2 * i + e, :, j * HD:(j + 1) * HD].astype(jnp.float32) * scale[:, j:j + 1]
                    for j in range(heads)
                )
                return den, nums

            zeros = jnp.zeros((share, HD), jnp.float32)
            den, nums = lax.fori_loop(0, peers // 2, add, (zeros, (zeros,) * heads))
            for j in range(heads):
                result = jnp.where(row_valid, nums[j] / den[:, j:j + 1], 0.0)
                at_head = (e * heads + j) * HD
                tout_ref[:, at_head:at_head + HD] = result.astype(jnp.bfloat16)

    def rest_arrived(i, _):
        sibling_arrived(lax.rem(first + text_chunks + i, chunks))
        return 0

    lax.fori_loop(0, chunks - text_chunks, rest_arrived, 0)
    for copy in loads[3:]:
        copy.wait()

    def got(d, c, condition, moved):
        @pl.when(condition & off(is_a) if fold and moved else condition)
        def _():
            direct(d, 0, c).wait_recv()
            direct(d, 1, c).wait_recv()

    def arrive(j, c, moved):
        for d in range(2):
            got(d, c, has[d], moved)
            for source, condition in forwards:
                if source == d:
                    @pl.when(condition)
                    def _(d=d):
                        forward(d, 0, c).start()
                        forward(d, 1, c).start()
        if fold and moved:
            @pl.when(is_d)
            def _():
                beside(0, j).start()
                beside(1, j).start()

    def attend(j, c, moved):
        skip = is_a if (fold and moved) else None
        got(2, c, has[2] & even, moved)
        got(3, c, has[3] & odd, moved)

        def mine():
            for h in range(PER):
                cols = pl.ds(pl.multiple_of(c * WIDTH + h * HD, HD), HD)
                here = slice(h * HD, (h + 1) * HD)
                blocks = [(k_ref[:, cols], v_ref[:, cols], bias_ref.at[0])]
                for d in range(4):
                    blocks.append((near[d, 0, c, :, here], near[d, 1, c, :, here], bias_ref.at[d + 1]))
                blocks.append((tk_ref[:, cols], tv_ref[:, cols], bias_ref.at[5]))
                result = softmax_block(q_ref[:, cols], blocks, half)
                out_ref[:, cols] = jnp.where(qv_ref[...] > 0, result, 0.0).astype(jnp.bfloat16)

        if skip is None:
            mine()
        else:
            pl.when(off(skip))(mine)

        if fold and moved:
            @pl.when(is_c)
            def _():
                @pl.when(j == 0)
                def _():
                    far_bias_copy().wait_recv()

                q_direct(j).wait_recv()
                for kv in range(2):
                    beside(kv, j).wait_recv()
                    above(kv, j).wait_recv()
                for h in range(PER):
                    cols = pl.ds(pl.multiple_of(c * WIDTH + h * HD, HD), HD)
                    here = slice(h * HD, (h + 1) * HD)
                    blocks = [
                        (near[1, 0, c, :, here], near[1, 1, c, :, here], far_bias.at[0]),
                        (k_ref[:, cols], v_ref[:, cols], far_bias.at[1]),
                        (side[1, 0, j, :, here], side[1, 1, j, :, here], far_bias.at[3]),
                        (side[0, 0, j, :, here], side[0, 1, j, :, here], far_bias.at[4]),
                        (tk_ref[:, cols], tv_ref[:, cols], far_bias.at[5]),
                    ]
                    result = softmax_block(far_q[j, :, here], blocks, half)
                    far_out[j, :, here] = result.astype(jnp.bfloat16)

                @pl.when(lax.rem(j, 2) == 0)
                def _():
                    out_to_relay(j).start()

                @pl.when(lax.rem(j, 2) == 1)
                def _():
                    out_direct(j).start()

    def step(j, _):
        if fold:
            @pl.when(j + far_ahead < pairs)
            def _():
                send_pair(far, j + far_ahead, start)

        arrive(j, 2 * j + 1, False)
        attend(j, 2 * j, True)

        @pl.when(j + 1 < pairs)
        def _():
            arrive(j + 1, 2 * j + 2, True)

        attend(j, 2 * j + 1, False)

        if fold:
            pass_pair(j + passed)

            @pl.when(j > 0)
            def _():
                pass_out(j - 1)

        @pl.when(j == min(1, pairs - 1))
        def _():
            text_exchange()

        @pl.when(j == pairs - 2)
        def _():
            text_finish()
        return 0

    arrive(jnp.int32(0), jnp.int32(0), True)
    lax.fori_loop(0, pairs, step, 0)

    if fold:
        pass_out(jnp.int32(pairs - 1))

        @pl.when(is_a)
        def _():
            def take(j, _):
                out_direct(j).wait_recv()
                for h in range(PER):
                    cols = pl.ds(pl.multiple_of(2 * j * WIDTH + h * HD, HD), HD)
                    result = back[j, :, h * HD:(h + 1) * HD].astype(jnp.float32)
                    out_ref[:, cols] = jnp.where(qv_ref[...] > 0, result, 0.0).astype(jnp.bfloat16)
                return 0

            lax.fori_loop(0, pairs, take, 0)

    for d in range(4):
        @pl.when(bias_sends[d])
        def _(d=d):
            bias_copy(d).wait_send()
    for copy in y_copies(1 - line):
        copy.wait_send()

    def finish(j, _):
        for sends in (early, far, handed, slow):
            send_pair(sends, j, wait_send)
        for o in range(2):
            c = 2 * j + o
            for d, condition in ((2, even), (3, odd)):
                @pl.when(condition)
                def _(d=d, c=c):
                    direct(d, 0, c).wait_send()
                    direct(d, 1, c).wait_send()
            for condition, d, kinds in onward:
                @pl.when(condition)
                def _(d=d, kinds=kinds, c=c):
                    for kv in kinds:
                        from_relay(d, kv, c).wait_send()
            for d, condition in forwards:
                @pl.when(condition)
                def _(d=d, c=c):
                    forward(d, 0, c).wait_send()
                    forward(d, 1, c).wait_send()
        if fold:
            @pl.when((me == 2) & (lax.rem(j, 2) == 1))
            def _():
                q_from_relay(j).wait_send()

            @pl.when((me == n - 2) & (lax.rem(j, 2) == 0))
            def _():
                out_from_relay(j).wait_send()

            @pl.when(is_c)
            def _():
                out_direct(j).wait_send()

            @pl.when(is_d)
            def _():
                beside(0, j).wait_send()
                beside(1, j).wait_send()
        return 0

    lax.fori_loop(0, pairs, finish, 0)
    if fold:
        @pl.when(is_a)
        def _():
            far_bias_copy().wait_send()


def per_device(video_q, video_k, video_v, text_q, text_k, text_v, window, counts, text_count):
    n = lax.axis_size("tiles")
    tokens, width = video_q.shape
    text = text_q.shape[0]
    share = text // n
    chunks = width // WIDTH
    pairs = chunks // 2
    peers = n // 2
    fold = n // 2 + NR + NR // 2 == n - 2
    vmem = pl.BlockSpec(memory_space=pltpu.VMEM)
    smem = pl.BlockSpec(memory_space=pltpu.SMEM)
    hbm = pl.BlockSpec(memory_space=pl.ANY)
    dma = pltpu.SemaphoreType.DMA
    bf16, f32 = jnp.bfloat16, jnp.float32
    block = (tokens, WIDTH)
    video_out, text_out = pl.pallas_call(
        functools.partial(main_kernel, n, fold),
        out_shape=(
            jax.ShapeDtypeStruct((tokens, width), bf16),
            jax.ShapeDtypeStruct((share, width), bf16),
        ),
        in_specs=[hbm] * 6 + [smem] * 3,
        out_specs=(vmem, vmem),
        scratch_shapes=[
            *[pltpu.VMEM((tokens, width), bf16)] * 3,
            *[pltpu.VMEM((text, width), bf16)] * 3,
            pltpu.VMEM((8, tokens), f32),
            pltpu.VMEM((6, 8, tokens), f32),
            pltpu.VMEM((tokens, HD), f32),
            pltpu.VMEM((4, 2, chunks, *block), bf16),
            pltpu.VMEM((4, 8, tokens), f32),
            pltpu.VMEM((2, chunks, *block), bf16),
            pltpu.VMEM((6, 8, tokens), f32),
            pltpu.VMEM((pairs, *block), bf16),
            pltpu.VMEM((2, 2, pairs, *block), bf16),
            pltpu.VMEM((pairs, *block), bf16),
            pltpu.VMEM((pairs, *block), bf16),
            pltpu.VMEM((2, peers, share, width // 2), f32),
            pltpu.VMEM((2, peers, share, 128), f32),
            pltpu.VMEM((peers, share, width // 2), f32),
            pltpu.VMEM((peers, share, 128), f32),
            pltpu.VMEM((peers, share, width // 2), bf16),
            pltpu.VMEM((peers, share, 128), f32),
            pltpu.VMEM((peers, share, width // 2), bf16),
            pltpu.VMEM((peers, share, 128), f32),
            dma((6,)),
            dma((4, 2, chunks)),
            dma((4, 2, chunks)),
            dma((5,)),
            dma((5,)),
            dma((2, chunks)),
            dma((2, chunks)),
            dma((2, chunks)),
            dma((pairs,)),
            dma((pairs,)),
            dma((2, pairs)),
            dma((2, 2, pairs)),
            dma((pairs,)),
            dma((pairs,)),
            dma((2,)),
            dma((2,)),
            dma((2, peers)),
            dma((2, peers)),
        ],
        compiler_params=pltpu.CompilerParams(
            collective_id=0, has_side_effects=True, vmem_limit_bytes=56 * 1024 * 1024
        ),
    )(video_q, video_k, video_v, text_q, text_k, text_v, window, counts, text_count)
    return (video_out, text_out)


def solution(mesh):
    return jax.shard_map(
        per_device,
        mesh=mesh,
        in_specs=(
            P(("groups", "tiles"), None),
            P(("groups", "tiles"), None),
            P(("groups", "tiles"), None),
            P("groups", None),
            P("groups", None),
            P("groups", None),
            P("tiles", None),
            P(("groups", "tiles")),
            P("groups"),
        ),
        out_specs=(P(("groups", "tiles"), None), P(("groups", "tiles"), None)),
        check_vma=False,
    )
```

```python
import functools
import math

import jax
import jax.numpy as jnp
from jax import lax
from jax.experimental import pallas as pl
from jax.experimental.pallas import tpu as pltpu
from jax.sharding import PartitionSpec as P

HD = 128
NR = 4
WIDTH = 256
PER = WIDTH // HD
AHEAD = 4
LOG2E_SCALE = math.log2(math.e) / math.sqrt(HD)
MESH = pl.DeviceIdType.MESH
NT = (((1,), (1,)), ((), ()))
NEG = -jnp.inf


def softmax_block(q, blocks, half):
    scores = []
    for key, _, bias in blocks:
        s = lax.dot_general(q, key, NT, preferred_element_type=jnp.float32)
        scores.append(
            jnp.concatenate([s[:half] + bias[0:1, :], s[half:] + bias[1:2, :]], axis=0)
        )
    top = functools.reduce(jnp.maximum, scores)
    top = jnp.max(top, axis=1, keepdims=True)
    total, num = None, None
    for s, (_, value, _) in zip(scores, blocks):
        p = jnp.exp2((s - top) * LOG2E_SCALE)
        total = p if total is None else total + p
        term = jnp.dot(p.astype(jnp.bfloat16), value, preferred_element_type=jnp.float32)
        num = term if num is None else num + term
    return num / jnp.sum(total, axis=1, keepdims=True)


def main_kernel(
    n, fold,
    q_hbm, k_hbm, v_hbm, tq_hbm, tk_hbm, tv_hbm, window_ref, counts_ref, tcount_ref,
    out_ref, tout_ref,
    q_ref, k_ref, v_ref, tq_ref, tk_ref, tv_ref,
    own_ref, bias_ref, qv_ref, near, near_bias,
    relay, far_bias, far_q, side, far_out, back,
    tnum, tstat, ynum, ystat, snum, sstat, rnum, rstat,
    load_sem, send_sem, recv_sem, bsend_sem, brecv_sem, fsend_sem, hsend_sem, rsend_sem, rrecv_sem,
    qsend_sem, qrecv_sem, xsend_sem, xrecv_sem, osend_sem, orecv_sem,
    ysend_sem, yrecv_sem, zsend_sem, zrecv_sem,
):
    group = lax.axis_index("groups")
    me = lax.axis_index("tiles")
    last = n // NR - 1
    tokens, width = q_hbm.shape
    chunks = width // WIDTH
    pairs = chunks // 2
    tiles = counts_ref.shape[0]
    tok = tokens // tiles
    half = tokens // 2
    share = tout_ref.shape[0]
    text = tq_hbm.shape[0]
    ahead = min(AHEAD, pairs)

    def at(offset):
        return lax.rem(me + offset + n, n)

    spot = lax.rem(me + n // 2 + NR + NR // 2, n)
    row = lax.rem(spot, NR)
    time = lax.div(spot, NR)
    core = lax.rem(me, 2)
    line = lax.rem(lax.div(me, 2), 2)
    has = (time > 0, time < last, row > 0, row < NR - 1)
    offs = (-NR, NR, -1, 1)
    even = lax.rem(row, 2) == 0
    odd = lax.rem(row, 2) == 1
    is_a = (me == 0) if fold else None
    is_b = (me == 1) if fold else None
    is_c = (me == n - 4) if fold else None
    is_d = (me == n - 3) if fold else None
    is_e = (me == n - 1) if fold else None

    barrier = pltpu.get_barrier_semaphore()

    def greet(i, _):
        pl.semaphore_signal(barrier, inc=1, device_id=(group, at(i)), device_id_type=MESH)
        return 0

    lax.fori_loop(1, n, greet, 0)

    loads = [
        pltpu.make_async_copy(source, target, load_sem.at[i])
        for i, (source, target) in enumerate((
            (k_hbm, k_ref), (tq_hbm, tq_ref), (v_hbm, v_ref),
            (q_hbm, q_ref), (tk_hbm, tk_ref), (tv_hbm, tv_ref),
        ))
    ]
    for copy in loads:
        copy.start()

    lane = lax.broadcasted_iota(jnp.int32, (8, tokens), 1)
    slot = lax.rem(lane, tok)
    count = jnp.full((8, tokens), counts_ref[0], jnp.int32)
    for s in range(1, tiles):
        count = jnp.where(lane >= s * tok, counts_ref[s], count)
    own_ref[...] = jnp.where(slot < count, 0.0, NEG)

    pl.semaphore_wait(barrier, n - 1)

    def remote(source, target, sent, got, to):
        return pltpu.make_async_remote_copy(
            src_ref=source, dst_ref=target, send_sem=sent, recv_sem=got,
            device_id=(group, to), device_id_type=MESH,
        )

    def columns(c):
        return pl.ds(pl.multiple_of(c * WIDTH, WIDTH), WIDTH)

    def block(kv, c):
        return (k_hbm, v_hbm)[kv].at[:, columns(c)]

    def bias_copy(d):
        return remote(own_ref, near_bias.at[d], bsend_sem.at[d], brecv_sem.at[d], at(-offs[d]))

    def direct(d, kv, c):
        return remote(
            block(kv, c), near.at[d, kv, c], send_sem.at[d, kv, c], recv_sem.at[d, kv, c], at(-offs[d])
        )

    def to_relay(d, kv, c):
        return remote(
            block(kv, c), relay.at[kv, c], send_sem.at[d, kv, c], rrecv_sem.at[kv, c],
            at(2 + kv if d == 3 else 1),
        )

    def from_relay(d, kv, c):
        return remote(
            relay.at[kv, c], near.at[d, kv, c], rsend_sem.at[kv, c], recv_sem.at[d, kv, c],
            at(-3 - kv if d == 3 else 3),
        )

    def forward(d, kv, c):
        slot, to = (2, at(1 - NR)) if d == 0 else (3, at(NR - 1))
        return remote(
            near.at[d, kv, c], near.at[slot, kv, c], fsend_sem.at[kv, c], recv_sem.at[slot, kv, c], to
        )

    def q_direct(j):
        return remote(
            q_hbm.at[:, columns(2 * j)], far_q.at[j], qsend_sem.at[j], qrecv_sem.at[j], at(-1)
        )

    def q_to_relay(j):
        return remote(
            q_hbm.at[:, columns(2 * j)], relay.at[1, j], qsend_sem.at[j], rrecv_sem.at[1, j], at(2)
        )

    def q_from_relay(j):
        return remote(relay.at[1, j], far_q.at[j], rsend_sem.at[1, j], qrecv_sem.at[j], at(-3))

    def out_copy(j):
        return remote(far_out.at[j], back.at[j], osend_sem.at[j], orecv_sem.at[j], at(1))

    def after(kv, c):
        return remote(
            near.at[3, kv, c], near.at[1, kv, c], hsend_sem.at[kv, c], recv_sem.at[1, kv, c], at(-3)
        )

    def beside(kv, j):
        return remote(
            near.at[1, kv, 2 * j], side.at[0, kv, j], xsend_sem.at[kv, j], xrecv_sem.at[0, kv, j], at(2)
        )

    def before(kv, j):
        return remote(
            block(kv, 2 * j), side.at[1, kv, j], xsend_sem.at[kv, j], xrecv_sem.at[1, kv, j], at(3)
        )

    def far_bias_copy():
        return remote(bias_ref, far_bias, bsend_sem.at[4], brecv_sem.at[4], at(-1))

    off = jnp.logical_not
    plain_next, plain_prev = time < last, time > 0
    plain_down = (row == 1) & (time == last)
    both = (0, 1)
    early, far, handed, slow, onward = [], [], [], [], []
    if fold:
        relays = ((me == 2) | (me == 3), me == n - 2)
        plain_next = plain_next & (me < n - NR) & off(relays[0])
        plain_prev = plain_prev & (me >= NR) & off(relays[1])
        plain_down = plain_down & off(is_e)
        early = [
            (direct, 0, is_c, both, (1,)),
            (to_relay, 0, is_d, (0,), (0, 2)),
            (direct, 0, is_d, (0,), (3,)),
            (direct, 0, is_d, (1,), (0, 1)),
            (direct, 2, is_e, both, (1,)),
        ]
        far = [(direct, 1, is_b, both, (0, 1))]
        handed = [(to_relay, 3, is_a, both, (0, 1))]
        slow = [(direct, 0, relays[0], both, (0, 1)), (direct, 1, relays[1], both, (0, 1))]
        onward = [
            (from_relay, 3, me == 2, (0,), (0, 1)),
            (from_relay, 3, me == 3, (1,), (0, 1)),
            (from_relay, 0, me == n - 2, (0,), (0, 2)),
        ]
    early = early + [
        (direct, 0, plain_next, both, (0, 1)),
        (direct, 1, plain_prev, both, (0, 1)),
        (direct, 2, plain_down, both, (0, 1)),
    ]
    late = [(direct, 3, (row == 2) & (time == 0), both, (0, 1))]
    carries = (row == 2) & (time < last)
    forwards = [(0, (row == 1) & (time > 0)), (1, carries & off(is_c) if fold else carries)]

    def when(condition, act):
        pl.when(condition)(act)

    def send_pair(sends, j, act):
        turn = lax.rem(j, 2)
        for o in range(2):
            c = 2 * j + o
            for make, d, condition, kinds, which in sends:
                if o == 0 and 0 not in which or o == 1 and which == (0,):
                    continue
                if o == 1 and 1 not in which:
                    condition = condition & (turn == (0 if 2 in which else 1))

                def go(make=make, d=d, kinds=kinds, c=c):
                    for kv in kinds:
                        act(make(d, kv, c))

                when(condition, go)
            if sends is handed and fold and o == 0:
                @pl.when(is_a & (turn == 1))
                def _():
                    act(q_direct(j))

                @pl.when(is_a & (turn == 0))
                def _():
                    act(q_to_relay(j))

            if sends is early and fold and o == 0:
                @pl.when(is_c)
                def _():
                    act(before(0, j))
                    act(before(1, j))

    def pass_on(j):
        for o in range(2):
            c = 2 * j + o
            for make, d, condition, kinds, which in onward:
                if o == 1 and 1 not in which:
                    condition = condition & (lax.rem(j, 2) == 0)

                @pl.when(condition)
                def _(d=d, kinds=kinds, c=c):
                    for kv in kinds:
                        to_relay(d, kv, c).wait_recv()
                        from_relay(d, kv, c).start()
        @pl.when((me == 2) & (lax.rem(j, 2) == 0))
        def _():
            q_to_relay(j).wait_recv()
            q_from_relay(j).start()

    def pass_pair(j):
        if fold:
            @pl.when(j < pairs)
            def _():
                pass_on(j)

            @pl.when(j + 1 < pairs)
            def _():
                send_pair(slow, j + 1, start)

    def start(copy):
        copy.start()

    def wait_send(copy):
        copy.wait_send()

    bias_sends = (has[1], has[0], has[3], has[2])
    for d in range(4):
        @pl.when(bias_sends[d])
        def _(d=d):
            bias_copy(d).start()

    text_chunks = chunks // 2
    first = core * text_chunks

    def start_sibling(i, _):
        c = lax.rem((1 - core) * text_chunks + i, chunks)
        for d, condition in ((2, even), (3, odd)):
            @pl.when(condition)
            def _(d=d):
                direct(d, 0, c).start()
                direct(d, 1, c).start()
        return 0

    def start_pairs(sends, low, high):
        def go(j, _):
            send_pair(sends, j, start)
            return 0

        if sends and high > low:
            lax.fori_loop(low, high, go, 0)

    far_ahead, handed_ahead, passed = min(2, pairs), min(3, pairs), text_chunks // 2
    start_pairs(early, 0, 1)
    start_pairs(far, 0, 1)
    start_pairs(handed, 0, 1)
    start_pairs(slow, 0, 1)
    lax.fori_loop(0, chunks, start_sibling, 0)
    start_pairs(early, 1, ahead)
    start_pairs(far, 1, far_ahead)
    start_pairs(handed, 1, handed_ahead)

    def missing(d):
        near_bias[d] = jnp.full(near_bias.shape[1:], NEG, jnp.float32)

        def clear(c, _):
            near[d, 0, c] = jnp.zeros(near.shape[3:], jnp.bfloat16)
            near[d, 1, c] = jnp.zeros(near.shape[3:], jnp.bfloat16)
            return 0

        lax.fori_loop(0, chunks, clear, 0)

    for d in range(4):
        @pl.when(off(has[d]))
        def _(d=d):
            missing(d)

        @pl.when(has[d])
        def _(d=d):
            bias_copy(d).wait_recv()

    codes = []
    for t in range(tiles):
        found = []
        for i in range(window_ref.shape[1]):
            w = window_ref[t, i]
            found.append(w + jnp.where(w >= 1, 1, 0))
        codes.append(found)
    for b in range(5):
        for t in range(tiles):
            pick = jnp.zeros((8, tokens), jnp.int32)
            for s in range(tiles):
                want = 3 * b + s - t + 1
                if want == 1:
                    hits = jnp.int32(1)
                elif 3 * b <= want < 3 * b + 3:
                    hits = functools.reduce(
                        jnp.add, [jnp.where(e == want, 1, 0) for e in codes[t]]
                    )
                else:
                    hits = jnp.int32(0)
                pick = jnp.where((lane >= s * tok) & (lane < (s + 1) * tok), hits, pick)
            extra = own_ref[...] if b == 0 else near_bias[b - 1]
            total = jnp.where(pick > 0, 0.0, NEG) + extra
            bias_ref[b, t:t + 1, :] = total[0:1]
    text_lane = lax.broadcasted_iota(jnp.int32, (8, text), 1)
    bias_ref[5] = jnp.where(text_lane < tcount_ref[0], 0.0, NEG)
    if fold:
        @pl.when(is_a)
        def _():
            far_bias_copy().start()
    rows = lax.broadcasted_iota(jnp.int32, (tokens, HD), 0)
    limit = jnp.full((tokens, HD), counts_ref[0], jnp.int32)
    for s in range(1, tiles):
        limit = jnp.where(rows >= s * tok, counts_ref[s], limit)
    qv_ref[...] = jnp.where(lax.rem(rows, tok) < limit, 1.0, 0.0)

    lanes = lax.broadcasted_iota(jnp.int32, (share, 128), 1)
    tstat[...] = jnp.zeros_like(tstat)
    pair_slot = 3 - lax.rem(row, 2)

    def sibling_arrived(c):
        for d, condition in ((3, even), (2, odd)):
            @pl.when(condition)
            def _(d=d):
                direct(d, 0, c).wait_recv()
                direct(d, 1, c).wait_recv()

    for copy in loads[:3]:
        copy.wait()

    def text_part(j, _):
        c = first + j
        sibling_arrived(c)
        for h in range(PER):
            cols = pl.ds(pl.multiple_of(c * WIDTH + h * HD, HD), HD)
            here = slice(h * HD, (h + 1) * HD)
            to = pl.ds(pl.multiple_of(j * WIDTH + h * HD, HD), HD)
            q = tq_ref[:, cols]
            s0 = lax.dot_general(q, k_ref[:, cols], NT, preferred_element_type=jnp.float32)
            s1 = lax.dot_general(
                q, near[pair_slot, 0, c, :, here], NT, preferred_element_type=jnp.float32
            )
            s0 = s0 + own_ref[0:1, :]
            s1 = s1 + near_bias[pair_slot, 0:1, :]
            top = jnp.max(jnp.maximum(s0, s1), axis=1, keepdims=True)
            p0 = jnp.exp2((s0 - top) * LOG2E_SCALE)
            p1 = jnp.exp2((s1 - top) * LOG2E_SCALE)
            total = jnp.sum(p0 + p1, axis=1, keepdims=True)
            num = None
            for p, value in ((p0, v_ref[:, cols]), (p1, near[pair_slot, 1, c, :, here])):
                wide = p * 65537.0
                high = wide - (wide - p)
                for part in (high, p - high):
                    term = jnp.dot(
                        part.astype(jnp.bfloat16), value, preferred_element_type=jnp.float32
                    )
                    num = term if num is None else num + term
            head = j * PER + h
            for b in range(n):
                y, k = (b // 2) % 2, (b // 4) * 2 + b % 2
                part = slice(b * share, (b + 1) * share)
                tnum[y, k, :, to] = num[part]
                stat = jnp.where(lanes == head, top[part], tstat[y, k])
                tstat[y, k] = jnp.where(lanes == head + 64, total[part], stat)

        if fold:
            @pl.when(lax.rem(j, 2) == 1)
            def _():
                pass_pair(lax.div(j, 2))
        return 0

    lax.fori_loop(0, text_chunks, text_part, 0)

    partner = at(2 - 4 * line)

    def y_copies(there):
        return (
            remote(tnum.at[there], ynum, ysend_sem.at[0], yrecv_sem.at[0], partner),
            remote(tstat.at[there], ystat, ysend_sem.at[1], yrecv_sem.at[1], partner),
        )

    for copy in y_copies(1 - line):
        copy.start()
    start_pairs(handed, handed_ahead, pairs)
    start_pairs(late, 0, 1)

    peers = n // 2
    my_peer = lax.div(me, 4) * 2 + core
    heads = snum.shape[2] // HD

    def z_copies(i, there, here):
        k = lax.rem(my_peer + i, peers)
        to = lax.div(k, 2) * 4 + 2 * line + lax.rem(k, 2)
        source = k if there is None else there
        target = my_peer if here is None else here
        return (
            remote(snum.at[source], rnum.at[target], zsend_sem.at[0, i], zrecv_sem.at[0, i], to),
            remote(sstat.at[source], rstat.at[target], zsend_sem.at[1, i], zrecv_sem.at[1, i], to),
        )

    def text_exchange():
        for copy in y_copies(1 - line):
            copy.wait_recv()

        def combine(k, _):
            mine, theirs = tstat[line, k], ystat[k]
            top = jnp.maximum(mine, theirs)
            one = jnp.exp2((mine - top) * LOG2E_SCALE)
            two = jnp.exp2((theirs - top) * LOG2E_SCALE)
            den = one * jnp.roll(mine, 64, axis=1) + two * jnp.roll(theirs, 64, axis=1)
            sstat[k] = jnp.where(lanes < 64, top, jnp.roll(den, 64, axis=1))
            for h in range(heads):
                cols = slice(h * HD, (h + 1) * HD)
                num = tnum[line, k, :, cols] * one[:, h:h + 1] + ynum[k, :, cols] * two[:, h:h + 1]
                snum[k, :, cols] = num.astype(jnp.bfloat16)
            return 0

        lax.fori_loop(0, peers, combine, 0)

        def start_z(i, _):
            for copy in z_copies(i, None, None):
                copy.start()
            return 0

        lax.fori_loop(1, peers, start_z, 0)
        start_pairs(early, ahead, pairs)
        rnum[my_peer] = snum[my_peer]
        rstat[my_peer] = sstat[my_peer]

    row_ids = me * share + lax.broadcasted_iota(jnp.int32, (share, HD), 0)
    row_valid = row_ids < jnp.full((share, HD), tcount_ref[0], jnp.int32)

    def text_finish():
        def arrived(i, _):
            for copy in z_copies(i, None, None):
                copy.wait_send()
                copy.wait_recv()
            return 0

        lax.fori_loop(1, peers, arrived, 0)
        for e in range(2):
            top = lax.fori_loop(
                1, peers // 2, lambda i, m: jnp.maximum(m, rstat[2 * i + e]), rstat[e]
            )

            def add(i, carry):
                den, nums = carry
                stat = rstat[2 * i + e]
                scale = jnp.exp2((stat - top) * LOG2E_SCALE)
                den = den + scale * jnp.roll(stat, 64, axis=1)
                nums = tuple(
                    nums[j]
                    + rnum[2 * i + e, :, j * HD:(j + 1) * HD].astype(jnp.float32) * scale[:, j:j + 1]
                    for j in range(heads)
                )
                return den, nums

            zeros = jnp.zeros((share, HD), jnp.float32)
            den, nums = lax.fori_loop(0, peers // 2, add, (zeros, (zeros,) * heads))
            for j in range(heads):
                result = jnp.where(row_valid, nums[j] / den[:, j:j + 1], 0.0)
                at_head = (e * heads + j) * HD
                tout_ref[:, at_head:at_head + HD] = result.astype(jnp.bfloat16)

    def rest_arrived(i, _):
        sibling_arrived(lax.rem(first + text_chunks + i, chunks))
        return 0

    lax.fori_loop(0, chunks - text_chunks, rest_arrived, 0)
    for copy in loads[3:]:
        copy.wait()

    def got(d, c, condition, moved):
        @pl.when(condition & off(is_a) if fold and moved else condition)
        def _():
            direct(d, 0, c).wait_recv()
            direct(d, 1, c).wait_recv()

    first_at = has[1] & off(is_c) if fold else has[1]

    def arrive(j, c, moved):
        for d, condition in ((0, has[0]), (1, first_at)):
            got(d, c, condition, moved)
            for source, sends in forwards:
                if source == d:
                    @pl.when(sends)
                    def _(d=d):
                        forward(d, 0, c).start()
                        forward(d, 1, c).start()
        if fold:
            @pl.when(is_e)
            def _():
                for kv in range(2):
                    direct(3, kv, c).wait_recv()
                    after(kv, c).start()
        if fold and moved:
            @pl.when(is_d)
            def _():
                beside(0, j).start()
                beside(1, j).start()

    def attend(j, c, moved):
        skip = is_a if (fold and moved) else None
        if fold:
            got(1, c, is_c, False)
        got(2, c, has[2] & even, moved)
        got(3, c, has[3] & odd & off(is_e) if fold else has[3] & odd, moved)

        def mine():
            for h in range(PER):
                cols = pl.ds(pl.multiple_of(c * WIDTH + h * HD, HD), HD)
                here = slice(h * HD, (h + 1) * HD)
                blocks = [(k_ref[:, cols], v_ref[:, cols], bias_ref.at[0])]
                for d in range(4):
                    blocks.append((near[d, 0, c, :, here], near[d, 1, c, :, here], bias_ref.at[d + 1]))
                blocks.append((tk_ref[:, cols], tv_ref[:, cols], bias_ref.at[5]))
                result = softmax_block(q_ref[:, cols], blocks, half)
                out_ref[:, cols] = jnp.where(qv_ref[...] > 0, result, 0.0).astype(jnp.bfloat16)

        if skip is None:
            mine()
        else:
            pl.when(off(skip))(mine)

        if fold and moved:
            @pl.when(is_e)
            def _():
                @pl.when(j == 0)
                def _():
                    far_bias_copy().wait_recv()

                q_direct(j).wait_recv()
                for kv in range(2):
                    beside(kv, j).wait_recv()
                    before(kv, j).wait_recv()
                for h in range(PER):
                    cols = pl.ds(pl.multiple_of(c * WIDTH + h * HD, HD), HD)
                    here = slice(h * HD, (h + 1) * HD)
                    blocks = [
                        (near[3, 0, c, :, here], near[3, 1, c, :, here], far_bias.at[0]),
                        (side[1, 0, j, :, here], side[1, 1, j, :, here], far_bias.at[1]),
                        (k_ref[:, cols], v_ref[:, cols], far_bias.at[3]),
                        (side[0, 0, j, :, here], side[0, 1, j, :, here], far_bias.at[4]),
                        (tk_ref[:, cols], tv_ref[:, cols], far_bias.at[5]),
                    ]
                    result = softmax_block(far_q[j, :, here], blocks, half)
                    far_out[j, :, here] = result.astype(jnp.bfloat16)
                out_copy(j).start()

    def step(j, _):
        if fold:
            @pl.when(j + far_ahead < pairs)
            def _():
                send_pair(far, j + far_ahead, start)

        @pl.when(j + 1 < pairs)
        def _():
            send_pair(late, j + 1, start)

        arrive(j, 2 * j + 1, False)
        attend(j, 2 * j, True)

        @pl.when(j + 1 < pairs)
        def _():
            arrive(j + 1, 2 * j + 2, True)

        attend(j, 2 * j + 1, False)

        if fold:
            pass_pair(j + passed)

        @pl.when(j == min(1, pairs - 1))
        def _():
            text_exchange()

        @pl.when(j == pairs - 2)
        def _():
            text_finish()
        return 0

    arrive(jnp.int32(0), jnp.int32(0), True)
    lax.fori_loop(0, pairs, step, 0)

    if fold:
        @pl.when(is_a)
        def _():
            def take(j, _):
                out_copy(j).wait_recv()
                for h in range(PER):
                    cols = pl.ds(pl.multiple_of(2 * j * WIDTH + h * HD, HD), HD)
                    result = back[j, :, h * HD:(h + 1) * HD].astype(jnp.float32)
                    out_ref[:, cols] = jnp.where(qv_ref[...] > 0, result, 0.0).astype(jnp.bfloat16)
                return 0

            lax.fori_loop(0, pairs, take, 0)

    for d in range(4):
        @pl.when(bias_sends[d])
        def _(d=d):
            bias_copy(d).wait_send()
    for copy in y_copies(1 - line):
        copy.wait_send()

    def finish(j, _):
        for sends in (early, far, handed, slow, late):
            send_pair(sends, j, wait_send)
        send_pair(onward, j, wait_send)
        for o in range(2):
            c = 2 * j + o
            for d, condition in ((2, even), (3, odd)):
                @pl.when(condition)
                def _(d=d, c=c):
                    direct(d, 0, c).wait_send()
                    direct(d, 1, c).wait_send()
            for d, condition in forwards:
                @pl.when(condition)
                def _(d=d, c=c):
                    forward(d, 0, c).wait_send()
                    forward(d, 1, c).wait_send()
        if fold:
            @pl.when((me == 2) & (lax.rem(j, 2) == 0))
            def _():
                q_from_relay(j).wait_send()

            @pl.when(is_e)
            def _():
                out_copy(j).wait_send()
                for o in range(2):
                    after(0, 2 * j + o).wait_send()
                    after(1, 2 * j + o).wait_send()

            @pl.when(is_d)
            def _():
                beside(0, j).wait_send()
                beside(1, j).wait_send()
        return 0

    lax.fori_loop(0, pairs, finish, 0)
    if fold:
        @pl.when(is_a)
        def _():
            far_bias_copy().wait_send()


def per_device(video_q, video_k, video_v, text_q, text_k, text_v, window, counts, text_count):
    n = lax.axis_size("tiles")
    tokens, width = video_q.shape
    text = text_q.shape[0]
    share = text // n
    chunks = width // WIDTH
    pairs = chunks // 2
    peers = n // 2
    fold = n // 2 + NR + NR // 2 == n - 2
    vmem = pl.BlockSpec(memory_space=pltpu.VMEM)
    smem = pl.BlockSpec(memory_space=pltpu.SMEM)
    hbm = pl.BlockSpec(memory_space=pl.ANY)
    dma = pltpu.SemaphoreType.DMA
    bf16, f32 = jnp.bfloat16, jnp.float32
    block = (tokens, WIDTH)
    video_out, text_out = pl.pallas_call(
        functools.partial(main_kernel, n, fold),
        out_shape=(
            jax.ShapeDtypeStruct((tokens, width), bf16),
            jax.ShapeDtypeStruct((share, width), bf16),
        ),
        in_specs=[hbm] * 6 + [smem] * 3,
        out_specs=(vmem, vmem),
        scratch_shapes=[
            *[pltpu.VMEM((tokens, width), bf16)] * 3,
            *[pltpu.VMEM((text, width), bf16)] * 3,
            pltpu.VMEM((8, tokens), f32),
            pltpu.VMEM((6, 8, tokens), f32),
            pltpu.VMEM((tokens, HD), f32),
            pltpu.VMEM((4, 2, chunks, *block), bf16),
            pltpu.VMEM((4, 8, tokens), f32),
            pltpu.VMEM((2, chunks, *block), bf16),
            pltpu.VMEM((6, 8, tokens), f32),
            pltpu.VMEM((pairs, *block), bf16),
            pltpu.VMEM((2, 2, pairs, *block), bf16),
            pltpu.VMEM((pairs, *block), bf16),
            pltpu.VMEM((pairs, *block), bf16),
            pltpu.VMEM((2, peers, share, width // 2), f32),
            pltpu.VMEM((2, peers, share, 128), f32),
            pltpu.VMEM((peers, share, width // 2), f32),
            pltpu.VMEM((peers, share, 128), f32),
            pltpu.VMEM((peers, share, width // 2), bf16),
            pltpu.VMEM((peers, share, 128), f32),
            pltpu.VMEM((peers, share, width // 2), bf16),
            pltpu.VMEM((peers, share, 128), f32),
            dma((6,)),
            dma((4, 2, chunks)),
            dma((4, 2, chunks)),
            dma((5,)),
            dma((5,)),
            dma((2, chunks)),
            dma((2, chunks)),
            dma((2, chunks)),
            dma((2, chunks)),
            dma((pairs,)),
            dma((pairs,)),
            dma((2, pairs)),
            dma((2, 2, pairs)),
            dma((pairs,)),
            dma((pairs,)),
            dma((2,)),
            dma((2,)),
            dma((2, peers)),
            dma((2, peers)),
        ],
        compiler_params=pltpu.CompilerParams(
            collective_id=0, has_side_effects=True, vmem_limit_bytes=56 * 1024 * 1024
        ),
    )(video_q, video_k, video_v, text_q, text_k, text_v, window, counts, text_count)
    return (video_out, text_out)


def solution(mesh):
    return jax.shard_map(
        per_device,
        mesh=mesh,
        in_specs=(
            P(("groups", "tiles"), None),
            P(("groups", "tiles"), None),
            P(("groups", "tiles"), None),
            P("groups", None),
            P("groups", None),
            P("groups", None),
            P("tiles", None),
            P(("groups", "tiles")),
            P("groups"),
        ),
        out_specs=(P(("groups", "tiles"), None), P(("groups", "tiles"), None)),
        check_vma=False,
    )
```

```python
import functools
import math

import jax
import jax.numpy as jnp
from jax import lax
from jax.experimental import pallas as pl
from jax.experimental.pallas import tpu as pltpu
from jax.sharding import PartitionSpec as P

HD = 128
NR = 4
WIDTH = 256
PER = WIDTH // HD
AHEAD = 5
LOG2E_SCALE = math.log2(math.e) / math.sqrt(HD)
MESH = pl.DeviceIdType.MESH
NT = (((1,), (1,)), ((), ()))
NEG = -jnp.inf


def softmax_block(q, blocks, half):
    scores = []
    for key, _, bias in blocks:
        s = lax.dot_general(q, key, NT, preferred_element_type=jnp.float32)
        scores.append(
            jnp.concatenate([s[:half] + bias[0:1, :], s[half:] + bias[1:2, :]], axis=0)
        )
    top = functools.reduce(jnp.maximum, scores)
    top = jnp.max(top, axis=1, keepdims=True)
    total, num = None, None
    for s, (_, value, _) in zip(scores, blocks):
        p = jnp.exp2((s - top) * LOG2E_SCALE)
        total = p if total is None else total + p
        term = jnp.dot(p.astype(jnp.bfloat16), value, preferred_element_type=jnp.float32)
        num = term if num is None else num + term
    return num / jnp.sum(total, axis=1, keepdims=True)


def main_kernel(
    n, fold,
    q_hbm, k_hbm, v_hbm, tq_hbm, tk_hbm, tv_hbm, window_ref, counts_ref, tcount_ref,
    out_hbm, tout_hbm,
    out_ref, tout_ref, q_ref, k_ref, v_ref, tq_ref, tk_ref, tv_ref,
    own_ref, bias_ref, qv_ref, near, near_bias,
    relay, far_bias, far_q, side, far_out, back,
    tnum, tstat, ynum, ystat, snum, sstat, rnum, rstat,
    load_sem, send_sem, recv_sem, bsend_sem, brecv_sem, fsend_sem, hsend_sem, rsend_sem, rrecv_sem,
    qsend_sem, qrecv_sem, xsend_sem, xrecv_sem, osend_sem, orecv_sem,
    ysend_sem, yrecv_sem, zsend_sem, zrecv_sem, store_sem,
):
    group = lax.axis_index("groups")
    me = lax.axis_index("tiles")
    last = n // NR - 1
    tokens, width = q_hbm.shape
    chunks = width // WIDTH
    pairs = chunks // 2
    tiles = counts_ref.shape[0]
    tok = tokens // tiles
    half = tokens // 2
    share = tout_ref.shape[0]
    text = tq_hbm.shape[0]
    ahead = min(AHEAD, pairs)

    def at(offset):
        return lax.rem(me + offset + n, n)

    spot = lax.rem(me + n // 2 + NR + NR // 2, n)
    row = lax.rem(spot, NR)
    time = lax.div(spot, NR)
    core = lax.rem(me, 2)
    line = lax.rem(lax.div(me, 2), 2)
    has = (time > 0, time < last, row > 0, row < NR - 1)
    offs = (-NR, NR, -1, 1)
    even = lax.rem(row, 2) == 0
    odd = lax.rem(row, 2) == 1
    is_a = (me == 0) if fold else None
    is_b = (me == 1) if fold else None
    is_c = (me == n - 4) if fold else None
    is_d = (me == n - 3) if fold else None
    is_e = (me == n - 1) if fold else None

    barrier = pltpu.get_barrier_semaphore()

    def greet(i, _):
        pl.semaphore_signal(barrier, inc=1, device_id=(group, at(i)), device_id_type=MESH)
        return 0

    lax.fori_loop(1, n, greet, 0)

    loads = [
        pltpu.make_async_copy(source, target, load_sem.at[i])
        for i, (source, target) in enumerate((
            (k_hbm, k_ref), (tq_hbm, tq_ref), (v_hbm, v_ref),
            (q_hbm, q_ref), (tk_hbm, tk_ref), (tv_hbm, tv_ref),
        ))
    ]
    for copy in loads:
        copy.start()

    lane = lax.broadcasted_iota(jnp.int32, (8, tokens), 1)
    slot = lax.rem(lane, tok)
    count = jnp.full((8, tokens), counts_ref[0], jnp.int32)
    for s in range(1, tiles):
        count = jnp.where(lane >= s * tok, counts_ref[s], count)
    own_ref[...] = jnp.where(slot < count, 0.0, NEG)

    pl.semaphore_wait(barrier, n - 1)

    def remote(source, target, sent, got, to):
        return pltpu.make_async_remote_copy(
            src_ref=source, dst_ref=target, send_sem=sent, recv_sem=got,
            device_id=(group, to), device_id_type=MESH,
        )

    def columns(c):
        return pl.ds(pl.multiple_of(c * WIDTH, WIDTH), WIDTH)

    def block(kv, c):
        return (k_hbm, v_hbm)[kv].at[:, columns(c)]

    def bias_copy(d):
        return remote(own_ref, near_bias.at[d], bsend_sem.at[d], brecv_sem.at[d], at(-offs[d]))

    def direct(d, kv, c):
        return remote(
            block(kv, c), near.at[d, kv, c], send_sem.at[d, kv, c], recv_sem.at[d, kv, c], at(-offs[d])
        )

    def to_relay(d, kv, c):
        return remote(
            block(kv, c), relay.at[kv, c], send_sem.at[d, kv, c], rrecv_sem.at[kv, c],
            at(2 if d == 3 else 1),
        )

    def from_relay(d, kv, c):
        return remote(
            relay.at[kv, c], near.at[d, kv, c], rsend_sem.at[kv, c], recv_sem.at[d, kv, c],
            at(-3 if d == 3 else 3),
        )

    def forward(d, kv, c):
        slot, to = (2, at(1 - NR)) if d == 0 else (3, at(NR - 1))
        return remote(
            near.at[d, kv, c], near.at[slot, kv, c], fsend_sem.at[kv, c], recv_sem.at[slot, kv, c], to
        )

    def moved_chunk(i):
        return jnp.maximum(2 * i - 1, 0)

    def q_direct(j):
        return remote(
            q_hbm.at[:, columns(moved_chunk(j))], far_q.at[j], qsend_sem.at[j], qrecv_sem.at[j], at(-1)
        )

    def q_to_relay(j):
        return remote(
            q_hbm.at[:, columns(moved_chunk(j))], relay.at[2, j], qsend_sem.at[j], rrecv_sem.at[2, j], at(2)
        )

    def q_from_relay(j):
        return remote(relay.at[2, j], far_q.at[j], rsend_sem.at[2, j], qrecv_sem.at[j], at(-3))

    def out_copy(j):
        return remote(far_out.at[j], back.at[j], osend_sem.at[j], orecv_sem.at[j], at(1))

    def after(kv, c):
        return remote(
            near.at[3, kv, c], near.at[1, kv, c], hsend_sem.at[kv, c], recv_sem.at[1, kv, c], at(-3)
        )

    def beside(kv, j):
        return remote(
            near.at[1, kv, moved_chunk(j)], side.at[0, kv, j], xsend_sem.at[kv, j], xrecv_sem.at[0, kv, j], at(2)
        )

    def before(kv, j):
        return remote(
            block(kv, moved_chunk(j)), side.at[1, kv, j], xsend_sem.at[kv, j], xrecv_sem.at[1, kv, j], at(3)
        )

    def far_bias_copy():
        return remote(bias_ref, far_bias, bsend_sem.at[4], brecv_sem.at[4], at(-1))

    off = jnp.logical_not
    plain_next, plain_prev = time < last, time > 0
    plain_down = (row == 1) & (time == last)
    both = (0, 1)
    always, never = (lambda j: None), (lambda j: False)
    every = (always, always)
    moved = ((lambda j: j == 0), (lambda j: j < pairs - 1))
    kept = ((lambda j: j > 0), (lambda j: j == pairs - 1))
    relayed = (always, lambda j: lax.rem(j, 2) == 0)
    unrelayed = (never, lambda j: lax.rem(j, 2) == 1)
    early, far, handed, slow, onward = [], [], [], [], []
    if fold:
        relays = (me == 2, me == n - 2)
        plain_next = plain_next & (me < n - NR) & off(relays[0])
        plain_prev = plain_prev & (me >= NR) & off(relays[1])
        plain_down = plain_down & off(is_e)
        early = [
            (direct, 0, is_c, both, kept),
            (to_relay, 0, is_d, (0,), relayed),
            (direct, 0, is_d, (0,), unrelayed),
            (direct, 0, is_d, (1,), every),
            (direct, 2, is_e, both, kept),
        ]
        far = [(direct, 1, is_b, both, every)]
        handed = [(to_relay, 3, is_a, both, every)]
        slow = [(direct, 0, relays[0], both, every), (direct, 1, relays[1], both, every)]
        onward = [
            (from_relay, 3, me == 2, both, every),
            (from_relay, 0, me == n - 2, (0,), relayed),
        ]
    early = early + [
        (direct, 0, plain_next, both, every),
        (direct, 1, plain_prev & (row < NR - 1), both, every),
        (direct, 2, plain_down, both, every),
    ]
    calm = [(direct, 1, plain_prev & (row == NR - 1), both, every)]
    late = [(direct, 3, (row == 2) & (time == 0), both, every)]
    carries = (row == 2) & (time < last)
    forwards = [(0, (row == 1) & (time > 0)), (1, carries & off(is_c) if fold else carries)]

    def when(condition, act):
        pl.when(condition)(act)

    def send_pair(sends, j, act):
        for o in range(2):
            c = 2 * j + o
            for make, d, condition, kinds, which in sends:
                only = which[o](j)
                if only is False:
                    continue
                if only is not None:
                    condition = condition & only

                def go(make=make, d=d, kinds=kinds, c=c):
                    for kv in kinds:
                        act(make(d, kv, c))

                when(condition, go)
            i = j + o
            if sends is handed and fold:
                @pl.when(is_a & moved[o](j))
                def _(i=i):
                    @pl.when(lax.rem(i, 2) == 1)
                    def _():
                        act(q_direct(i))

                    @pl.when(lax.rem(i, 2) == 0)
                    def _():
                        act(q_to_relay(i))

            if sends is early and fold:
                @pl.when(is_c & moved[o](j))
                def _(i=i):
                    act(before(0, i))
                    act(before(1, i))

    def pass_on(j):
        for o in range(2):
            c = 2 * j + o
            for make, d, condition, kinds, which in onward:
                only = which[o](j)
                if only is not None:
                    condition = condition & only

                @pl.when(condition)
                def _(make=make, d=d, kinds=kinds, c=c):
                    for kv in kinds:
                        to_relay(d, kv, c).wait_recv()
                        make(d, kv, c).start()

            @pl.when((me == 2) & moved[o](j) & (lax.rem(j + o, 2) == 0))
            def _(i=j + o):
                q_to_relay(i).wait_recv()
                q_from_relay(i).start()

    def pass_pair(j):
        if fold:
            @pl.when(j < pairs)
            def _():
                pass_on(j)
                send_pair(slow, j, start)

    def start(copy):
        copy.start()

    def wait_send(copy):
        copy.wait_send()

    bias_sends = (has[1], has[0], has[3], has[2])
    for d in range(4):
        @pl.when(bias_sends[d])
        def _(d=d):
            bias_copy(d).start()

    text_chunks = chunks // 2
    first = core * text_chunks

    def start_sibling(i, _):
        c = lax.rem((1 - core) * text_chunks + i, chunks)
        for d, condition in ((2, even), (3, odd)):
            @pl.when(condition)
            def _(d=d):
                direct(d, 0, c).start()
                direct(d, 1, c).start()
        return 0

    def start_pairs(sends, low, high):
        def go(j, _):
            send_pair(sends, j, start)
            return 0

        if sends and high > low:
            lax.fori_loop(low, high, go, 0)

    far_ahead, handed_ahead, passed = min(2, pairs), min(3, pairs), text_chunks // 2
    start_pairs(early, 0, 1)
    start_pairs(far, 0, 1)
    start_pairs(handed, 0, 1)
    lax.fori_loop(0, chunks, start_sibling, 0)
    start_pairs(early, 1, ahead)
    start_pairs(far, 1, far_ahead)
    start_pairs(handed, 1, handed_ahead)

    def missing(d):
        near_bias[d] = jnp.full(near_bias.shape[1:], NEG, jnp.float32)

        def clear(c, _):
            near[d, 0, c] = jnp.zeros(near.shape[3:], jnp.bfloat16)
            near[d, 1, c] = jnp.zeros(near.shape[3:], jnp.bfloat16)
            return 0

        lax.fori_loop(0, chunks, clear, 0)

    for d in range(4):
        @pl.when(off(has[d]))
        def _(d=d):
            missing(d)

        @pl.when(has[d])
        def _(d=d):
            bias_copy(d).wait_recv()

    codes = []
    for t in range(tiles):
        found = []
        for i in range(window_ref.shape[1]):
            w = window_ref[t, i]
            found.append(w + jnp.where(w >= 1, 1, 0))
        codes.append(found)
    for b in range(5):
        for t in range(tiles):
            pick = jnp.zeros((8, tokens), jnp.int32)
            for s in range(tiles):
                want = 3 * b + s - t + 1
                if want == 1:
                    hits = jnp.int32(1)
                elif 3 * b <= want < 3 * b + 3:
                    hits = functools.reduce(
                        jnp.add, [jnp.where(e == want, 1, 0) for e in codes[t]]
                    )
                else:
                    hits = jnp.int32(0)
                pick = jnp.where((lane >= s * tok) & (lane < (s + 1) * tok), hits, pick)
            extra = own_ref[...] if b == 0 else near_bias[b - 1]
            total = jnp.where(pick > 0, 0.0, NEG) + extra
            bias_ref[b, t:t + 1, :] = total[0:1]
    text_lane = lax.broadcasted_iota(jnp.int32, (8, text), 1)
    bias_ref[5] = jnp.where(text_lane < tcount_ref[0], 0.0, NEG)
    if fold:
        @pl.when(is_a)
        def _():
            far_bias_copy().start()
    rows = lax.broadcasted_iota(jnp.int32, (tokens, HD), 0)
    limit = jnp.full((tokens, HD), counts_ref[0], jnp.int32)
    for s in range(1, tiles):
        limit = jnp.where(rows >= s * tok, counts_ref[s], limit)
    qv_ref[...] = jnp.where(lax.rem(rows, tok) < limit, 1.0, 0.0)

    lanes = lax.broadcasted_iota(jnp.int32, (share, 128), 1)
    tstat[...] = jnp.zeros_like(tstat)
    pair_slot = 3 - lax.rem(row, 2)

    def sibling_arrived(c):
        for d, condition in ((3, even), (2, odd)):
            @pl.when(condition)
            def _(d=d):
                direct(d, 0, c).wait_recv()
                direct(d, 1, c).wait_recv()

    for copy in loads[:3]:
        copy.wait()

    def text_part(j, _):
        c = first + j
        sibling_arrived(c)
        for h in range(PER):
            cols = pl.ds(pl.multiple_of(c * WIDTH + h * HD, HD), HD)
            here = slice(h * HD, (h + 1) * HD)
            to = pl.ds(pl.multiple_of(j * WIDTH + h * HD, HD), HD)
            q = tq_ref[:, cols]
            s0 = lax.dot_general(q, k_ref[:, cols], NT, preferred_element_type=jnp.float32)
            s1 = lax.dot_general(
                q, near[pair_slot, 0, c, :, here], NT, preferred_element_type=jnp.float32
            )
            s0 = s0 + own_ref[0:1, :]
            s1 = s1 + near_bias[pair_slot, 0:1, :]
            top = jnp.max(jnp.maximum(s0, s1), axis=1, keepdims=True)
            p0 = jnp.exp2((s0 - top) * LOG2E_SCALE)
            p1 = jnp.exp2((s1 - top) * LOG2E_SCALE)
            total = jnp.sum(p0 + p1, axis=1, keepdims=True)
            num = None
            for p, value in ((p0, v_ref[:, cols]), (p1, near[pair_slot, 1, c, :, here])):
                wide = p * 65537.0
                high = wide - (wide - p)
                for part in (high, p - high):
                    term = jnp.dot(
                        part.astype(jnp.bfloat16), value, preferred_element_type=jnp.float32
                    )
                    num = term if num is None else num + term
            head = j * PER + h
            for b in range(n):
                y, k = (b // 2) % 2, (b // 4) * 2 + b % 2
                part = slice(b * share, (b + 1) * share)
                tnum[y, k, :, to] = num[part]
                stat = jnp.where(lanes == head, top[part], tstat[y, k])
                tstat[y, k] = jnp.where(lanes == head + 64, total[part], stat)

        if fold:
            @pl.when(lax.rem(j, 2) == 1)
            def _():
                pass_pair(lax.div(j, 2))
        return 0

    lax.fori_loop(0, text_chunks, text_part, 0)

    partner = at(2 - 4 * line)

    def y_copies(there):
        return (
            remote(tnum.at[there], ynum, ysend_sem.at[0], yrecv_sem.at[0], partner),
            remote(tstat.at[there], ystat, ysend_sem.at[1], yrecv_sem.at[1], partner),
        )

    for copy in y_copies(1 - line):
        copy.start()
    start_pairs(handed, handed_ahead, pairs)
    start_pairs(calm, 0, ahead)
    start_pairs(late, 0, 1)

    peers = n // 2
    my_peer = lax.div(me, 4) * 2 + core
    heads = snum.shape[2] // HD

    def z_copies(i, there, here):
        k = lax.rem(my_peer + i, peers)
        to = lax.div(k, 2) * 4 + 2 * line + lax.rem(k, 2)
        source = k if there is None else there
        target = my_peer if here is None else here
        return (
            remote(snum.at[source], rnum.at[target], zsend_sem.at[0, i], zrecv_sem.at[0, i], to),
            remote(sstat.at[source], rstat.at[target], zsend_sem.at[1, i], zrecv_sem.at[1, i], to),
        )

    def text_exchange():
        for copy in y_copies(1 - line):
            copy.wait_recv()

        def combine(k, _):
            mine, theirs = tstat[line, k], ystat[k]
            top = jnp.maximum(mine, theirs)
            one = jnp.exp2((mine - top) * LOG2E_SCALE)
            two = jnp.exp2((theirs - top) * LOG2E_SCALE)
            den = one * jnp.roll(mine, 64, axis=1) + two * jnp.roll(theirs, 64, axis=1)
            sstat[k] = jnp.where(lanes < 64, top, jnp.roll(den, 64, axis=1))
            for h in range(heads):
                cols = slice(h * HD, (h + 1) * HD)
                num = tnum[line, k, :, cols] * one[:, h:h + 1] + ynum[k, :, cols] * two[:, h:h + 1]
                snum[k, :, cols] = num.astype(jnp.bfloat16)
            return 0

        lax.fori_loop(0, peers, combine, 0)

        def start_z(i, _):
            for copy in z_copies(i, None, None):
                copy.start()
            return 0

        lax.fori_loop(1, peers, start_z, 0)
        start_pairs(early, ahead, pairs)
        start_pairs(calm, ahead, pairs)
        rnum[my_peer] = snum[my_peer]
        rstat[my_peer] = sstat[my_peer]

    row_ids = me * share + lax.broadcasted_iota(jnp.int32, (share, HD), 0)
    row_valid = row_ids < jnp.full((share, HD), tcount_ref[0], jnp.int32)

    def text_finish():
        def arrived(i, _):
            for copy in z_copies(i, None, None):
                copy.wait_send()
                copy.wait_recv()
            return 0

        lax.fori_loop(1, peers, arrived, 0)
        for e in range(2):
            top = lax.fori_loop(
                1, peers // 2, lambda i, m: jnp.maximum(m, rstat[2 * i + e]), rstat[e]
            )

            def add(i, carry):
                den, nums = carry
                stat = rstat[2 * i + e]
                scale = jnp.exp2((stat - top) * LOG2E_SCALE)
                den = den + scale * jnp.roll(stat, 64, axis=1)
                nums = tuple(
                    nums[j]
                    + rnum[2 * i + e, :, j * HD:(j + 1) * HD].astype(jnp.float32) * scale[:, j:j + 1]
                    for j in range(heads)
                )
                return den, nums

            zeros = jnp.zeros((share, HD), jnp.float32)
            den, nums = lax.fori_loop(0, peers // 2, add, (zeros, (zeros,) * heads))
            for j in range(heads):
                result = jnp.where(row_valid, nums[j] / den[:, j:j + 1], 0.0)
                at_head = (e * heads + j) * HD
                tout_ref[:, at_head:at_head + HD] = result.astype(jnp.bfloat16)
        text_stored.start()

    def rest_arrived(i, _):
        sibling_arrived(lax.rem(first + text_chunks + i, chunks))
        return 0

    lax.fori_loop(0, chunks - text_chunks, rest_arrived, 0)
    for copy in loads[3:]:
        copy.wait()

    def stored(c):
        return pltpu.make_async_copy(
            out_ref.at[:, columns(c)], out_hbm.at[:, columns(c)], store_sem.at[c]
        )

    text_stored = pltpu.make_async_copy(tout_ref, tout_hbm, store_sem.at[chunks])

    hands0, hands1 = forwards[0][1], forwards[1][1]
    if fold:
        hands1 = hands1 | is_d

    def arrive(j, o):
        c = 2 * j + o
        for d, condition in forwards:
            @pl.when(condition)
            def _(d=d):
                for kv in range(2):
                    direct(d, kv, c).wait_recv()
                    forward(d, kv, c).start()
        if fold:
            @pl.when(is_d)
            def _():
                for kv in range(2):
                    direct(1, kv, c).wait_recv()

                    @pl.when(moved[o](j))
                    def _(kv=kv):
                        beside(kv, j + o).start()

            @pl.when(is_e)
            def _():
                for kv in range(2):
                    direct(3, kv, c).wait_recv()
                    after(kv, c).start()

    def attend(j, o):
        c = 2 * j + o
        skip = is_a & moved[o](j) if fold else None
        awaited = [
            (0, has[0] & off(hands0)), (1, has[1] & off(hands1)),
            (2, has[2] & even), (3, has[3] & odd & off(is_e) if fold else has[3] & odd),
        ]
        for d, condition in awaited:
            @pl.when(condition if skip is None or d % 2 else condition & off(skip))
            def _(d=d):
                direct(d, 0, c).wait_recv()
                direct(d, 1, c).wait_recv()

        def mine():
            for h in range(PER):
                cols = pl.ds(pl.multiple_of(c * WIDTH + h * HD, HD), HD)
                here = slice(h * HD, (h + 1) * HD)
                blocks = [(k_ref[:, cols], v_ref[:, cols], bias_ref.at[0])]
                for d in range(4):
                    blocks.append((near[d, 0, c, :, here], near[d, 1, c, :, here], bias_ref.at[d + 1]))
                blocks.append((tk_ref[:, cols], tv_ref[:, cols], bias_ref.at[5]))
                result = softmax_block(q_ref[:, cols], blocks, half)
                out_ref[:, cols] = jnp.where(qv_ref[...] > 0, result, 0.0).astype(jnp.bfloat16)
            stored(c).start()

        if skip is None:
            mine()
        else:
            pl.when(off(skip))(mine)

        if fold:
            @pl.when(is_e & moved[o](j))
            def _(i=j + o):
                @pl.when(i == 0)
                def _():
                    far_bias_copy().wait_recv()

                q_direct(i).wait_recv()
                for kv in range(2):
                    beside(kv, i).wait_recv()
                    before(kv, i).wait_recv()
                for h in range(PER):
                    cols = pl.ds(pl.multiple_of(c * WIDTH + h * HD, HD), HD)
                    here = slice(h * HD, (h + 1) * HD)
                    blocks = [
                        (near[3, 0, c, :, here], near[3, 1, c, :, here], far_bias.at[0]),
                        (side[1, 0, i, :, here], side[1, 1, i, :, here], far_bias.at[1]),
                        (k_ref[:, cols], v_ref[:, cols], far_bias.at[3]),
                        (side[0, 0, i, :, here], side[0, 1, i, :, here], far_bias.at[4]),
                        (tk_ref[:, cols], tv_ref[:, cols], far_bias.at[5]),
                    ]
                    result = softmax_block(far_q[i, :, here], blocks, half)
                    far_out[i, :, here] = result.astype(jnp.bfloat16)
                out_copy(i).start()

    def take(j):
        @pl.when(is_a)
        def _():
            out_copy(j).wait_recv()
            for h in range(PER):
                cols = pl.ds(pl.multiple_of(moved_chunk(j) * WIDTH + h * HD, HD), HD)
                result = back[j, :, h * HD:(h + 1) * HD].astype(jnp.float32)
                out_ref[:, cols] = jnp.where(qv_ref[...] > 0, result, 0.0).astype(jnp.bfloat16)
            stored(moved_chunk(j)).start()

    def finish(j):
        for sends in (early, calm, far, handed, slow, late):
            send_pair(sends, j, wait_send)
        send_pair(onward, j, wait_send)
        for o in range(2):
            c = 2 * j + o
            for d, condition in ((2, even), (3, odd)):
                @pl.when(condition)
                def _(d=d, c=c):
                    direct(d, 0, c).wait_send()
                    direct(d, 1, c).wait_send()
            for d, condition in forwards:
                @pl.when(condition)
                def _(d=d, c=c):
                    forward(d, 0, c).wait_send()
                    forward(d, 1, c).wait_send()
        if fold:
            @pl.when((me == 2) & (lax.rem(j, 2) == 0))
            def _():
                q_from_relay(j).wait_send()

            @pl.when(is_e)
            def _():
                out_copy(j).wait_send()
                for o in range(2):
                    after(0, 2 * j + o).wait_send()
                    after(1, 2 * j + o).wait_send()

            @pl.when(is_d)
            def _():
                beside(0, j).wait_send()
                beside(1, j).wait_send()

    def step(j, _):
        if fold:
            @pl.when(j + far_ahead < pairs)
            def _():
                send_pair(far, j + far_ahead, start)

        @pl.when(j + 1 < pairs)
        def _():
            send_pair(late, j + 1, start)

        arrive(j, 1)
        attend(j, 0)

        @pl.when(j + 1 < pairs)
        def _():
            arrive(j + 1, 0)

        attend(j, 1)

        @pl.when(j > 2)
        def _():
            finish(j - 3)

        if fold:
            pass_pair(j + passed)

            @pl.when(j == 1)
            def _():
                take(0)

            @pl.when(j > 0)
            def _():
                take(j)

        @pl.when(j == min(1, pairs - 1))
        def _():
            text_exchange()

        @pl.when(j == pairs - 2)
        def _():
            text_finish()
        return 0

    arrive(jnp.int32(0), 0)
    lax.fori_loop(0, pairs, step, 0)

    def stores(c, _):
        stored(c).wait()
        return 0

    lax.fori_loop(0, chunks, stores, 0)
    text_stored.wait()

    for d in range(4):
        @pl.when(bias_sends[d])
        def _(d=d):
            bias_copy(d).wait_send()
    for copy in y_copies(1 - line):
        copy.wait_send()

    def finish_rest(j, _):
        finish(j)
        return 0

    lax.fori_loop(max(pairs - 3, 0), pairs, finish_rest, 0)
    if fold:
        @pl.when(is_a)
        def _():
            far_bias_copy().wait_send()


def per_device(video_q, video_k, video_v, text_q, text_k, text_v, window, counts, text_count):
    n = lax.axis_size("tiles")
    tokens, width = video_q.shape
    text = text_q.shape[0]
    share = text // n
    chunks = width // WIDTH
    pairs = chunks // 2
    peers = n // 2
    fold = n // 2 + NR + NR // 2 == n - 2
    smem = pl.BlockSpec(memory_space=pltpu.SMEM)
    hbm = pl.BlockSpec(memory_space=pl.ANY)
    dma = pltpu.SemaphoreType.DMA
    bf16, f32 = jnp.bfloat16, jnp.float32
    block = (tokens, WIDTH)
    video_out, text_out = pl.pallas_call(
        functools.partial(main_kernel, n, fold),
        out_shape=(
            jax.ShapeDtypeStruct((tokens, width), bf16),
            jax.ShapeDtypeStruct((share, width), bf16),
        ),
        in_specs=[hbm] * 6 + [smem] * 3,
        out_specs=(hbm, hbm),
        scratch_shapes=[
            pltpu.VMEM((tokens, width), bf16),
            pltpu.VMEM((share, width), bf16),
            *[pltpu.VMEM((tokens, width), bf16)] * 3,
            *[pltpu.VMEM((text, width), bf16)] * 3,
            pltpu.VMEM((8, tokens), f32),
            pltpu.VMEM((6, 8, tokens), f32),
            pltpu.VMEM((tokens, HD), f32),
            pltpu.VMEM((4, 2, chunks, *block), bf16),
            pltpu.VMEM((4, 8, tokens), f32),
            pltpu.VMEM((3, chunks, *block), bf16),
            pltpu.VMEM((6, 8, tokens), f32),
            pltpu.VMEM((pairs, *block), bf16),
            pltpu.VMEM((2, 2, pairs, *block), bf16),
            pltpu.VMEM((pairs, *block), bf16),
            pltpu.VMEM((pairs, *block), bf16),
            pltpu.VMEM((2, peers, share, width // 2), f32),
            pltpu.VMEM((2, peers, share, 128), f32),
            pltpu.VMEM((peers, share, width // 2), f32),
            pltpu.VMEM((peers, share, 128), f32),
            pltpu.VMEM((peers, share, width // 2), bf16),
            pltpu.VMEM((peers, share, 128), f32),
            pltpu.VMEM((peers, share, width // 2), bf16),
            pltpu.VMEM((peers, share, 128), f32),
            dma((6,)),
            dma((4, 2, chunks)),
            dma((4, 2, chunks)),
            dma((5,)),
            dma((5,)),
            dma((2, chunks)),
            dma((2, chunks)),
            dma((3, chunks)),
            dma((3, chunks)),
            dma((pairs,)),
            dma((pairs,)),
            dma((2, pairs)),
            dma((2, 2, pairs)),
            dma((pairs,)),
            dma((pairs,)),
            dma((2,)),
            dma((2,)),
            dma((2, peers)),
            dma((2, peers)),
            dma((chunks + 1,)),
        ],
        compiler_params=pltpu.CompilerParams(
            collective_id=0, has_side_effects=True, vmem_limit_bytes=56 * 1024 * 1024
        ),
    )(video_q, video_k, video_v, text_q, text_k, text_v, window, counts, text_count)
    return (video_out, text_out)


def solution(mesh):
    return jax.shard_map(
        per_device,
        mesh=mesh,
        in_specs=(
            P(("groups", "tiles"), None),
            P(("groups", "tiles"), None),
            P(("groups", "tiles"), None),
            P("groups", None),
            P("groups", None),
            P("groups", None),
            P("tiles", None),
            P(("groups", "tiles")),
            P("groups"),
        ),
        out_specs=(P(("groups", "tiles"), None), P(("groups", "tiles"), None)),
        check_vma=False,
    )
```

```python
import functools
import math

import jax
import jax.numpy as jnp
from jax import lax
from jax.experimental import pallas as pl
from jax.experimental.pallas import tpu as pltpu
from jax.sharding import PartitionSpec as P

HD = 128
NR = 4
WIDTH = 256
PER = WIDTH // HD
AHEAD = 5
PARTS = 8
LOG2E_SCALE = math.log2(math.e) / math.sqrt(HD)
MESH = pl.DeviceIdType.MESH
NT = (((1,), (1,)), ((), ()))
NEG = -jnp.inf


def softmax_block(q, blocks, half):
    scores = []
    for key, _, bias in blocks:
        s = lax.dot_general(q, key, NT, preferred_element_type=jnp.float32)
        scores.append(
            jnp.concatenate([s[:half] + bias[0:1, :], s[half:] + bias[1:2, :]], axis=0)
        )
    top = functools.reduce(jnp.maximum, scores)
    top = jnp.max(top, axis=1, keepdims=True)
    total, num = None, None
    for s, (_, value, _) in zip(scores, blocks):
        p = jnp.exp2((s - top) * LOG2E_SCALE)
        total = p if total is None else total + p
        term = jnp.dot(p.astype(jnp.bfloat16), value, preferred_element_type=jnp.float32)
        num = term if num is None else num + term
    return num / jnp.sum(total, axis=1, keepdims=True)


def main_kernel(
    n, fold,
    q_hbm, k_hbm, v_hbm, tq_hbm, tk_hbm, tv_hbm, window_ref, counts_ref, tcount_ref,
    out_hbm, tout_hbm,
    out_ref, tout_ref, q_ref, k_ref, v_ref, tq_ref, tk_ref, tv_ref,
    own_ref, bias_ref, qv_ref, near, near_bias,
    relay, far_bias, far_q, side, far_out, back,
    tnum, tstat, ynum, ystat, snum, sstat, rnum, rstat,
    load_sem, send_sem, recv_sem, bsend_sem, brecv_sem, fsend_sem, hsend_sem, rsend_sem, rrecv_sem,
    qsend_sem, qrecv_sem, xsend_sem, xrecv_sem, osend_sem, orecv_sem,
    ysend_sem, yrecv_sem, zsend_sem, zrecv_sem, store_sem,
):
    group = lax.axis_index("groups")
    me = lax.axis_index("tiles")
    last = n // NR - 1
    tokens, width = q_hbm.shape
    chunks = width // WIDTH
    pairs = chunks // 2
    tiles = counts_ref.shape[0]
    tok = tokens // tiles
    half = tokens // 2
    share = tout_ref.shape[0]
    text = tq_hbm.shape[0]
    ahead = min(AHEAD, pairs)

    def at(offset):
        return lax.rem(me + offset + n, n)

    spot = lax.rem(me + n // 2 + NR + NR // 2, n)
    row = lax.rem(spot, NR)
    time = lax.div(spot, NR)
    core = lax.rem(me, 2)
    line = lax.rem(lax.div(me, 2), 2)
    has = (time > 0, time < last, row > 0, row < NR - 1)
    offs = (-NR, NR, -1, 1)
    even = lax.rem(row, 2) == 0
    odd = lax.rem(row, 2) == 1
    is_a = (me == 0) if fold else None
    is_b = (me == 1) if fold else None
    is_c = (me == n - 4) if fold else None
    is_d = (me == n - 3) if fold else None
    is_e = (me == n - 1) if fold else None

    barrier = pltpu.get_barrier_semaphore()

    def greet(i, _):
        pl.semaphore_signal(barrier, inc=1, device_id=(group, at(i)), device_id_type=MESH)
        return 0

    lax.fori_loop(1, n, greet, 0)

    loads = [
        pltpu.make_async_copy(source, target, load_sem.at[i])
        for i, (source, target) in enumerate((
            (k_hbm, k_ref), (tq_hbm, tq_ref), (v_hbm, v_ref),
            (q_hbm, q_ref), (tk_hbm, tk_ref), (tv_hbm, tv_ref),
        ))
    ]
    for copy in loads:
        copy.start()

    lane = lax.broadcasted_iota(jnp.int32, (8, tokens), 1)
    slot = lax.rem(lane, tok)
    count = jnp.full((8, tokens), counts_ref[0], jnp.int32)
    for s in range(1, tiles):
        count = jnp.where(lane >= s * tok, counts_ref[s], count)
    own_ref[...] = jnp.where(slot < count, 0.0, NEG)

    pl.semaphore_wait(barrier, n - 1)

    def remote(source, target, sent, got, to):
        return pltpu.make_async_remote_copy(
            src_ref=source, dst_ref=target, send_sem=sent, recv_sem=got,
            device_id=(group, to), device_id_type=MESH,
        )

    def columns(c):
        return pl.ds(pl.multiple_of(c * WIDTH, WIDTH), WIDTH)

    def block(kv, c):
        return (k_hbm, v_hbm)[kv].at[:, columns(c)]

    def bias_copy(d):
        return remote(own_ref, near_bias.at[d], bsend_sem.at[d], brecv_sem.at[d], at(-offs[d]))

    def direct(d, kv, c):
        return remote(
            block(kv, c), near.at[d, kv, c], send_sem.at[d, kv, c], recv_sem.at[d, kv, c], at(-offs[d])
        )

    def to_relay(d, kv, c):
        return remote(
            block(kv, c), relay.at[kv, c], send_sem.at[d, kv, c], rrecv_sem.at[kv, c],
            at(2 if d == 3 else 1),
        )

    def from_relay(d, kv, c):
        return remote(
            relay.at[kv, c], near.at[d, kv, c], rsend_sem.at[kv, c], recv_sem.at[d, kv, c],
            at(-3 if d == 3 else 3),
        )

    def forward(d, kv, c):
        slot, to = (2, at(1 - NR)) if d == 0 else (3, at(NR - 1))
        return remote(
            near.at[d, kv, c], near.at[slot, kv, c], fsend_sem.at[kv, c], recv_sem.at[slot, kv, c], to
        )

    def moved_chunk(i):
        return jnp.maximum(2 * i - 1, 0)

    def q_direct(j):
        return remote(
            q_hbm.at[:, columns(moved_chunk(j))], far_q.at[j], qsend_sem.at[j], qrecv_sem.at[j], at(-1)
        )

    def q_to_relay(j):
        return remote(
            q_hbm.at[:, columns(moved_chunk(j))], relay.at[2, j], qsend_sem.at[j], rrecv_sem.at[2, j], at(2)
        )

    def q_from_relay(j):
        return remote(relay.at[2, j], far_q.at[j], rsend_sem.at[2, j], qrecv_sem.at[j], at(-3))

    def out_copy(j):
        return remote(far_out.at[j], back.at[j], osend_sem.at[j], orecv_sem.at[j], at(1))

    def after(kv, c):
        return remote(
            near.at[3, kv, c], near.at[1, kv, c], hsend_sem.at[kv, c], recv_sem.at[1, kv, c], at(-3)
        )

    def beside(kv, j):
        return remote(
            near.at[1, kv, moved_chunk(j)], side.at[0, kv, j], xsend_sem.at[kv, j], xrecv_sem.at[0, kv, j], at(2)
        )

    def before(kv, j):
        return remote(
            block(kv, moved_chunk(j)), side.at[1, kv, j], xsend_sem.at[kv, j], xrecv_sem.at[1, kv, j], at(3)
        )

    def far_bias_copy():
        return remote(bias_ref, far_bias, bsend_sem.at[4], brecv_sem.at[4], at(-1))

    off = jnp.logical_not
    plain_next, plain_prev = time < last, time > 0
    plain_down = (row == 1) & (time == last)
    both = (0, 1)
    always, never = (lambda j: None), (lambda j: False)
    every = (always, always)
    moved = ((lambda j: j == 0), (lambda j: j < pairs - 1))
    kept = ((lambda j: j > 0), (lambda j: j == pairs - 1))
    relayed = (always, lambda j: lax.rem(j, 2) == 0)
    unrelayed = (never, lambda j: lax.rem(j, 2) == 1)
    leading, far, handed, slow, onward = [], [], [], [], []
    if fold:
        relays = (me == 2, me == n - 2)
        plain_next = plain_next & (me < n - NR) & off(relays[0])
        plain_prev = plain_prev & (me >= NR) & off(relays[1])
        plain_down = plain_down & off(is_e)
        leading = [
            (direct, 0, is_c, both, kept),
            (to_relay, 0, is_d, (0,), relayed),
            (direct, 0, is_d, (0,), unrelayed),
            (direct, 0, is_d, (1,), every),
            (direct, 2, is_e, both, kept),
        ]
        far = [(direct, 1, is_b, both, every)]
        handed = [(to_relay, 3, is_a, both, every)]
        slow = [(direct, 0, relays[0], both, every), (direct, 1, relays[1], both, every)]
        onward = [
            (from_relay, 3, me == 2, both, every),
            (from_relay, 0, me == n - 2, (0,), relayed),
        ]
    early = [
        (direct, 0, plain_next, both, every),
        (direct, 1, plain_prev & (row < NR - 1), both, every),
        (direct, 2, plain_down, both, every),
    ]
    calm = [(direct, 1, plain_prev & (row == NR - 1), both, every)]
    late = [(direct, 3, (row == 2) & (time == 0), both, every)]
    carries = (row == 2) & (time < last)
    forwards = [(0, (row == 1) & (time > 0)), (1, carries & off(is_c) if fold else carries)]

    def when(condition, act):
        pl.when(condition)(act)

    def send_pair(sends, j, act):
        for o in range(2):
            c = 2 * j + o
            for make, d, condition, kinds, which in sends:
                only = which[o](j)
                if only is False:
                    continue
                if only is not None:
                    condition = condition & only

                def go(make=make, d=d, kinds=kinds, c=c):
                    for kv in kinds:
                        act(make(d, kv, c))

                when(condition, go)
            i = j + o
            if sends is handed and fold:
                @pl.when(is_a & moved[o](j))
                def _(i=i):
                    @pl.when(lax.rem(i, 2) == 1)
                    def _():
                        act(q_direct(i))

                    @pl.when(lax.rem(i, 2) == 0)
                    def _():
                        act(q_to_relay(i))

            if sends is early and fold:
                @pl.when(is_c & moved[o](j))
                def _(i=i):
                    act(before(0, i))
                    act(before(1, i))

    def pass_on(j):
        for o in range(2):
            c = 2 * j + o
            for make, d, condition, kinds, which in onward:
                only = which[o](j)
                if only is not None:
                    condition = condition & only

                @pl.when(condition)
                def _(make=make, d=d, kinds=kinds, c=c):
                    for kv in kinds:
                        to_relay(d, kv, c).wait_recv()
                        make(d, kv, c).start()

            @pl.when((me == 2) & moved[o](j) & (lax.rem(j + o, 2) == 0))
            def _(i=j + o):
                q_to_relay(i).wait_recv()
                q_from_relay(i).start()

    def pass_pair(j):
        if fold:
            @pl.when(j < pairs)
            def _():
                pass_on(j)
                send_pair(slow, j, start)

    def start(copy):
        copy.start()

    def wait_send(copy):
        copy.wait_send()

    bias_sends = (has[1], has[0], has[3], has[2])
    for d in range(4):
        @pl.when(bias_sends[d])
        def _(d=d):
            bias_copy(d).start()

    text_chunks = chunks // 2
    first = core * text_chunks

    def start_sibling(i, _):
        c = lax.rem((1 - core) * text_chunks + i, chunks)
        for d, condition in ((2, even), (3, odd)):
            @pl.when(condition)
            def _(d=d):
                direct(d, 0, c).start()
                direct(d, 1, c).start()
        return 0

    def start_pairs(sends, low, high):
        def go(j, _):
            send_pair(sends, j, start)
            return 0

        if sends and high > low:
            lax.fori_loop(low, high, go, 0)

    far_ahead, handed_ahead, passed = min(2, pairs), min(3, pairs), text_chunks // 2
    start_pairs(leading, 0, min(2, pairs))
    start_pairs(early, 0, 1)
    start_pairs(far, 0, 1)
    start_pairs(handed, 0, 1)
    lax.fori_loop(0, chunks, start_sibling, 0)
    for j in range(1, ahead):
        start_pairs(leading, j + 1, min(j + 2, pairs))
        start_pairs(early, j, j + 1)
    start_pairs(far, 1, far_ahead)
    start_pairs(handed, 1, handed_ahead)

    def missing(d):
        near_bias[d] = jnp.full(near_bias.shape[1:], NEG, jnp.float32)

        def clear(c, _):
            near[d, 0, c] = jnp.zeros(near.shape[3:], jnp.bfloat16)
            near[d, 1, c] = jnp.zeros(near.shape[3:], jnp.bfloat16)
            return 0

        lax.fori_loop(0, chunks, clear, 0)

    for d in range(4):
        @pl.when(off(has[d]))
        def _(d=d):
            missing(d)

        @pl.when(has[d])
        def _(d=d):
            bias_copy(d).wait_recv()

    codes = []
    for t in range(tiles):
        found = []
        for i in range(window_ref.shape[1]):
            w = window_ref[t, i]
            found.append(w + jnp.where(w >= 1, 1, 0))
        codes.append(found)
    for b in range(5):
        for t in range(tiles):
            pick = jnp.zeros((8, tokens), jnp.int32)
            for s in range(tiles):
                want = 3 * b + s - t + 1
                if want == 1:
                    hits = jnp.int32(1)
                elif 3 * b <= want < 3 * b + 3:
                    hits = functools.reduce(
                        jnp.add, [jnp.where(e == want, 1, 0) for e in codes[t]]
                    )
                else:
                    hits = jnp.int32(0)
                pick = jnp.where((lane >= s * tok) & (lane < (s + 1) * tok), hits, pick)
            extra = own_ref[...] if b == 0 else near_bias[b - 1]
            total = jnp.where(pick > 0, 0.0, NEG) + extra
            bias_ref[b, t:t + 1, :] = total[0:1]
    text_lane = lax.broadcasted_iota(jnp.int32, (8, text), 1)
    bias_ref[5] = jnp.where(text_lane < tcount_ref[0], 0.0, NEG)
    if fold:
        @pl.when(is_a)
        def _():
            far_bias_copy().start()
    rows = lax.broadcasted_iota(jnp.int32, (tokens, HD), 0)
    limit = jnp.full((tokens, HD), counts_ref[0], jnp.int32)
    for s in range(1, tiles):
        limit = jnp.where(rows >= s * tok, counts_ref[s], limit)
    qv_ref[...] = jnp.where(lax.rem(rows, tok) < limit, 1.0, 0.0)

    lanes = lax.broadcasted_iota(jnp.int32, (share, 128), 1)
    tstat[...] = jnp.zeros_like(tstat)
    pair_slot = 3 - lax.rem(row, 2)

    def sibling_arrived(c):
        for d, condition in ((3, even), (2, odd)):
            @pl.when(condition)
            def _(d=d):
                direct(d, 0, c).wait_recv()
                direct(d, 1, c).wait_recv()

    for copy in loads[:3]:
        copy.wait()

    def text_part(j, _):
        c = first + j
        sibling_arrived(c)
        for h in range(PER):
            cols = pl.ds(pl.multiple_of(c * WIDTH + h * HD, HD), HD)
            here = slice(h * HD, (h + 1) * HD)
            to = pl.ds(pl.multiple_of(j * WIDTH + h * HD, HD), HD)
            q = tq_ref[:, cols]
            s0 = lax.dot_general(q, k_ref[:, cols], NT, preferred_element_type=jnp.float32)
            s1 = lax.dot_general(
                q, near[pair_slot, 0, c, :, here], NT, preferred_element_type=jnp.float32
            )
            s0 = s0 + own_ref[0:1, :]
            s1 = s1 + near_bias[pair_slot, 0:1, :]
            top = jnp.max(jnp.maximum(s0, s1), axis=1, keepdims=True)
            p0 = jnp.exp2((s0 - top) * LOG2E_SCALE)
            p1 = jnp.exp2((s1 - top) * LOG2E_SCALE)
            total = jnp.sum(p0 + p1, axis=1, keepdims=True)
            num = None
            for p, value in ((p0, v_ref[:, cols]), (p1, near[pair_slot, 1, c, :, here])):
                wide = p * 65537.0
                high = wide - (wide - p)
                for part in (high, p - high):
                    term = jnp.dot(
                        part.astype(jnp.bfloat16), value, preferred_element_type=jnp.float32
                    )
                    num = term if num is None else num + term
            head = j * PER + h
            for b in range(n):
                y, k = (b // 2) % 2, (b // 4) * 2 + b % 2
                part = slice(b * share, (b + 1) * share)
                tnum[y, k, :, to] = num[part]
                stat = jnp.where(lanes == head, top[part], tstat[y, k])
                tstat[y, k] = jnp.where(lanes == head + 64, total[part], stat)

        if fold:
            @pl.when(lax.rem(j, 2) == 1)
            def _():
                pass_pair(lax.div(j, 2))
        return 0

    lax.fori_loop(0, text_chunks, text_part, 0)

    partner = at(2 - 4 * line)

    def y_copies(there):
        return (
            remote(tnum.at[there], ynum, ysend_sem.at[0], yrecv_sem.at[0], partner),
            remote(tstat.at[there], ystat, ysend_sem.at[1], yrecv_sem.at[1], partner),
        )

    for copy in y_copies(1 - line):
        copy.start()
    start_pairs(handed, handed_ahead, pairs)
    start_pairs(calm, 0, ahead)
    start_pairs(late, 0, 1)

    peers = n // 2
    my_peer = lax.div(me, 4) * 2 + core
    heads = snum.shape[2] // HD

    def z_copies(i, there, here):
        k = lax.rem(my_peer + i, peers)
        to = lax.div(k, 2) * 4 + 2 * line + lax.rem(k, 2)
        source = k if there is None else there
        target = my_peer if here is None else here
        return (
            remote(snum.at[source], rnum.at[target], zsend_sem.at[0, i], zrecv_sem.at[0, i], to),
            remote(sstat.at[source], rstat.at[target], zsend_sem.at[1, i], zrecv_sem.at[1, i], to),
        )

    def text_exchange():
        for copy in y_copies(1 - line):
            copy.wait_recv()

        def combine(k, _):
            mine, theirs = tstat[line, k], ystat[k]
            top = jnp.maximum(mine, theirs)
            one = jnp.exp2((mine - top) * LOG2E_SCALE)
            two = jnp.exp2((theirs - top) * LOG2E_SCALE)
            den = one * jnp.roll(mine, 64, axis=1) + two * jnp.roll(theirs, 64, axis=1)
            sstat[k] = jnp.where(lanes < 64, top, jnp.roll(den, 64, axis=1))
            for h in range(heads):
                cols = slice(h * HD, (h + 1) * HD)
                num = tnum[line, k, :, cols] * one[:, h:h + 1] + ynum[k, :, cols] * two[:, h:h + 1]
                snum[k, :, cols] = num.astype(jnp.bfloat16)
            return 0

        lax.fori_loop(0, peers, combine, 0)

        def start_z(i, _):
            for copy in z_copies(i, None, None):
                copy.start()
            return 0

        lax.fori_loop(1, peers, start_z, 0)
        start_pairs(leading, min(ahead + 1, pairs), pairs)
        start_pairs(early, ahead, pairs)
        start_pairs(calm, ahead, pairs)
        rnum[my_peer] = snum[my_peer]
        rstat[my_peer] = sstat[my_peer]

    row_ids = me * share + lax.broadcasted_iota(jnp.int32, (share, HD), 0)
    row_valid = row_ids < jnp.full((share, HD), tcount_ref[0], jnp.int32)

    def text_finish():
        def arrived(i, _):
            for copy in z_copies(i, None, None):
                copy.wait_send()
                copy.wait_recv()
            return 0

        lax.fori_loop(1, peers, arrived, 0)
        for e in range(2):
            top = lax.fori_loop(
                1, peers // 2, lambda i, m: jnp.maximum(m, rstat[2 * i + e]), rstat[e]
            )

            def add(i, carry):
                den, nums = carry
                stat = rstat[2 * i + e]
                scale = jnp.exp2((stat - top) * LOG2E_SCALE)
                den = den + scale * jnp.roll(stat, 64, axis=1)
                nums = tuple(
                    nums[j]
                    + rnum[2 * i + e, :, j * HD:(j + 1) * HD].astype(jnp.float32) * scale[:, j:j + 1]
                    for j in range(heads)
                )
                return den, nums

            zeros = jnp.zeros((share, HD), jnp.float32)
            den, nums = lax.fori_loop(0, peers // 2, add, (zeros, (zeros,) * heads))
            for j in range(heads):
                result = jnp.where(row_valid, nums[j] / den[:, j:j + 1], 0.0)
                at_head = (e * heads + j) * HD
                tout_ref[:, at_head:at_head + HD] = result.astype(jnp.bfloat16)
        text_stored.start()

    def rest_arrived(i, _):
        sibling_arrived(lax.rem(first + text_chunks + i, chunks))
        return 0

    lax.fori_loop(0, chunks - text_chunks, rest_arrived, 0)
    for copy in loads[3:]:
        copy.wait()

    def stored(c):
        return pltpu.make_async_copy(
            out_ref.at[:, columns(c)], out_hbm.at[:, columns(c)], store_sem.at[c]
        )

    text_stored = pltpu.make_async_copy(tout_ref, tout_hbm, store_sem.at[chunks])

    hands0, hands1 = forwards[0][1], forwards[1][1]
    if fold:
        hands1 = hands1 | is_d

    def arrive(j, o):
        c = 2 * j + o
        for d, condition in forwards:
            @pl.when(condition)
            def _(d=d):
                for kv in range(2):
                    direct(d, kv, c).wait_recv()
                    forward(d, kv, c).start()
        if fold:
            @pl.when(is_d)
            def _():
                for kv in range(2):
                    direct(1, kv, c).wait_recv()

                    @pl.when(moved[o](j))
                    def _(kv=kv):
                        beside(kv, j + o).start()

            @pl.when(is_e)
            def _():
                for kv in range(2):
                    direct(3, kv, c).wait_recv()
                    after(kv, c).start()

    def attend(j, o):
        c = 2 * j + o
        skip = is_a & moved[o](j) if fold else None
        awaited = [
            (0, has[0] & off(hands0)), (1, has[1] & off(hands1)),
            (2, has[2] & even), (3, has[3] & odd & off(is_e) if fold else has[3] & odd),
        ]
        for d, condition in awaited:
            @pl.when(condition if skip is None or d % 2 else condition & off(skip))
            def _(d=d):
                direct(d, 0, c).wait_recv()
                direct(d, 1, c).wait_recv()

        def mine():
            for h in range(PER):
                cols = pl.ds(pl.multiple_of(c * WIDTH + h * HD, HD), HD)
                here = slice(h * HD, (h + 1) * HD)
                blocks = [(k_ref[:, cols], v_ref[:, cols], bias_ref.at[0])]
                for d in range(4):
                    blocks.append((near[d, 0, c, :, here], near[d, 1, c, :, here], bias_ref.at[d + 1]))
                blocks.append((tk_ref[:, cols], tv_ref[:, cols], bias_ref.at[5]))
                result = softmax_block(q_ref[:, cols], blocks, half)
                out_ref[:, cols] = jnp.where(qv_ref[...] > 0, result, 0.0).astype(jnp.bfloat16)
            stored(c).start()

        if skip is None:
            mine()
        else:
            pl.when(off(skip))(mine)

        if fold:
            @pl.when(is_e & moved[o](j))
            def _(i=j + o):
                @pl.when(i == 0)
                def _():
                    far_bias_copy().wait_recv()

                q_direct(i).wait_recv()
                for kv in range(2):
                    beside(kv, i).wait_recv()
                    before(kv, i).wait_recv()
                for h in range(PER):
                    cols = pl.ds(pl.multiple_of(c * WIDTH + h * HD, HD), HD)
                    here = slice(h * HD, (h + 1) * HD)
                    blocks = [
                        (near[3, 0, c, :, here], near[3, 1, c, :, here], far_bias.at[0]),
                        (side[1, 0, i, :, here], side[1, 1, i, :, here], far_bias.at[1]),
                        (k_ref[:, cols], v_ref[:, cols], far_bias.at[3]),
                        (side[0, 0, i, :, here], side[0, 1, i, :, here], far_bias.at[4]),
                        (tk_ref[:, cols], tv_ref[:, cols], far_bias.at[5]),
                    ]
                    result = softmax_block(far_q[i, :, here], blocks, half)
                    far_out[i, :, here] = result.astype(jnp.bfloat16)
                out_copy(i).start()

    def take(j):
        @pl.when(is_a)
        def _():
            out_copy(j).wait_recv()
            for h in range(PER):
                cols = pl.ds(pl.multiple_of(moved_chunk(j) * WIDTH + h * HD, HD), HD)
                result = back[j, :, h * HD:(h + 1) * HD].astype(jnp.float32)
                out_ref[:, cols] = jnp.where(qv_ref[...] > 0, result, 0.0).astype(jnp.bfloat16)
            stored(moved_chunk(j)).start()

    def finish(j):
        for sends in (leading, early, calm, far, handed, slow, late):
            send_pair(sends, j, wait_send)
        send_pair(onward, j, wait_send)
        for o in range(2):
            c = 2 * j + o
            for d, condition in ((2, even), (3, odd)):
                @pl.when(condition)
                def _(d=d, c=c):
                    direct(d, 0, c).wait_send()
                    direct(d, 1, c).wait_send()
            for d, condition in forwards:
                @pl.when(condition)
                def _(d=d, c=c):
                    forward(d, 0, c).wait_send()
                    forward(d, 1, c).wait_send()
        if fold:
            @pl.when((me == 2) & (lax.rem(j, 2) == 0))
            def _():
                q_from_relay(j).wait_send()

            @pl.when(is_e)
            def _():
                out_copy(j).wait_send()
                for o in range(2):
                    after(0, 2 * j + o).wait_send()
                    after(1, 2 * j + o).wait_send()

            @pl.when(is_d)
            def _():
                beside(0, j).wait_send()
                beside(1, j).wait_send()

    def step(j, _):
        if fold:
            @pl.when(j + far_ahead < pairs)
            def _():
                send_pair(far, j + far_ahead, start)

        @pl.when(j + 1 < pairs)
        def _():
            send_pair(late, j + 1, start)

        arrive(j, 1)
        attend(j, 0)

        @pl.when(j + 1 < pairs)
        def _():
            arrive(j + 1, 0)

        attend(j, 1)

        @pl.when(j > 2)
        def _():
            finish(j - 3)

        if fold:
            pass_pair(j + passed)

            @pl.when(j == 1)
            def _():
                take(0)

            @pl.when(j > 0)
            def _():
                take(j)

        @pl.when(j == min(1, pairs - 1))
        def _():
            text_exchange()

        @pl.when(j == pairs - 2)
        def _():
            text_finish()
        return 0

    arrive(jnp.int32(0), 0)
    lax.fori_loop(0, pairs, step, 0)

    def stores(c, _):
        stored(c).wait()
        return 0

    lax.fori_loop(0, chunks, stores, 0)
    text_stored.wait()

    for d in range(4):
        @pl.when(bias_sends[d])
        def _(d=d):
            bias_copy(d).wait_send()
    for copy in y_copies(1 - line):
        copy.wait_send()

    def finish_rest(j, _):
        finish(j)
        return 0

    lax.fori_loop(max(pairs - 3, 0), pairs, finish_rest, 0)
    if fold:
        @pl.when(is_a)
        def _():
            far_bias_copy().wait_send()


def hand_over(video_ref, text_ref, video_out, text_out, video_part, text_part, sem):
    rows = video_ref.shape[0] // PARTS
    parts = [pl.ds(i * rows, rows) for i in range(PARTS)]
    into = [pltpu.make_async_copy(video_ref.at[p], video_part.at[p], sem.at[0, i]) for i, p in enumerate(parts)]
    onto = [pltpu.make_async_copy(video_part.at[p], video_out.at[p], sem.at[1, i]) for i, p in enumerate(parts)]
    into.append(pltpu.make_async_copy(text_ref, text_part, sem.at[0, PARTS]))
    onto.append(pltpu.make_async_copy(text_part, text_out, sem.at[1, PARTS]))
    for copy in into:
        copy.start()
    for first, second in zip(into, onto):
        first.wait()
        second.start()
    for copy in onto:
        copy.wait()


def per_device(video_q, video_k, video_v, text_q, text_k, text_v, window, counts, text_count):
    n = lax.axis_size("tiles")
    tokens, width = video_q.shape
    text = text_q.shape[0]
    share = text // n
    chunks = width // WIDTH
    pairs = chunks // 2
    peers = n // 2
    fold = n // 2 + NR + NR // 2 == n - 2
    smem = pl.BlockSpec(memory_space=pltpu.SMEM)
    hbm = pl.BlockSpec(memory_space=pl.ANY)
    dma = pltpu.SemaphoreType.DMA
    bf16, f32 = jnp.bfloat16, jnp.float32
    block = (tokens, WIDTH)
    video_out, text_out = pl.pallas_call(
        functools.partial(main_kernel, n, fold),
        out_shape=(
            jax.ShapeDtypeStruct((tokens, width), bf16),
            jax.ShapeDtypeStruct((share, width), bf16),
        ),
        in_specs=[hbm] * 6 + [smem] * 3,
        out_specs=(hbm, hbm),
        scratch_shapes=[
            pltpu.VMEM((tokens, width), bf16),
            pltpu.VMEM((share, width), bf16),
            *[pltpu.VMEM((tokens, width), bf16)] * 3,
            *[pltpu.VMEM((text, width), bf16)] * 3,
            pltpu.VMEM((8, tokens), f32),
            pltpu.VMEM((6, 8, tokens), f32),
            pltpu.VMEM((tokens, HD), f32),
            pltpu.VMEM((4, 2, chunks, *block), bf16),
            pltpu.VMEM((4, 8, tokens), f32),
            pltpu.VMEM((3, chunks, *block), bf16),
            pltpu.VMEM((6, 8, tokens), f32),
            pltpu.VMEM((pairs, *block), bf16),
            pltpu.VMEM((2, 2, pairs, *block), bf16),
            pltpu.VMEM((pairs, *block), bf16),
            pltpu.VMEM((pairs, *block), bf16),
            pltpu.VMEM((2, peers, share, width // 2), f32),
            pltpu.VMEM((2, peers, share, 128), f32),
            pltpu.VMEM((peers, share, width // 2), f32),
            pltpu.VMEM((peers, share, 128), f32),
            pltpu.VMEM((peers, share, width // 2), bf16),
            pltpu.VMEM((peers, share, 128), f32),
            pltpu.VMEM((peers, share, width // 2), bf16),
            pltpu.VMEM((peers, share, 128), f32),
            dma((6,)),
            dma((4, 2, chunks)),
            dma((4, 2, chunks)),
            dma((5,)),
            dma((5,)),
            dma((2, chunks)),
            dma((2, chunks)),
            dma((3, chunks)),
            dma((3, chunks)),
            dma((pairs,)),
            dma((pairs,)),
            dma((2, pairs)),
            dma((2, 2, pairs)),
            dma((pairs,)),
            dma((pairs,)),
            dma((2,)),
            dma((2,)),
            dma((2, peers)),
            dma((2, peers)),
            dma((chunks + 1,)),
        ],
        compiler_params=pltpu.CompilerParams(
            collective_id=0, has_side_effects=True, vmem_limit_bytes=56 * 1024 * 1024
        ),
    )(video_q, video_k, video_v, text_q, text_k, text_v, window, counts, text_count)
    return pl.pallas_call(
        hand_over,
        out_shape=(
            jax.ShapeDtypeStruct((tokens, width), bf16),
            jax.ShapeDtypeStruct((share, width), bf16),
        ),
        in_specs=[hbm] * 2,
        out_specs=(hbm, hbm),
        scratch_shapes=[
            pltpu.VMEM((tokens, width), bf16),
            pltpu.VMEM((share, width), bf16),
            dma((2, PARTS + 1)),
        ],
    )(video_out, text_out)


def solution(mesh):
    return jax.shard_map(
        per_device,
        mesh=mesh,
        in_specs=(
            P(("groups", "tiles"), None),
            P(("groups", "tiles"), None),
            P(("groups", "tiles"), None),
            P("groups", None),
            P("groups", None),
            P("groups", None),
            P("tiles", None),
            P(("groups", "tiles")),
            P("groups"),
        ),
        out_specs=(P(("groups", "tiles"), None), P(("groups", "tiles"), None)),
        check_vma=False,
    )
```

```python
import functools
import math

import jax
import jax.numpy as jnp
from jax import lax
from jax.experimental import pallas as pl
from jax.experimental.pallas import tpu as pltpu
from jax.sharding import PartitionSpec as P

HD = 128
NR = 4
WIDTH = 256
PER = WIDTH // HD
AHEAD = 5
PARTS = 8
LOG2E_SCALE = math.log2(math.e) / math.sqrt(HD)
MESH = pl.DeviceIdType.MESH
NT = (((1,), (1,)), ((), ()))
NEG = -jnp.inf


def softmax_block(q, blocks, half):
    scores = []
    for key, _, bias in blocks:
        s = lax.dot_general(q, key, NT, preferred_element_type=jnp.float32)
        scores.append(
            jnp.concatenate([s[:half] + bias[0:1, :], s[half:] + bias[1:2, :]], axis=0)
        )
    top = functools.reduce(jnp.maximum, scores)
    top = jnp.max(top, axis=1, keepdims=True)
    total, num = None, None
    for s, (_, value, _) in zip(scores, blocks):
        p = jnp.exp2((s - top) * LOG2E_SCALE)
        total = p if total is None else total + p
        term = jnp.dot(p.astype(jnp.bfloat16), value, preferred_element_type=jnp.float32)
        num = term if num is None else num + term
    return num / jnp.sum(total, axis=1, keepdims=True)


def main_kernel(
    n, fold,
    q_hbm, k_hbm, v_hbm, tq_hbm, tk_hbm, tv_hbm, window_ref, counts_ref, tcount_ref,
    out_hbm, tout_hbm,
    out_ref, tout_ref, q_ref, k_ref, v_ref, tq_ref, tk_ref, tv_ref,
    own_ref, bias_ref, qv_ref, near, near_bias,
    relay, far_bias, far_q, side, far_out, back,
    tnum, tstat, ynum, ystat, snum, sstat, rnum, rstat, fnum,
    load_sem, send_sem, recv_sem, bsend_sem, brecv_sem, fsend_sem, hsend_sem, rsend_sem, rrecv_sem,
    qsend_sem, qrecv_sem, xsend_sem, xrecv_sem, osend_sem, orecv_sem,
    ysend_sem, yrecv_sem, zsend_sem, zrecv_sem, store_sem,
):
    group = lax.axis_index("groups")
    me = lax.axis_index("tiles")
    last = n // NR - 1
    tokens, width = q_hbm.shape
    chunks = width // WIDTH
    pairs = chunks // 2
    tiles = counts_ref.shape[0]
    tok = tokens // tiles
    half = tokens // 2
    share = tout_ref.shape[0]
    text = tq_hbm.shape[0]
    ahead = min(AHEAD, pairs)

    def at(offset):
        return lax.rem(me + offset + n, n)

    spot = lax.rem(me + n // 2 + NR + NR // 2, n)
    row = lax.rem(spot, NR)
    time = lax.div(spot, NR)
    core = lax.rem(me, 2)
    line = lax.rem(lax.div(me, 2), 2)
    has = (time > 0, time < last, row > 0, row < NR - 1)
    offs = (-NR, NR, -1, 1)
    even = lax.rem(row, 2) == 0
    odd = lax.rem(row, 2) == 1
    is_a = (me == 0) if fold else None
    is_b = (me == 1) if fold else None
    is_c = (me == n - 4) if fold else None
    is_d = (me == n - 3) if fold else None
    is_e = (me == n - 1) if fold else None

    barrier = pltpu.get_barrier_semaphore()

    def greet(i, _):
        pl.semaphore_signal(barrier, inc=1, device_id=(group, at(i)), device_id_type=MESH)
        return 0

    lax.fori_loop(1, n, greet, 0)

    loads = [
        pltpu.make_async_copy(source, target, load_sem.at[i])
        for i, (source, target) in enumerate((
            (k_hbm, k_ref), (tq_hbm, tq_ref), (v_hbm, v_ref),
            (q_hbm, q_ref), (tk_hbm, tk_ref), (tv_hbm, tv_ref),
        ))
    ]
    for copy in loads:
        copy.start()

    lane = lax.broadcasted_iota(jnp.int32, (8, tokens), 1)
    slot = lax.rem(lane, tok)
    count = jnp.full((8, tokens), counts_ref[0], jnp.int32)
    for s in range(1, tiles):
        count = jnp.where(lane >= s * tok, counts_ref[s], count)
    own_ref[...] = jnp.where(slot < count, 0.0, NEG)

    pl.semaphore_wait(barrier, n - 1)

    def remote(source, target, sent, got, to):
        return pltpu.make_async_remote_copy(
            src_ref=source, dst_ref=target, send_sem=sent, recv_sem=got,
            device_id=(group, to), device_id_type=MESH,
        )

    def columns(c):
        return pl.ds(pl.multiple_of(c * WIDTH, WIDTH), WIDTH)

    def block(kv, c):
        return (k_hbm, v_hbm)[kv].at[:, columns(c)]

    def bias_copy(d):
        return remote(own_ref, near_bias.at[d], bsend_sem.at[d], brecv_sem.at[d], at(-offs[d]))

    def direct(d, kv, c):
        return remote(
            block(kv, c), near.at[d, kv, c], send_sem.at[d, kv, c], recv_sem.at[d, kv, c], at(-offs[d])
        )

    def to_relay(d, kv, c):
        return remote(
            block(kv, c), relay.at[kv, c], send_sem.at[d, kv, c], rrecv_sem.at[kv, c],
            at(2 if d == 3 else 1),
        )

    def from_relay(d, kv, c):
        return remote(
            relay.at[kv, c], near.at[d, kv, c], rsend_sem.at[kv, c], recv_sem.at[d, kv, c],
            at(-3 if d == 3 else 3),
        )

    def forward(d, kv, c):
        slot, to = (2, at(1 - NR)) if d == 0 else (3, at(NR - 1))
        return remote(
            near.at[d, kv, c], near.at[slot, kv, c], fsend_sem.at[kv, c], recv_sem.at[slot, kv, c], to
        )

    def moved_chunk(i):
        return jnp.maximum(2 * i - 1, 0)

    def q_direct(j):
        return remote(
            q_hbm.at[:, columns(moved_chunk(j))], far_q.at[j], qsend_sem.at[j], qrecv_sem.at[j], at(-1)
        )

    def q_to_relay(j):
        return remote(
            q_hbm.at[:, columns(moved_chunk(j))], relay.at[2, j], qsend_sem.at[j], rrecv_sem.at[2, j], at(2)
        )

    def q_from_relay(j):
        return remote(relay.at[2, j], far_q.at[j], rsend_sem.at[2, j], qrecv_sem.at[j], at(-3))

    def out_copy(j):
        return remote(far_out.at[j], back.at[j], osend_sem.at[j], orecv_sem.at[j], at(1))

    def after(kv, c):
        return remote(
            near.at[3, kv, c], near.at[1, kv, c], hsend_sem.at[kv, c], recv_sem.at[1, kv, c], at(-3)
        )

    def beside(kv, j):
        return remote(
            near.at[1, kv, moved_chunk(j)], side.at[0, kv, j], xsend_sem.at[kv, j], xrecv_sem.at[0, kv, j], at(2)
        )

    def before(kv, j):
        return remote(
            block(kv, moved_chunk(j)), side.at[1, kv, j], xsend_sem.at[kv, j], xrecv_sem.at[1, kv, j], at(3)
        )

    def far_bias_copy():
        return remote(bias_ref, far_bias, bsend_sem.at[4], brecv_sem.at[4], at(-1))

    off = jnp.logical_not
    plain_next, plain_prev = time < last, time > 0
    plain_down = (row == 1) & (time == last)
    both = (0, 1)
    always, never = (lambda j: None), (lambda j: False)
    every = (always, always)
    moved = ((lambda j: j == 0), (lambda j: j < pairs - 1))
    kept = ((lambda j: j > 0), (lambda j: j == pairs - 1))
    relayed = (always, lambda j: lax.rem(j, 2) == 0)
    unrelayed = (never, lambda j: lax.rem(j, 2) == 1)
    leading, far, handed, slow, onward = [], [], [], [], []
    if fold:
        relays = (me == 2, me == n - 2)
        plain_next = plain_next & (me < n - NR) & off(relays[0])
        plain_prev = plain_prev & (me >= NR) & off(relays[1])
        plain_down = plain_down & off(is_e)
        leading = [
            (direct, 0, is_c, both, kept),
            (to_relay, 0, is_d, (0,), relayed),
            (direct, 0, is_d, (0,), unrelayed),
            (direct, 0, is_d, (1,), every),
            (direct, 2, is_e, both, kept),
        ]
        far = [(direct, 1, is_b, both, every)]
        handed = [(to_relay, 3, is_a, both, every)]
        slow = [(direct, 0, relays[0], both, every), (direct, 1, relays[1], both, every)]
        onward = [
            (from_relay, 3, me == 2, both, every),
            (from_relay, 0, me == n - 2, (0,), relayed),
        ]
    early = [
        (direct, 0, plain_next, both, every),
        (direct, 1, plain_prev & (row < NR - 1), both, every),
        (direct, 2, plain_down, both, every),
    ]
    calm = [(direct, 1, plain_prev & (row == NR - 1), both, every)]
    late = [(direct, 3, (row == 2) & (time == 0), both, every)]
    carries = (row == 2) & (time < last)
    forwards = [(0, (row == 1) & (time > 0)), (1, carries & off(is_c) if fold else carries)]

    def when(condition, act):
        pl.when(condition)(act)

    def send_pair(sends, j, act):
        for o in range(2):
            c = 2 * j + o
            for make, d, condition, kinds, which in sends:
                only = which[o](j)
                if only is False:
                    continue
                if only is not None:
                    condition = condition & only

                def go(make=make, d=d, kinds=kinds, c=c):
                    for kv in kinds:
                        act(make(d, kv, c))

                when(condition, go)
            i = j + o
            if sends is handed and fold:
                @pl.when(is_a & moved[o](j))
                def _(i=i):
                    @pl.when(lax.rem(i, 2) == 1)
                    def _():
                        act(q_direct(i))

                    @pl.when(lax.rem(i, 2) == 0)
                    def _():
                        act(q_to_relay(i))

            if sends is early and fold:
                @pl.when(is_c & moved[o](j))
                def _(i=i):
                    act(before(0, i))
                    act(before(1, i))

    def pass_on(j):
        for o in range(2):
            c = 2 * j + o
            for make, d, condition, kinds, which in onward:
                only = which[o](j)
                if only is not None:
                    condition = condition & only

                @pl.when(condition)
                def _(make=make, d=d, kinds=kinds, c=c):
                    for kv in kinds:
                        to_relay(d, kv, c).wait_recv()
                        make(d, kv, c).start()

            @pl.when((me == 2) & moved[o](j) & (lax.rem(j + o, 2) == 0))
            def _(i=j + o):
                q_to_relay(i).wait_recv()
                q_from_relay(i).start()

    def pass_pair(j):
        if fold:
            @pl.when(j < pairs)
            def _():
                pass_on(j)
                send_pair(slow, j, start)

    def start(copy):
        copy.start()

    def wait_send(copy):
        copy.wait_send()

    bias_sends = (has[1], has[0], has[3], has[2])
    for d in range(4):
        @pl.when(bias_sends[d])
        def _(d=d):
            bias_copy(d).start()

    text_chunks = chunks // 2
    first = core * text_chunks

    def start_sibling(i, _):
        c = lax.rem((1 - core) * text_chunks + i, chunks)
        for d, condition in ((2, even), (3, odd)):
            @pl.when(condition)
            def _(d=d):
                direct(d, 0, c).start()
                direct(d, 1, c).start()
        return 0

    def start_pairs(sends, low, high):
        def go(j, _):
            send_pair(sends, j, start)
            return 0

        if sends and high > low:
            lax.fori_loop(low, high, go, 0)

    far_ahead, handed_ahead, passed = min(2, pairs), min(3, pairs), text_chunks // 2
    start_pairs(leading, 0, min(2, pairs))
    start_pairs(early, 0, 1)
    start_pairs(far, 0, 1)
    start_pairs(handed, 0, 1)
    lax.fori_loop(0, chunks, start_sibling, 0)
    for j in range(1, ahead):
        start_pairs(leading, j + 1, min(j + 2, pairs))
        start_pairs(early, j, j + 1)
    start_pairs(far, 1, far_ahead)
    start_pairs(handed, 1, handed_ahead)

    def missing(d):
        near_bias[d] = jnp.full(near_bias.shape[1:], NEG, jnp.float32)

        def clear(c, _):
            near[d, 0, c] = jnp.zeros(near.shape[3:], jnp.bfloat16)
            near[d, 1, c] = jnp.zeros(near.shape[3:], jnp.bfloat16)
            return 0

        lax.fori_loop(0, chunks, clear, 0)

    for d in range(4):
        @pl.when(off(has[d]))
        def _(d=d):
            missing(d)

        @pl.when(has[d])
        def _(d=d):
            bias_copy(d).wait_recv()

    codes = []
    for t in range(tiles):
        found = []
        for i in range(window_ref.shape[1]):
            w = window_ref[t, i]
            found.append(w + jnp.where(w >= 1, 1, 0))
        codes.append(found)
    for b in range(5):
        for t in range(tiles):
            pick = jnp.zeros((8, tokens), jnp.int32)
            for s in range(tiles):
                want = 3 * b + s - t + 1
                if want == 1:
                    hits = jnp.int32(1)
                elif 3 * b <= want < 3 * b + 3:
                    hits = functools.reduce(
                        jnp.add, [jnp.where(e == want, 1, 0) for e in codes[t]]
                    )
                else:
                    hits = jnp.int32(0)
                pick = jnp.where((lane >= s * tok) & (lane < (s + 1) * tok), hits, pick)
            extra = own_ref[...] if b == 0 else near_bias[b - 1]
            total = jnp.where(pick > 0, 0.0, NEG) + extra
            bias_ref[b, t:t + 1, :] = total[0:1]
    text_lane = lax.broadcasted_iota(jnp.int32, (8, text), 1)
    bias_ref[5] = jnp.where(text_lane < tcount_ref[0], 0.0, NEG)
    if fold:
        @pl.when(is_a)
        def _():
            far_bias_copy().start()
    rows = lax.broadcasted_iota(jnp.int32, (tokens, HD), 0)
    limit = jnp.full((tokens, HD), counts_ref[0], jnp.int32)
    for s in range(1, tiles):
        limit = jnp.where(rows >= s * tok, counts_ref[s], limit)
    qv_ref[...] = jnp.where(lax.rem(rows, tok) < limit, 1.0, 0.0)

    lanes = lax.broadcasted_iota(jnp.int32, (share, 128), 1)
    tstat[...] = jnp.zeros_like(tstat)
    pair_slot = 3 - lax.rem(row, 2)

    def sibling_arrived(c):
        for d, condition in ((3, even), (2, odd)):
            @pl.when(condition)
            def _(d=d):
                direct(d, 0, c).wait_recv()
                direct(d, 1, c).wait_recv()

    for copy in loads[:3]:
        copy.wait()

    def text_part(j, _):
        c = first + j
        sibling_arrived(c)
        for h in range(PER):
            cols = pl.ds(pl.multiple_of(c * WIDTH + h * HD, HD), HD)
            here = slice(h * HD, (h + 1) * HD)
            to = pl.ds(pl.multiple_of(j * WIDTH + h * HD, HD), HD)
            q = tq_ref[:, cols]
            s0 = lax.dot_general(q, k_ref[:, cols], NT, preferred_element_type=jnp.float32)
            s1 = lax.dot_general(
                q, near[pair_slot, 0, c, :, here], NT, preferred_element_type=jnp.float32
            )
            s0 = s0 + own_ref[0:1, :]
            s1 = s1 + near_bias[pair_slot, 0:1, :]
            top = jnp.max(jnp.maximum(s0, s1), axis=1, keepdims=True)
            p0 = jnp.exp2((s0 - top) * LOG2E_SCALE)
            p1 = jnp.exp2((s1 - top) * LOG2E_SCALE)
            total = jnp.sum(p0 + p1, axis=1, keepdims=True)
            num = None
            for p, value in ((p0, v_ref[:, cols]), (p1, near[pair_slot, 1, c, :, here])):
                wide = p * 65537.0
                high = wide - (wide - p)
                for part in (high, p - high):
                    term = jnp.dot(
                        part.astype(jnp.bfloat16), value, preferred_element_type=jnp.float32
                    )
                    num = term if num is None else num + term
            head = j * PER + h
            for b in range(n):
                y, k = (b // 2) % 2, (b // 4) * 2 + b % 2
                part = slice(b * share, (b + 1) * share)
                tnum[y, k, :, to] = num[part]
                stat = jnp.where(lanes == head, top[part], tstat[y, k])
                tstat[y, k] = jnp.where(lanes == head + 64, total[part], stat)

        if fold:
            @pl.when(lax.rem(j, 2) == 1)
            def _():
                pass_pair(lax.div(j, 2))
        return 0

    lax.fori_loop(0, text_chunks, text_part, 0)

    partner = at(2 - 4 * line)

    def y_copies(there):
        return (
            remote(tnum.at[there], ynum, ysend_sem.at[0], yrecv_sem.at[0], partner),
            remote(tstat.at[there], ystat, ysend_sem.at[1], yrecv_sem.at[1], partner),
        )

    for copy in y_copies(1 - line):
        copy.start()
    start_pairs(handed, handed_ahead, pairs)
    start_pairs(calm, 0, ahead)
    start_pairs(late, 0, 1)

    peers = n // 2
    my_peer = lax.div(me, 4) * 2 + core
    heads = snum.shape[2] // HD

    def z_copies(i, there, here):
        k = lax.rem(my_peer + i, peers)
        to = lax.div(k, 2) * 4 + 2 * line + lax.rem(k, 2)
        source = k if there is None else there
        target = my_peer if here is None else here
        return (
            remote(snum.at[source], rnum.at[target], zsend_sem.at[0, i], zrecv_sem.at[0, i], to),
            remote(sstat.at[source], rstat.at[target], zsend_sem.at[1, i], zrecv_sem.at[1, i], to),
        )

    def whole_copy():
        return remote(
            ynum.at[my_peer + 1 - 2 * core], fnum, ysend_sem.at[2], yrecv_sem.at[2], at(1 - 2 * core)
        )

    def text_exchange():
        for copy in y_copies(1 - line):
            copy.wait_recv()

        def combine(k, _):
            mine, theirs = tstat[line, k], ystat[k]
            top = jnp.maximum(mine, theirs)
            one = jnp.exp2((mine - top) * LOG2E_SCALE)
            two = jnp.exp2((theirs - top) * LOG2E_SCALE)
            den = one * jnp.roll(mine, 64, axis=1) + two * jnp.roll(theirs, 64, axis=1)
            sstat[k] = jnp.where(lanes < 64, top, jnp.roll(den, 64, axis=1))
            for h in range(heads):
                cols = slice(h * HD, (h + 1) * HD)
                num = tnum[line, k, :, cols] * one[:, h:h + 1] + ynum[k, :, cols] * two[:, h:h + 1]
                ynum[k, :, cols] = num
                snum[k, :, cols] = num.astype(jnp.bfloat16)
            return 0

        lax.fori_loop(0, peers, combine, 0)

        def start_z(i, _):
            for copy in z_copies(i, None, None):
                copy.start()
            return 0

        whole_copy().start()
        lax.fori_loop(1, peers, start_z, 0)
        start_pairs(leading, min(ahead + 1, pairs), pairs)
        start_pairs(early, ahead, pairs)
        start_pairs(calm, ahead, pairs)
        rnum[my_peer] = snum[my_peer]
        rstat[my_peer] = sstat[my_peer]

    row_ids = me * share + lax.broadcasted_iota(jnp.int32, (share, HD), 0)
    row_valid = row_ids < jnp.full((share, HD), tcount_ref[0], jnp.int32)

    def value(i, e, cols):
        sent = rnum[2 * i + e, :, cols].astype(jnp.float32)
        own = jnp.where(core == e, ynum[my_peer, :, cols], fnum[:, cols])
        return jnp.where(i == lax.div(me, 4), own, sent)

    def text_finish():
        def arrived(i, _):
            for copy in z_copies(i, None, None):
                copy.wait_send()
                copy.wait_recv()
            return 0

        lax.fori_loop(1, peers, arrived, 0)
        whole_copy().wait_send()
        whole_copy().wait_recv()
        for e in range(2):
            top = lax.fori_loop(
                1, peers // 2, lambda i, m: jnp.maximum(m, rstat[2 * i + e]), rstat[e]
            )

            def add(i, carry):
                den, nums = carry
                stat = rstat[2 * i + e]
                scale = jnp.exp2((stat - top) * LOG2E_SCALE)
                den = den + scale * jnp.roll(stat, 64, axis=1)
                nums = tuple(
                    nums[j] + value(i, e, slice(j * HD, (j + 1) * HD)) * scale[:, j:j + 1]
                    for j in range(heads)
                )
                return den, nums

            zeros = jnp.zeros((share, HD), jnp.float32)
            den, nums = lax.fori_loop(0, peers // 2, add, (zeros, (zeros,) * heads))
            for j in range(heads):
                result = jnp.where(row_valid, nums[j] / den[:, j:j + 1], 0.0)
                at_head = (e * heads + j) * HD
                tout_ref[:, at_head:at_head + HD] = result.astype(jnp.bfloat16)
        text_stored.start()

    def rest_arrived(i, _):
        sibling_arrived(lax.rem(first + text_chunks + i, chunks))
        return 0

    lax.fori_loop(0, chunks - text_chunks, rest_arrived, 0)
    for copy in loads[3:]:
        copy.wait()

    def stored(c):
        return pltpu.make_async_copy(
            out_ref.at[:, columns(c)], out_hbm.at[:, columns(c)], store_sem.at[c]
        )

    text_stored = pltpu.make_async_copy(tout_ref, tout_hbm, store_sem.at[chunks])

    hands0, hands1 = forwards[0][1], forwards[1][1]
    if fold:
        hands1 = hands1 | is_d

    def arrive(j, o):
        c = 2 * j + o
        for d, condition in forwards:
            @pl.when(condition)
            def _(d=d):
                for kv in range(2):
                    direct(d, kv, c).wait_recv()
                    forward(d, kv, c).start()
        if fold:
            @pl.when(is_d)
            def _():
                for kv in range(2):
                    direct(1, kv, c).wait_recv()

                    @pl.when(moved[o](j))
                    def _(kv=kv):
                        beside(kv, j + o).start()

            @pl.when(is_e)
            def _():
                for kv in range(2):
                    direct(3, kv, c).wait_recv()
                    after(kv, c).start()

    def attend(j, o):
        c = 2 * j + o
        skip = is_a & moved[o](j) if fold else None
        awaited = [
            (0, has[0] & off(hands0)), (1, has[1] & off(hands1)),
            (2, has[2] & even), (3, has[3] & odd & off(is_e) if fold else has[3] & odd),
        ]
        for d, condition in awaited:
            @pl.when(condition if skip is None or d % 2 else condition & off(skip))
            def _(d=d):
                direct(d, 0, c).wait_recv()
                direct(d, 1, c).wait_recv()

        def mine():
            for h in range(PER):
                cols = pl.ds(pl.multiple_of(c * WIDTH + h * HD, HD), HD)
                here = slice(h * HD, (h + 1) * HD)
                blocks = [(k_ref[:, cols], v_ref[:, cols], bias_ref.at[0])]
                for d in range(4):
                    blocks.append((near[d, 0, c, :, here], near[d, 1, c, :, here], bias_ref.at[d + 1]))
                blocks.append((tk_ref[:, cols], tv_ref[:, cols], bias_ref.at[5]))
                result = softmax_block(q_ref[:, cols], blocks, half)
                out_ref[:, cols] = jnp.where(qv_ref[...] > 0, result, 0.0).astype(jnp.bfloat16)
            stored(c).start()

        if skip is None:
            mine()
        else:
            pl.when(off(skip))(mine)

        if fold:
            @pl.when(is_e & moved[o](j))
            def _(i=j + o):
                @pl.when(i == 0)
                def _():
                    far_bias_copy().wait_recv()

                q_direct(i).wait_recv()
                for kv in range(2):
                    beside(kv, i).wait_recv()
                    before(kv, i).wait_recv()
                for h in range(PER):
                    cols = pl.ds(pl.multiple_of(c * WIDTH + h * HD, HD), HD)
                    here = slice(h * HD, (h + 1) * HD)
                    blocks = [
                        (near[3, 0, c, :, here], near[3, 1, c, :, here], far_bias.at[0]),
                        (side[1, 0, i, :, here], side[1, 1, i, :, here], far_bias.at[1]),
                        (k_ref[:, cols], v_ref[:, cols], far_bias.at[3]),
                        (side[0, 0, i, :, here], side[0, 1, i, :, here], far_bias.at[4]),
                        (tk_ref[:, cols], tv_ref[:, cols], far_bias.at[5]),
                    ]
                    result = softmax_block(far_q[i, :, here], blocks, half)
                    far_out[i, :, here] = result.astype(jnp.bfloat16)
                out_copy(i).start()

    def take(j):
        @pl.when(is_a)
        def _():
            out_copy(j).wait_recv()
            for h in range(PER):
                cols = pl.ds(pl.multiple_of(moved_chunk(j) * WIDTH + h * HD, HD), HD)
                result = back[j, :, h * HD:(h + 1) * HD].astype(jnp.float32)
                out_ref[:, cols] = jnp.where(qv_ref[...] > 0, result, 0.0).astype(jnp.bfloat16)
            stored(moved_chunk(j)).start()

    def finish(j):
        for sends in (leading, early, calm, far, handed, slow, late):
            send_pair(sends, j, wait_send)
        send_pair(onward, j, wait_send)
        for o in range(2):
            c = 2 * j + o
            for d, condition in ((2, even), (3, odd)):
                @pl.when(condition)
                def _(d=d, c=c):
                    direct(d, 0, c).wait_send()
                    direct(d, 1, c).wait_send()
            for d, condition in forwards:
                @pl.when(condition)
                def _(d=d, c=c):
                    forward(d, 0, c).wait_send()
                    forward(d, 1, c).wait_send()
        if fold:
            @pl.when((me == 2) & (lax.rem(j, 2) == 0))
            def _():
                q_from_relay(j).wait_send()

            @pl.when(is_e)
            def _():
                out_copy(j).wait_send()
                for o in range(2):
                    after(0, 2 * j + o).wait_send()
                    after(1, 2 * j + o).wait_send()

            @pl.when(is_d)
            def _():
                beside(0, j).wait_send()
                beside(1, j).wait_send()

    def step(j, _):
        if fold:
            @pl.when(j + far_ahead < pairs)
            def _():
                send_pair(far, j + far_ahead, start)

        @pl.when(j + 1 < pairs)
        def _():
            send_pair(late, j + 1, start)

        arrive(j, 1)
        attend(j, 0)

        @pl.when(j + 1 < pairs)
        def _():
            arrive(j + 1, 0)

        @pl.when(j > 1)
        def _():
            finish(j - 2)

        @pl.when(j == pairs - 1)
        def _():
            finish(pairs - 2)

        attend(j, 1)

        if fold:
            pass_pair(j + passed)

            @pl.when(j == 1)
            def _():
                take(0)

            @pl.when(j > 0)
            def _():
                take(j)

        @pl.when(j == min(1, pairs - 1))
        def _():
            text_exchange()

        @pl.when(j == pairs - 2)
        def _():
            text_finish()
        return 0

    arrive(jnp.int32(0), 0)
    lax.fori_loop(0, pairs, step, 0)

    def stores(c, _):
        stored(c).wait()
        return 0

    lax.fori_loop(0, chunks, stores, 0)
    text_stored.wait()

    for d in range(4):
        @pl.when(bias_sends[d])
        def _(d=d):
            bias_copy(d).wait_send()
    for copy in y_copies(1 - line):
        copy.wait_send()

    def finish_rest(j, _):
        finish(j)
        return 0

    lax.fori_loop(pairs - 1, pairs, finish_rest, 0)
    if fold:
        @pl.when(is_a)
        def _():
            far_bias_copy().wait_send()


def hand_over(video_ref, text_ref, video_out, text_out, video_part, text_part, sem):
    rows = video_ref.shape[0] // PARTS
    parts = [pl.ds(i * rows, rows) for i in range(PARTS)]
    into = [pltpu.make_async_copy(video_ref.at[p], video_part.at[p], sem.at[0, i]) for i, p in enumerate(parts)]
    onto = [pltpu.make_async_copy(video_part.at[p], video_out.at[p], sem.at[1, i]) for i, p in enumerate(parts)]
    into.append(pltpu.make_async_copy(text_ref, text_part, sem.at[0, PARTS]))
    onto.append(pltpu.make_async_copy(text_part, text_out, sem.at[1, PARTS]))
    for copy in into:
        copy.start()
    for first, second in zip(into, onto):
        first.wait()
        second.start()
    for copy in onto:
        copy.wait()


def per_device(video_q, video_k, video_v, text_q, text_k, text_v, window, counts, text_count):
    n = lax.axis_size("tiles")
    tokens, width = video_q.shape
    text = text_q.shape[0]
    share = text // n
    chunks = width // WIDTH
    pairs = chunks // 2
    peers = n // 2
    fold = n // 2 + NR + NR // 2 == n - 2
    smem = pl.BlockSpec(memory_space=pltpu.SMEM)
    hbm = pl.BlockSpec(memory_space=pl.ANY)
    dma = pltpu.SemaphoreType.DMA
    bf16, f32 = jnp.bfloat16, jnp.float32
    block = (tokens, WIDTH)
    video_out, text_out = pl.pallas_call(
        functools.partial(main_kernel, n, fold),
        out_shape=(
            jax.ShapeDtypeStruct((tokens, width), bf16),
            jax.ShapeDtypeStruct((share, width), bf16),
        ),
        in_specs=[hbm] * 6 + [smem] * 3,
        out_specs=(hbm, hbm),
        scratch_shapes=[
            pltpu.VMEM((tokens, width), bf16),
            pltpu.VMEM((share, width), bf16),
            *[pltpu.VMEM((tokens, width), bf16)] * 3,
            *[pltpu.VMEM((text, width), bf16)] * 3,
            pltpu.VMEM((8, tokens), f32),
            pltpu.VMEM((6, 8, tokens), f32),
            pltpu.VMEM((tokens, HD), f32),
            pltpu.VMEM((4, 2, chunks, *block), bf16),
            pltpu.VMEM((4, 8, tokens), f32),
            pltpu.VMEM((3, chunks, *block), bf16),
            pltpu.VMEM((6, 8, tokens), f32),
            pltpu.VMEM((pairs, *block), bf16),
            pltpu.VMEM((2, 2, pairs, *block), bf16),
            pltpu.VMEM((pairs, *block), bf16),
            pltpu.VMEM((pairs, *block), bf16),
            pltpu.VMEM((2, peers, share, width // 2), f32),
            pltpu.VMEM((2, peers, share, 128), f32),
            pltpu.VMEM((peers, share, width // 2), f32),
            pltpu.VMEM((peers, share, 128), f32),
            pltpu.VMEM((peers, share, width // 2), bf16),
            pltpu.VMEM((peers, share, 128), f32),
            pltpu.VMEM((peers, share, width // 2), bf16),
            pltpu.VMEM((peers, share, 128), f32),
            pltpu.VMEM((share, width // 2), f32),
            dma((6,)),
            dma((4, 2, chunks)),
            dma((4, 2, chunks)),
            dma((5,)),
            dma((5,)),
            dma((2, chunks)),
            dma((2, chunks)),
            dma((3, chunks)),
            dma((3, chunks)),
            dma((pairs,)),
            dma((pairs,)),
            dma((2, pairs)),
            dma((2, 2, pairs)),
            dma((pairs,)),
            dma((pairs,)),
            dma((3,)),
            dma((3,)),
            dma((2, peers)),
            dma((2, peers)),
            dma((chunks + 1,)),
        ],
        compiler_params=pltpu.CompilerParams(
            collective_id=0, has_side_effects=True, vmem_limit_bytes=56 * 1024 * 1024
        ),
    )(video_q, video_k, video_v, text_q, text_k, text_v, window, counts, text_count)
    return pl.pallas_call(
        hand_over,
        out_shape=(
            jax.ShapeDtypeStruct((tokens, width), bf16),
            jax.ShapeDtypeStruct((share, width), bf16),
        ),
        in_specs=[hbm] * 2,
        out_specs=(hbm, hbm),
        scratch_shapes=[
            pltpu.VMEM((tokens, width), bf16),
            pltpu.VMEM((share, width), bf16),
            dma((2, PARTS + 1)),
        ],
    )(video_out, text_out)


def solution(mesh):
    return jax.shard_map(
        per_device,
        mesh=mesh,
        in_specs=(
            P(("groups", "tiles"), None),
            P(("groups", "tiles"), None),
            P(("groups", "tiles"), None),
            P("groups", None),
            P("groups", None),
            P("groups", None),
            P("tiles", None),
            P(("groups", "tiles")),
            P("groups"),
        ),
        out_specs=(P(("groups", "tiles"), None), P(("groups", "tiles"), None)),
        check_vma=False,
    )
```

```python
import functools
import math

import jax
import jax.numpy as jnp
from jax import lax
from jax.experimental import pallas as pl
from jax.experimental.pallas import tpu as pltpu
from jax.sharding import PartitionSpec as P

HD = 128
NR = 4
WIDTH = 256
PER = WIDTH // HD
AHEAD = 5
PARTS = 8
LOG2E_SCALE = math.log2(math.e) / math.sqrt(HD)
MESH = pl.DeviceIdType.MESH
NT = (((1,), (1,)), ((), ()))
NEG = -jnp.inf


def softmax_block(q, blocks, half):
    scores = []
    for key, _, bias in blocks:
        s = lax.dot_general(q, key, NT, preferred_element_type=jnp.float32)
        scores.append(
            jnp.concatenate([s[:half] + bias[0:1, :], s[half:] + bias[1:2, :]], axis=0)
        )
    top = functools.reduce(jnp.maximum, scores)
    top = jnp.max(top, axis=1, keepdims=True)
    total, num = None, None
    for s, (_, value, _) in zip(scores, blocks):
        p = jnp.exp2((s - top) * LOG2E_SCALE)
        total = p if total is None else total + p
        term = jnp.dot(p.astype(jnp.bfloat16), value, preferred_element_type=jnp.float32)
        num = term if num is None else num + term
    return num / jnp.sum(total, axis=1, keepdims=True)


def main_kernel(
    n, fold,
    q_hbm, k_hbm, v_hbm, tq_hbm, tk_hbm, tv_hbm, window_ref, counts_ref, tcount_ref,
    out_hbm, tout_hbm,
    out_ref, tout_ref, q_ref, k_ref, v_ref, tq_ref, tk_ref, tv_ref,
    own_ref, bias_ref, qv_ref, near, near_bias,
    relay, far_bias, far_q, side, far_out, back,
    tnum, tstat, ynum, ystat, snum, sstat, rnum, rstat, fnum,
    load_sem, send_sem, recv_sem, bsend_sem, brecv_sem, fsend_sem, hsend_sem, rsend_sem, rrecv_sem,
    qsend_sem, qrecv_sem, xsend_sem, xrecv_sem, osend_sem, orecv_sem,
    ysend_sem, yrecv_sem, zsend_sem, zrecv_sem, store_sem,
):
    group = lax.axis_index("groups")
    me = lax.axis_index("tiles")
    last = n // NR - 1
    tokens, width = q_hbm.shape
    chunks = width // WIDTH
    pairs = chunks // 2
    tiles = counts_ref.shape[0]
    tok = tokens // tiles
    half = tokens // 2
    share = tout_ref.shape[0]
    text = tq_hbm.shape[0]
    ahead = min(AHEAD, pairs)

    def at(offset):
        return lax.rem(me + offset + n, n)

    spot = lax.rem(me + n // 2 + NR + NR // 2, n)
    row = lax.rem(spot, NR)
    time = lax.div(spot, NR)
    core = lax.rem(me, 2)
    line = lax.rem(lax.div(me, 2), 2)
    has = (time > 0, time < last, row > 0, row < NR - 1)
    offs = (-NR, NR, -1, 1)
    even = lax.rem(row, 2) == 0
    odd = lax.rem(row, 2) == 1
    is_a = (me == 0) if fold else None
    is_b = (me == 1) if fold else None
    is_c = (me == n - 4) if fold else None
    is_d = (me == n - 3) if fold else None
    is_e = (me == n - 1) if fold else None

    barrier = pltpu.get_barrier_semaphore()

    def greet(i, _):
        pl.semaphore_signal(barrier, inc=1, device_id=(group, at(i)), device_id_type=MESH)
        return 0

    lax.fori_loop(1, n, greet, 0)

    loads = [
        pltpu.make_async_copy(source, target, load_sem.at[i])
        for i, (source, target) in enumerate((
            (k_hbm, k_ref), (tq_hbm, tq_ref), (v_hbm, v_ref),
            (q_hbm, q_ref), (tk_hbm, tk_ref), (tv_hbm, tv_ref),
        ))
    ]
    for copy in loads:
        copy.start()

    lane = lax.broadcasted_iota(jnp.int32, (8, tokens), 1)
    slot = lax.rem(lane, tok)
    count = jnp.full((8, tokens), counts_ref[0], jnp.int32)
    for s in range(1, tiles):
        count = jnp.where(lane >= s * tok, counts_ref[s], count)
    own_ref[...] = jnp.where(slot < count, 0.0, NEG)

    pl.semaphore_wait(barrier, n - 1)

    def remote(source, target, sent, got, to):
        return pltpu.make_async_remote_copy(
            src_ref=source, dst_ref=target, send_sem=sent, recv_sem=got,
            device_id=(group, to), device_id_type=MESH,
        )

    def columns(c):
        return pl.ds(pl.multiple_of(c * WIDTH, WIDTH), WIDTH)

    def block(kv, c):
        return (k_hbm, v_hbm)[kv].at[:, columns(c)]

    def bias_copy(d):
        return remote(own_ref, near_bias.at[d], bsend_sem.at[d], brecv_sem.at[d], at(-offs[d]))

    def direct(d, kv, c):
        return remote(
            block(kv, c), near.at[d, kv, c], send_sem.at[d, kv, c], recv_sem.at[d, kv, c], at(-offs[d])
        )

    def to_relay(d, kv, c):
        return remote(
            block(kv, c), relay.at[kv, c], send_sem.at[d, kv, c], rrecv_sem.at[kv, c],
            at(2 if d == 3 else 1),
        )

    def from_relay(d, kv, c):
        return remote(
            relay.at[kv, c], near.at[d, kv, c], rsend_sem.at[kv, c], recv_sem.at[d, kv, c],
            at(-3 if d == 3 else 3),
        )

    def forward(d, kv, c):
        slot, to = (2, at(1 - NR)) if d == 0 else (3, at(NR - 1))
        return remote(
            near.at[d, kv, c], near.at[slot, kv, c], fsend_sem.at[kv, c], recv_sem.at[slot, kv, c], to
        )

    def moved_chunk(i):
        return jnp.maximum(2 * i - 1, 0)

    def q_direct(j):
        return remote(
            q_hbm.at[:, columns(moved_chunk(j))], far_q.at[j], qsend_sem.at[j], qrecv_sem.at[j], at(-1)
        )

    def q_to_relay(j):
        return remote(
            q_hbm.at[:, columns(moved_chunk(j))], relay.at[2, j], qsend_sem.at[j], rrecv_sem.at[2, j], at(2)
        )

    def q_from_relay(j):
        return remote(relay.at[2, j], far_q.at[j], rsend_sem.at[2, j], qrecv_sem.at[j], at(-3))

    def out_copy(j):
        return remote(far_out.at[j], back.at[j], osend_sem.at[j], orecv_sem.at[j], at(1))

    def after(kv, c):
        return remote(
            near.at[3, kv, c], near.at[1, kv, c], hsend_sem.at[kv, c], recv_sem.at[1, kv, c], at(-3)
        )

    def beside(kv, j):
        return remote(
            near.at[1, kv, moved_chunk(j)], side.at[0, kv, j], xsend_sem.at[kv, j], xrecv_sem.at[0, kv, j], at(2)
        )

    def before(kv, j):
        return remote(
            block(kv, moved_chunk(j)), side.at[1, kv, j], xsend_sem.at[kv, j], xrecv_sem.at[1, kv, j], at(3)
        )

    def far_bias_copy():
        return remote(bias_ref, far_bias, bsend_sem.at[4], brecv_sem.at[4], at(-1))

    off = jnp.logical_not
    plain_next, plain_prev = time < last, time > 0
    plain_down = (row == 1) & (time == last)
    both = (0, 1)
    always, never = (lambda j: None), (lambda j: False)
    every = (always, always)
    moved = ((lambda j: j == 0), (lambda j: j < pairs - 1))
    kept = ((lambda j: j > 0), (lambda j: j == pairs - 1))
    relayed = (always, lambda j: lax.rem(j, 2) == 0)
    unrelayed = (never, lambda j: lax.rem(j, 2) == 1)
    leading, far, handed, slow, onward = [], [], [], [], []
    if fold:
        relays = (me == 2, me == n - 2)
        plain_next = plain_next & (me < n - NR) & off(relays[0])
        plain_prev = plain_prev & (me >= NR) & off(relays[1])
        plain_down = plain_down & off(is_e)
        leading = [
            (direct, 0, is_c, both, kept),
            (to_relay, 0, is_d, (0,), relayed),
            (direct, 0, is_d, (0,), unrelayed),
            (direct, 0, is_d, (1,), every),
            (direct, 2, is_e, both, kept),
        ]
        far = [(direct, 1, is_b, both, every)]
        handed = [(to_relay, 3, is_a, both, every)]
        slow = [(direct, 0, relays[0], both, every), (direct, 1, relays[1], both, every)]
        onward = [
            (from_relay, 3, me == 2, both, every),
            (from_relay, 0, me == n - 2, (0,), relayed),
        ]
    paced = (row == NR - 1) | is_e if fold else row == NR - 1
    early = [
        (direct, 0, plain_next & (row > 0), both, every),
        (direct, 1, plain_prev & off(paced), both, every),
        (direct, 2, plain_down, both, every),
    ]
    calm = [
        (direct, 1, plain_prev & paced, both, every),
        (direct, 0, plain_next & (row == 0), both, every),
    ]
    late = [(direct, 3, (row == 2) & (time == 0), both, every)]
    carries = (row == 2) & (time < last)
    forwards = [(0, (row == 1) & (time > 0)), (1, carries & off(is_c) if fold else carries)]

    def when(condition, act):
        pl.when(condition)(act)

    def send_pair(sends, j, act):
        for o in range(2):
            c = 2 * j + o
            for make, d, condition, kinds, which in sends:
                only = which[o](j)
                if only is False:
                    continue
                if only is not None:
                    condition = condition & only

                def go(make=make, d=d, kinds=kinds, c=c):
                    for kv in kinds:
                        act(make(d, kv, c))

                when(condition, go)
            i = j + o
            if sends is handed and fold:
                @pl.when(is_a & moved[o](j))
                def _(i=i):
                    @pl.when(lax.rem(i, 2) == 1)
                    def _():
                        act(q_direct(i))

                    @pl.when(lax.rem(i, 2) == 0)
                    def _():
                        act(q_to_relay(i))

            if sends is early and fold:
                @pl.when(is_c & moved[o](j))
                def _(i=i):
                    act(before(0, i))
                    act(before(1, i))

    def pass_on(j):
        for o in range(2):
            c = 2 * j + o
            for make, d, condition, kinds, which in onward:
                only = which[o](j)
                if only is not None:
                    condition = condition & only

                @pl.when(condition)
                def _(make=make, d=d, kinds=kinds, c=c):
                    for kv in kinds:
                        to_relay(d, kv, c).wait_recv()
                        make(d, kv, c).start()

            @pl.when((me == 2) & moved[o](j) & (lax.rem(j + o, 2) == 0))
            def _(i=j + o):
                q_to_relay(i).wait_recv()
                q_from_relay(i).start()

    def pass_pair(j):
        if fold:
            @pl.when(j < pairs)
            def _():
                pass_on(j)
                send_pair(slow, j, start)

    def start(copy):
        copy.start()

    def wait_send(copy):
        copy.wait_send()

    bias_sends = (has[1], has[0], has[3], has[2])
    for d in range(4):
        @pl.when(bias_sends[d])
        def _(d=d):
            bias_copy(d).start()

    text_chunks = chunks // 2
    first = core * text_chunks

    def start_sibling(i, _):
        c = lax.rem((1 - core) * text_chunks + i, chunks)
        for d, condition in ((2, even), (3, odd)):
            @pl.when(condition)
            def _(d=d):
                direct(d, 0, c).start()
                direct(d, 1, c).start()
        return 0

    def start_pairs(sends, low, high):
        def go(j, _):
            send_pair(sends, j, start)
            return 0

        if sends and high > low:
            lax.fori_loop(low, high, go, 0)

    far_ahead, handed_ahead, passed = min(2, pairs), min(3, pairs), text_chunks // 2
    start_pairs(leading, 0, min(2, pairs))
    start_pairs(early, 0, 1)
    start_pairs(far, 0, 1)
    start_pairs(handed, 0, 1)
    lax.fori_loop(0, chunks, start_sibling, 0)
    for j in range(1, ahead):
        start_pairs(leading, j + 1, min(j + 2, pairs))
        start_pairs(early, j, j + 1)
    start_pairs(far, 1, far_ahead)
    start_pairs(handed, 1, handed_ahead)

    def missing(d):
        near_bias[d] = jnp.full(near_bias.shape[1:], NEG, jnp.float32)

        def clear(c, _):
            near[d, 0, c] = jnp.zeros(near.shape[3:], jnp.bfloat16)
            near[d, 1, c] = jnp.zeros(near.shape[3:], jnp.bfloat16)
            return 0

        lax.fori_loop(0, chunks, clear, 0)

    for d in range(4):
        @pl.when(off(has[d]))
        def _(d=d):
            missing(d)

        @pl.when(has[d])
        def _(d=d):
            bias_copy(d).wait_recv()

    codes = []
    for t in range(tiles):
        found = []
        for i in range(window_ref.shape[1]):
            w = window_ref[t, i]
            found.append(w + jnp.where(w >= 1, 1, 0))
        codes.append(found)
    for b in range(5):
        for t in range(tiles):
            pick = jnp.zeros((8, tokens), jnp.int32)
            for s in range(tiles):
                want = 3 * b + s - t + 1
                if want == 1:
                    hits = jnp.int32(1)
                elif 3 * b <= want < 3 * b + 3:
                    hits = functools.reduce(
                        jnp.add, [jnp.where(e == want, 1, 0) for e in codes[t]]
                    )
                else:
                    hits = jnp.int32(0)
                pick = jnp.where((lane >= s * tok) & (lane < (s + 1) * tok), hits, pick)
            extra = own_ref[...] if b == 0 else near_bias[b - 1]
            total = jnp.where(pick > 0, 0.0, NEG) + extra
            bias_ref[b, t:t + 1, :] = total[0:1]
    text_lane = lax.broadcasted_iota(jnp.int32, (8, text), 1)
    bias_ref[5] = jnp.where(text_lane < tcount_ref[0], 0.0, NEG)
    if fold:
        @pl.when(is_a)
        def _():
            far_bias_copy().start()
    rows = lax.broadcasted_iota(jnp.int32, (tokens, HD), 0)
    limit = jnp.full((tokens, HD), counts_ref[0], jnp.int32)
    for s in range(1, tiles):
        limit = jnp.where(rows >= s * tok, counts_ref[s], limit)
    qv_ref[...] = jnp.where(lax.rem(rows, tok) < limit, 1.0, 0.0)

    lanes = lax.broadcasted_iota(jnp.int32, (share, 128), 1)
    tstat[...] = jnp.zeros_like(tstat)
    pair_slot = 3 - lax.rem(row, 2)

    def sibling_arrived(c):
        for d, condition in ((3, even), (2, odd)):
            @pl.when(condition)
            def _(d=d):
                direct(d, 0, c).wait_recv()
                direct(d, 1, c).wait_recv()

    for copy in loads[:3]:
        copy.wait()

    def text_part(j, _):
        c = first + j
        sibling_arrived(c)
        for h in range(PER):
            cols = pl.ds(pl.multiple_of(c * WIDTH + h * HD, HD), HD)
            here = slice(h * HD, (h + 1) * HD)
            to = pl.ds(pl.multiple_of(j * WIDTH + h * HD, HD), HD)
            q = tq_ref[:, cols]
            s0 = lax.dot_general(q, k_ref[:, cols], NT, preferred_element_type=jnp.float32)
            s1 = lax.dot_general(
                q, near[pair_slot, 0, c, :, here], NT, preferred_element_type=jnp.float32
            )
            s0 = s0 + own_ref[0:1, :]
            s1 = s1 + near_bias[pair_slot, 0:1, :]
            top = jnp.max(jnp.maximum(s0, s1), axis=1, keepdims=True)
            p0 = jnp.exp2((s0 - top) * LOG2E_SCALE)
            p1 = jnp.exp2((s1 - top) * LOG2E_SCALE)
            total = jnp.sum(p0 + p1, axis=1, keepdims=True)
            num = None
            for p, value in ((p0, v_ref[:, cols]), (p1, near[pair_slot, 1, c, :, here])):
                wide = p * 65537.0
                high = wide - (wide - p)
                for part in (high, p - high):
                    term = jnp.dot(
                        part.astype(jnp.bfloat16), value, preferred_element_type=jnp.float32
                    )
                    num = term if num is None else num + term
            head = j * PER + h
            for b in range(n):
                y, k = (b // 2) % 2, (b // 4) * 2 + b % 2
                part = slice(b * share, (b + 1) * share)
                tnum[y, k, :, to] = num[part]
                stat = jnp.where(lanes == head, top[part], tstat[y, k])
                tstat[y, k] = jnp.where(lanes == head + 64, total[part], stat)

        if fold:
            @pl.when(lax.rem(j, 2) == 1)
            def _():
                pass_pair(lax.div(j, 2))
        return 0

    lax.fori_loop(0, text_chunks, text_part, 0)

    partner = at(2 - 4 * line)

    def y_copies(there):
        return (
            remote(tnum.at[there], ynum, ysend_sem.at[0], yrecv_sem.at[0], partner),
            remote(tstat.at[there], ystat, ysend_sem.at[1], yrecv_sem.at[1], partner),
        )

    for copy in y_copies(1 - line):
        copy.start()
    start_pairs(handed, handed_ahead, pairs)
    start_pairs(calm, 0, min(1, pairs))
    start_pairs(late, 0, 1)

    peers = n // 2
    my_peer = lax.div(me, 4) * 2 + core
    heads = snum.shape[2] // HD

    def z_copies(i, there, here):
        k = lax.rem(my_peer + i, peers)
        to = lax.div(k, 2) * 4 + 2 * line + lax.rem(k, 2)
        source = k if there is None else there
        target = my_peer if here is None else here
        return (
            remote(snum.at[source], rnum.at[target], zsend_sem.at[0, i], zrecv_sem.at[0, i], to),
            remote(sstat.at[source], rstat.at[target], zsend_sem.at[1, i], zrecv_sem.at[1, i], to),
        )

    def whole_copy():
        return remote(
            ynum.at[my_peer + 1 - 2 * core], fnum, ysend_sem.at[2], yrecv_sem.at[2], at(1 - 2 * core)
        )

    def text_exchange():
        for copy in y_copies(1 - line):
            copy.wait_recv()

        def combine(k, _):
            mine, theirs = tstat[line, k], ystat[k]
            top = jnp.maximum(mine, theirs)
            one = jnp.exp2((mine - top) * LOG2E_SCALE)
            two = jnp.exp2((theirs - top) * LOG2E_SCALE)
            den = one * jnp.roll(mine, 64, axis=1) + two * jnp.roll(theirs, 64, axis=1)
            sstat[k] = jnp.where(lanes < 64, top, jnp.roll(den, 64, axis=1))
            for h in range(heads):
                cols = slice(h * HD, (h + 1) * HD)
                num = tnum[line, k, :, cols] * one[:, h:h + 1] + ynum[k, :, cols] * two[:, h:h + 1]
                ynum[k, :, cols] = num
                snum[k, :, cols] = num.astype(jnp.bfloat16)
            return 0

        lax.fori_loop(0, peers, combine, 0)

        def start_z(i, _):
            for copy in z_copies(i, None, None):
                copy.start()
            return 0

        whole_copy().start()
        lax.fori_loop(1, peers, start_z, 0)
        start_pairs(leading, min(ahead + 1, pairs), pairs)
        start_pairs(early, ahead, pairs)
        rnum[my_peer] = snum[my_peer]
        rstat[my_peer] = sstat[my_peer]

    row_ids = me * share + lax.broadcasted_iota(jnp.int32, (share, HD), 0)
    row_valid = row_ids < jnp.full((share, HD), tcount_ref[0], jnp.int32)

    def value(i, e, cols):
        sent = rnum[2 * i + e, :, cols].astype(jnp.float32)
        own = jnp.where(core == e, ynum[my_peer, :, cols], fnum[:, cols])
        return jnp.where(i == lax.div(me, 4), own, sent)

    def text_finish():
        def arrived(i, _):
            for copy in z_copies(i, None, None):
                copy.wait_send()
                copy.wait_recv()
            return 0

        lax.fori_loop(1, peers, arrived, 0)
        whole_copy().wait_send()
        whole_copy().wait_recv()
        for e in range(2):
            top = lax.fori_loop(
                1, peers // 2, lambda i, m: jnp.maximum(m, rstat[2 * i + e]), rstat[e]
            )

            def add(i, carry):
                den, nums = carry
                stat = rstat[2 * i + e]
                scale = jnp.exp2((stat - top) * LOG2E_SCALE)
                den = den + scale * jnp.roll(stat, 64, axis=1)
                nums = tuple(
                    nums[j] + value(i, e, slice(j * HD, (j + 1) * HD)) * scale[:, j:j + 1]
                    for j in range(heads)
                )
                return den, nums

            zeros = jnp.zeros((share, HD), jnp.float32)
            den, nums = lax.fori_loop(0, peers // 2, add, (zeros, (zeros,) * heads))
            for j in range(heads):
                result = jnp.where(row_valid, nums[j] / den[:, j:j + 1], 0.0)
                at_head = (e * heads + j) * HD
                tout_ref[:, at_head:at_head + HD] = result.astype(jnp.bfloat16)
        text_stored.start()

    def rest_arrived(i, _):
        sibling_arrived(lax.rem(first + text_chunks + i, chunks))
        return 0

    lax.fori_loop(0, chunks - text_chunks, rest_arrived, 0)
    for copy in loads[3:]:
        copy.wait()

    def stored(c):
        return pltpu.make_async_copy(
            out_ref.at[:, columns(c)], out_hbm.at[:, columns(c)], store_sem.at[c]
        )

    text_stored = pltpu.make_async_copy(tout_ref, tout_hbm, store_sem.at[chunks])

    hands0, hands1 = forwards[0][1], forwards[1][1]
    if fold:
        hands1 = hands1 | is_d

    def arrive(j, o):
        c = 2 * j + o
        for d, condition in forwards:
            @pl.when(condition)
            def _(d=d):
                for kv in range(2):
                    direct(d, kv, c).wait_recv()
                    forward(d, kv, c).start()
        if fold:
            @pl.when(is_d)
            def _():
                for kv in range(2):
                    direct(1, kv, c).wait_recv()

                    @pl.when(moved[o](j))
                    def _(kv=kv):
                        beside(kv, j + o).start()

            @pl.when(is_e)
            def _():
                for kv in range(2):
                    direct(3, kv, c).wait_recv()
                    after(kv, c).start()

    def attend(j, o):
        c = 2 * j + o
        if fold:
            @pl.when(is_e & moved[o](j))
            def _(i=j + o):
                @pl.when(i == 0)
                def _():
                    far_bias_copy().wait_recv()

                q_direct(i).wait_recv()
                for kv in range(2):
                    beside(kv, i).wait_recv()
                    before(kv, i).wait_recv()
                for h in range(PER):
                    cols = pl.ds(pl.multiple_of(c * WIDTH + h * HD, HD), HD)
                    here = slice(h * HD, (h + 1) * HD)
                    blocks = [
                        (near[3, 0, c, :, here], near[3, 1, c, :, here], far_bias.at[0]),
                        (side[1, 0, i, :, here], side[1, 1, i, :, here], far_bias.at[1]),
                        (k_ref[:, cols], v_ref[:, cols], far_bias.at[3]),
                        (side[0, 0, i, :, here], side[0, 1, i, :, here], far_bias.at[4]),
                        (tk_ref[:, cols], tv_ref[:, cols], far_bias.at[5]),
                    ]
                    result = softmax_block(far_q[i, :, here], blocks, half)
                    far_out[i, :, here] = result.astype(jnp.bfloat16)
                out_copy(i).start()

        skip = is_a & moved[o](j) if fold else None
        awaited = [
            (0, has[0] & off(hands0)), (1, has[1] & off(hands1)),
            (2, has[2] & even), (3, has[3] & odd & off(is_e) if fold else has[3] & odd),
        ]
        for d, condition in awaited:
            @pl.when(condition if skip is None or d % 2 else condition & off(skip))
            def _(d=d):
                direct(d, 0, c).wait_recv()
                direct(d, 1, c).wait_recv()

        def mine():
            for h in range(PER):
                cols = pl.ds(pl.multiple_of(c * WIDTH + h * HD, HD), HD)
                here = slice(h * HD, (h + 1) * HD)
                blocks = [(k_ref[:, cols], v_ref[:, cols], bias_ref.at[0])]
                for d in range(4):
                    blocks.append((near[d, 0, c, :, here], near[d, 1, c, :, here], bias_ref.at[d + 1]))
                blocks.append((tk_ref[:, cols], tv_ref[:, cols], bias_ref.at[5]))
                result = softmax_block(q_ref[:, cols], blocks, half)
                out_ref[:, cols] = jnp.where(qv_ref[...] > 0, result, 0.0).astype(jnp.bfloat16)
            stored(c).start()

        if skip is None:
            mine()
        else:
            pl.when(off(skip))(mine)

    def take(j):
        @pl.when(is_a)
        def _():
            out_copy(j).wait_recv()
            for h in range(PER):
                cols = pl.ds(pl.multiple_of(moved_chunk(j) * WIDTH + h * HD, HD), HD)
                result = back[j, :, h * HD:(h + 1) * HD].astype(jnp.float32)
                out_ref[:, cols] = jnp.where(qv_ref[...] > 0, result, 0.0).astype(jnp.bfloat16)
            stored(moved_chunk(j)).start()

    def finish(j):
        for sends in (leading, early, calm, far, handed, slow, late):
            send_pair(sends, j, wait_send)
        send_pair(onward, j, wait_send)
        for o in range(2):
            c = 2 * j + o
            for d, condition in ((2, even), (3, odd)):
                @pl.when(condition)
                def _(d=d, c=c):
                    direct(d, 0, c).wait_send()
                    direct(d, 1, c).wait_send()
            for d, condition in forwards:
                @pl.when(condition)
                def _(d=d, c=c):
                    forward(d, 0, c).wait_send()
                    forward(d, 1, c).wait_send()
        if fold:
            @pl.when((me == 2) & (lax.rem(j, 2) == 0))
            def _():
                q_from_relay(j).wait_send()

            @pl.when(is_e)
            def _():
                out_copy(j).wait_send()
                for o in range(2):
                    after(0, 2 * j + o).wait_send()
                    after(1, 2 * j + o).wait_send()

            @pl.when(is_d)
            def _():
                beside(0, j).wait_send()
                beside(1, j).wait_send()

    def step(j, _):
        if fold:
            @pl.when(j + far_ahead < pairs)
            def _():
                send_pair(far, j + far_ahead, start)

        @pl.when(j + 1 < pairs)
        def _():
            send_pair(calm, j + 1, start)

        @pl.when(j + 1 < pairs)
        def _():
            send_pair(late, j + 1, start)

        arrive(j, 1)
        attend(j, 0)

        @pl.when(j + 1 < pairs)
        def _():
            arrive(j + 1, 0)

        @pl.when(j > 1)
        def _():
            finish(j - 2)

        @pl.when(j == pairs - 1)
        def _():
            finish(pairs - 2)

        attend(j, 1)

        if fold:
            pass_pair(j + passed)

            @pl.when(j == 1)
            def _():
                take(0)

            @pl.when(j > 0)
            def _():
                take(j)

        @pl.when(j == min(1, pairs - 1))
        def _():
            text_exchange()

        @pl.when(j == pairs - 2)
        def _():
            text_finish()
        return 0

    arrive(jnp.int32(0), 0)
    lax.fori_loop(0, pairs, step, 0)

    def stores(c, _):
        stored(c).wait()
        return 0

    lax.fori_loop(0, chunks, stores, 0)
    text_stored.wait()

    for d in range(4):
        @pl.when(bias_sends[d])
        def _(d=d):
            bias_copy(d).wait_send()
    for copy in y_copies(1 - line):
        copy.wait_send()

    def finish_rest(j, _):
        finish(j)
        return 0

    lax.fori_loop(pairs - 1, pairs, finish_rest, 0)
    if fold:
        @pl.when(is_a)
        def _():
            far_bias_copy().wait_send()


def hand_over(video_ref, text_ref, video_out, text_out, video_part, text_part, sem):
    rows = video_ref.shape[0] // PARTS
    parts = [pl.ds(i * rows, rows) for i in range(PARTS)]
    into = [pltpu.make_async_copy(video_ref.at[p], video_part.at[p], sem.at[0, i]) for i, p in enumerate(parts)]
    onto = [pltpu.make_async_copy(video_part.at[p], video_out.at[p], sem.at[1, i]) for i, p in enumerate(parts)]
    into.append(pltpu.make_async_copy(text_ref, text_part, sem.at[0, PARTS]))
    onto.append(pltpu.make_async_copy(text_part, text_out, sem.at[1, PARTS]))
    for copy in into:
        copy.start()
    for first, second in zip(into, onto):
        first.wait()
        second.start()
    for copy in onto:
        copy.wait()


def per_device(video_q, video_k, video_v, text_q, text_k, text_v, window, counts, text_count):
    n = lax.axis_size("tiles")
    tokens, width = video_q.shape
    text = text_q.shape[0]
    share = text // n
    chunks = width // WIDTH
    pairs = chunks // 2
    peers = n // 2
    fold = n // 2 + NR + NR // 2 == n - 2
    smem = pl.BlockSpec(memory_space=pltpu.SMEM)
    hbm = pl.BlockSpec(memory_space=pl.ANY)
    dma = pltpu.SemaphoreType.DMA
    bf16, f32 = jnp.bfloat16, jnp.float32
    block = (tokens, WIDTH)
    video_out, text_out = pl.pallas_call(
        functools.partial(main_kernel, n, fold),
        out_shape=(
            jax.ShapeDtypeStruct((tokens, width), bf16),
            jax.ShapeDtypeStruct((share, width), bf16),
        ),
        in_specs=[hbm] * 6 + [smem] * 3,
        out_specs=(hbm, hbm),
        scratch_shapes=[
            pltpu.VMEM((tokens, width), bf16),
            pltpu.VMEM((share, width), bf16),
            *[pltpu.VMEM((tokens, width), bf16)] * 3,
            *[pltpu.VMEM((text, width), bf16)] * 3,
            pltpu.VMEM((8, tokens), f32),
            pltpu.VMEM((6, 8, tokens), f32),
            pltpu.VMEM((tokens, HD), f32),
            pltpu.VMEM((4, 2, chunks, *block), bf16),
            pltpu.VMEM((4, 8, tokens), f32),
            pltpu.VMEM((3, chunks, *block), bf16),
            pltpu.VMEM((6, 8, tokens), f32),
            pltpu.VMEM((pairs, *block), bf16),
            pltpu.VMEM((2, 2, pairs, *block), bf16),
            pltpu.VMEM((pairs, *block), bf16),
            pltpu.VMEM((pairs, *block), bf16),
            pltpu.VMEM((2, peers, share, width // 2), f32),
            pltpu.VMEM((2, peers, share, 128), f32),
            pltpu.VMEM((peers, share, width // 2), f32),
            pltpu.VMEM((peers, share, 128), f32),
            pltpu.VMEM((peers, share, width // 2), bf16),
            pltpu.VMEM((peers, share, 128), f32),
            pltpu.VMEM((peers, share, width // 2), bf16),
            pltpu.VMEM((peers, share, 128), f32),
            pltpu.VMEM((share, width // 2), f32),
            dma((6,)),
            dma((4, 2, chunks)),
            dma((4, 2, chunks)),
            dma((5,)),
            dma((5,)),
            dma((2, chunks)),
            dma((2, chunks)),
            dma((3, chunks)),
            dma((3, chunks)),
            dma((pairs,)),
            dma((pairs,)),
            dma((2, pairs)),
            dma((2, 2, pairs)),
            dma((pairs,)),
            dma((pairs,)),
            dma((3,)),
            dma((3,)),
            dma((2, peers)),
            dma((2, peers)),
            dma((chunks + 1,)),
        ],
        compiler_params=pltpu.CompilerParams(
            collective_id=0, has_side_effects=True, vmem_limit_bytes=56 * 1024 * 1024
        ),
    )(video_q, video_k, video_v, text_q, text_k, text_v, window, counts, text_count)
    return pl.pallas_call(
        hand_over,
        out_shape=(
            jax.ShapeDtypeStruct((tokens, width), bf16),
            jax.ShapeDtypeStruct((share, width), bf16),
        ),
        in_specs=[hbm] * 2,
        out_specs=(hbm, hbm),
        scratch_shapes=[
            pltpu.VMEM((tokens, width), bf16),
            pltpu.VMEM((share, width), bf16),
            dma((2, PARTS + 1)),
        ],
    )(video_out, text_out)


def solution(mesh):
    return jax.shard_map(
        per_device,
        mesh=mesh,
        in_specs=(
            P(("groups", "tiles"), None),
            P(("groups", "tiles"), None),
            P(("groups", "tiles"), None),
            P("groups", None),
            P("groups", None),
            P("groups", None),
            P("tiles", None),
            P(("groups", "tiles")),
            P("groups"),
        ),
        out_specs=(P(("groups", "tiles"), None), P(("groups", "tiles"), None)),
        check_vma=False,
    )
```

```python
import functools
import math

import jax
import jax.numpy as jnp
from jax import lax
from jax.experimental import pallas as pl
from jax.experimental.pallas import tpu as pltpu
from jax.sharding import PartitionSpec as P

HD = 128
NR = 4
WIDTH = 256
PER = WIDTH // HD
AHEAD = 4
PARTS = 8
LOG2E_SCALE = math.log2(math.e) / math.sqrt(HD)
MESH = pl.DeviceIdType.MESH
NT = (((1,), (1,)), ((), ()))
NEG = -jnp.inf


def softmax_block(q, blocks, half):
    scores = []
    for key, _, bias in blocks:
        s = lax.dot_general(q, key, NT, preferred_element_type=jnp.float32)
        scores.append(
            jnp.concatenate([s[:half] + bias[0:1, :], s[half:] + bias[1:2, :]], axis=0)
        )
    top = functools.reduce(jnp.maximum, scores)
    top = jnp.max(top, axis=1, keepdims=True)
    total, num = None, None
    for s, (_, value, _) in zip(scores, blocks):
        p = jnp.exp2((s - top) * LOG2E_SCALE)
        total = p if total is None else total + p
        term = jnp.dot(p.astype(jnp.bfloat16), value, preferred_element_type=jnp.float32)
        num = term if num is None else num + term
    return num / jnp.sum(total, axis=1, keepdims=True)


def main_kernel(
    n, fold,
    q_hbm, k_hbm, v_hbm, tq_hbm, tk_hbm, tv_hbm, window_ref, counts_ref, tcount_ref,
    out_hbm, tout_hbm,
    out_ref, tout_ref, q_ref, k_ref, v_ref, tq_ref, tk_ref, tv_ref,
    own_ref, bias_ref, qv_ref, near, near_bias,
    relay, far_bias, far_q, side, far_out, back,
    tnum, tstat, ynum, ystat, snum, sstat, rnum, rstat, fnum,
    load_sem, send_sem, recv_sem, bsend_sem, brecv_sem, fsend_sem, hsend_sem, rsend_sem, rrecv_sem,
    qsend_sem, qrecv_sem, xsend_sem, xrecv_sem, osend_sem, orecv_sem,
    ysend_sem, yrecv_sem, zsend_sem, zrecv_sem, store_sem,
):
    group = lax.axis_index("groups")
    me = lax.axis_index("tiles")
    last = n // NR - 1
    tokens, width = q_hbm.shape
    chunks = width // WIDTH
    pairs = chunks // 2
    tiles = counts_ref.shape[0]
    tok = tokens // tiles
    half = tokens // 2
    share = tout_ref.shape[0]
    text = tq_hbm.shape[0]
    ahead = min(AHEAD, pairs)

    def at(offset):
        return lax.rem(me + offset + n, n)

    spot = lax.rem(me + n // 2 + NR + NR // 2, n)
    row = lax.rem(spot, NR)
    time = lax.div(spot, NR)
    core = lax.rem(me, 2)
    line = lax.rem(lax.div(me, 2), 2)
    has = (time > 0, time < last, row > 0, row < NR - 1)
    offs = (-NR, NR, -1, 1)
    even = lax.rem(row, 2) == 0
    odd = lax.rem(row, 2) == 1
    is_a = (me == 0) if fold else None
    is_b = (me == 1) if fold else None
    is_c = (me == n - 4) if fold else None
    is_d = (me == n - 3) if fold else None
    is_e = (me == n - 1) if fold else None

    barrier = pltpu.get_barrier_semaphore()

    def greet(i, _):
        pl.semaphore_signal(barrier, inc=1, device_id=(group, at(i)), device_id_type=MESH)
        return 0

    lax.fori_loop(1, n, greet, 0)

    loads = [
        pltpu.make_async_copy(source, target, load_sem.at[i])
        for i, (source, target) in enumerate((
            (k_hbm, k_ref), (tq_hbm, tq_ref), (v_hbm, v_ref),
            (q_hbm, q_ref), (tk_hbm, tk_ref), (tv_hbm, tv_ref),
        ))
    ]
    for copy in loads:
        copy.start()

    lane = lax.broadcasted_iota(jnp.int32, (8, tokens), 1)
    slot = lax.rem(lane, tok)
    count = jnp.full((8, tokens), counts_ref[0], jnp.int32)
    for s in range(1, tiles):
        count = jnp.where(lane >= s * tok, counts_ref[s], count)
    own_ref[...] = jnp.where(slot < count, 0.0, NEG)

    pl.semaphore_wait(barrier, n - 1)

    def remote(source, target, sent, got, to):
        return pltpu.make_async_remote_copy(
            src_ref=source, dst_ref=target, send_sem=sent, recv_sem=got,
            device_id=(group, to), device_id_type=MESH,
        )

    def columns(c):
        return pl.ds(pl.multiple_of(c * WIDTH, WIDTH), WIDTH)

    def block(kv, c):
        return (k_hbm, v_hbm)[kv].at[:, columns(c)]

    def bias_copy(d):
        return remote(own_ref, near_bias.at[d], bsend_sem.at[d], brecv_sem.at[d], at(-offs[d]))

    def direct(d, kv, c):
        return remote(
            block(kv, c), near.at[d, kv, c], send_sem.at[d, kv, c], recv_sem.at[d, kv, c], at(-offs[d])
        )

    def to_relay(d, kv, c):
        return remote(
            block(kv, c), relay.at[kv, c], send_sem.at[d, kv, c], rrecv_sem.at[kv, c],
            at(2 if d == 3 else 1),
        )

    def from_relay(d, kv, c):
        return remote(
            relay.at[kv, c], near.at[d, kv, c], rsend_sem.at[kv, c], recv_sem.at[d, kv, c],
            at(-3 if d == 3 else 3),
        )

    def forward(d, kv, c):
        slot, to = (2, at(1 - NR)) if d == 0 else (3, at(NR - 1))
        return remote(
            near.at[d, kv, c], near.at[slot, kv, c], fsend_sem.at[kv, c], recv_sem.at[slot, kv, c], to
        )

    def moved_chunk(i):
        return jnp.maximum(2 * i - 1, 0)

    def q_direct(j):
        return remote(
            q_hbm.at[:, columns(moved_chunk(j))], far_q.at[j], qsend_sem.at[j], qrecv_sem.at[j], at(-1)
        )

    def q_to_relay(j):
        return remote(
            q_hbm.at[:, columns(moved_chunk(j))], relay.at[2, j], qsend_sem.at[j], rrecv_sem.at[2, j], at(2)
        )

    def q_from_relay(j):
        return remote(relay.at[2, j], far_q.at[j], rsend_sem.at[2, j], qrecv_sem.at[j], at(-3))

    def out_copy(j):
        return remote(far_out.at[j], back.at[j], osend_sem.at[j], orecv_sem.at[j], at(1))

    def after(kv, c):
        return remote(
            near.at[3, kv, c], near.at[1, kv, c], hsend_sem.at[kv, c], recv_sem.at[1, kv, c], at(-3)
        )

    def beside(kv, j):
        return remote(
            near.at[1, kv, moved_chunk(j)], side.at[0, kv, j], xsend_sem.at[kv, j], xrecv_sem.at[0, kv, j], at(2)
        )

    def before(kv, j):
        return remote(
            block(kv, moved_chunk(j)), side.at[1, kv, j], xsend_sem.at[kv, j], xrecv_sem.at[1, kv, j], at(3)
        )

    def far_bias_copy():
        return remote(bias_ref, far_bias, bsend_sem.at[4], brecv_sem.at[4], at(-1))

    off = jnp.logical_not
    plain_next, plain_prev = time < last, time > 0
    plain_down = (row == 1) & (time == last)
    both = (0, 1)
    always, never = (lambda j: None), (lambda j: False)
    every = (always, always)
    moved = ((lambda j: j == 0), (lambda j: j < pairs - 1))
    kept = ((lambda j: j > 0), (lambda j: j == pairs - 1))
    relayed = (always, lambda j: lax.rem(j, 2) == 0)
    unrelayed = (never, lambda j: lax.rem(j, 2) == 1)
    leading, far, handed, slow, onward = [], [], [], [], []
    if fold:
        relays = (me == 2, me == n - 2)
        plain_next = plain_next & (me < n - NR) & off(relays[0])
        plain_prev = plain_prev & (me >= NR) & off(relays[1])
        plain_down = plain_down & off(is_e)
        leading = [
            (direct, 0, is_c, both, kept),
            (to_relay, 0, is_d, (0,), relayed),
            (direct, 0, is_d, (0,), unrelayed),
            (direct, 0, is_d, (1,), every),
            (direct, 2, is_e, both, kept),
        ]
        far = [(direct, 1, is_b, both, every)]
        handed = [(to_relay, 3, is_a, both, every)]
        slow = [(direct, 0, relays[0], both, every), (direct, 1, relays[1], both, every)]
        onward = [
            (from_relay, 3, me == 2, both, every),
            (from_relay, 0, me == n - 2, (0,), relayed),
        ]
    paced = (row == NR - 1) | is_e if fold else row == NR - 1
    early = [
        (direct, 0, plain_next & (row > 0), both, every),
        (direct, 1, plain_prev & off(paced), both, every),
        (direct, 2, plain_down, both, every),
    ]
    calm = [
        (direct, 1, plain_prev & paced, both, every),
        (direct, 0, plain_next & (row == 0), both, every),
    ]
    late = [(direct, 3, (row == 2) & (time == 0), both, every)]
    carries = (row == 2) & (time < last)
    forwards = [(0, (row == 1) & (time > 0)), (1, carries & off(is_c) if fold else carries)]

    def when(condition, act):
        pl.when(condition)(act)

    def send_pair(sends, j, act):
        for o in range(2):
            c = 2 * j + o
            for make, d, condition, kinds, which in sends:
                only = which[o](j)
                if only is False:
                    continue
                if only is not None:
                    condition = condition & only

                def go(make=make, d=d, kinds=kinds, c=c):
                    for kv in kinds:
                        act(make(d, kv, c))

                when(condition, go)
            i = j + o
            if sends is handed and fold:
                @pl.when(is_a & moved[o](j))
                def _(i=i):
                    @pl.when(lax.rem(i, 2) == 1)
                    def _():
                        act(q_direct(i))

                    @pl.when(lax.rem(i, 2) == 0)
                    def _():
                        act(q_to_relay(i))

            if sends is early and fold:
                @pl.when(is_c & moved[o](j))
                def _(i=i):
                    act(before(0, i))
                    act(before(1, i))

    def pass_on(j):
        for o in range(2):
            c = 2 * j + o
            for make, d, condition, kinds, which in onward:
                only = which[o](j)
                if only is not None:
                    condition = condition & only

                @pl.when(condition)
                def _(make=make, d=d, kinds=kinds, c=c):
                    for kv in kinds:
                        to_relay(d, kv, c).wait_recv()
                        make(d, kv, c).start()

            @pl.when((me == 2) & moved[o](j) & (lax.rem(j + o, 2) == 0))
            def _(i=j + o):
                q_to_relay(i).wait_recv()
                q_from_relay(i).start()

    def pass_pair(j):
        if fold:
            @pl.when(j < pairs)
            def _():
                pass_on(j)
                send_pair(slow, j, start)

    def start(copy):
        copy.start()

    def wait_send(copy):
        copy.wait_send()

    bias_sends = (has[1], has[0], has[3], has[2])
    for d in range(4):
        @pl.when(bias_sends[d])
        def _(d=d):
            bias_copy(d).start()

    text_chunks = chunks // 2
    first = core * text_chunks

    def start_sibling(i, _):
        c = lax.rem((1 - core) * text_chunks + i, chunks)
        for d, condition in ((2, even), (3, odd)):
            @pl.when(condition)
            def _(d=d):
                direct(d, 0, c).start()
                direct(d, 1, c).start()
        return 0

    def start_pairs(sends, low, high):
        def go(j, _):
            send_pair(sends, j, start)
            return 0

        if sends and high > low:
            lax.fori_loop(low, high, go, 0)

    far_ahead, handed_ahead, passed = min(2, pairs), min(3, pairs), text_chunks // 2
    start_pairs(leading, 0, min(2, pairs))
    start_pairs(early, 0, 1)
    start_pairs(far, 0, 1)
    start_pairs(handed, 0, 1)
    lax.fori_loop(0, chunks, start_sibling, 0)
    for j in range(1, ahead):
        start_pairs(leading, j + 1, min(j + 2, pairs))
        start_pairs(early, j, j + 1)
    start_pairs(far, 1, far_ahead)
    start_pairs(handed, 1, handed_ahead)

    def missing(d):
        near_bias[d] = jnp.full(near_bias.shape[1:], NEG, jnp.float32)

        def clear(c, _):
            near[d, 0, c] = jnp.zeros(near.shape[3:], jnp.bfloat16)
            near[d, 1, c] = jnp.zeros(near.shape[3:], jnp.bfloat16)
            return 0

        lax.fori_loop(0, chunks, clear, 0)

    for d in range(4):
        @pl.when(off(has[d]))
        def _(d=d):
            missing(d)

        @pl.when(has[d])
        def _(d=d):
            bias_copy(d).wait_recv()

    codes = []
    for t in range(tiles):
        found = []
        for i in range(window_ref.shape[1]):
            w = window_ref[t, i]
            found.append(w + jnp.where(w >= 1, 1, 0))
        codes.append(found)
    for b in range(5):
        for t in range(tiles):
            pick = jnp.zeros((8, tokens), jnp.int32)
            for s in range(tiles):
                want = 3 * b + s - t + 1
                if want == 1:
                    hits = jnp.int32(1)
                elif 3 * b <= want < 3 * b + 3:
                    hits = functools.reduce(
                        jnp.add, [jnp.where(e == want, 1, 0) for e in codes[t]]
                    )
                else:
                    hits = jnp.int32(0)
                pick = jnp.where((lane >= s * tok) & (lane < (s + 1) * tok), hits, pick)
            extra = own_ref[...] if b == 0 else near_bias[b - 1]
            total = jnp.where(pick > 0, 0.0, NEG) + extra
            bias_ref[b, t:t + 1, :] = total[0:1]
    text_lane = lax.broadcasted_iota(jnp.int32, (8, text), 1)
    bias_ref[5] = jnp.where(text_lane < tcount_ref[0], 0.0, NEG)
    if fold:
        @pl.when(is_a)
        def _():
            far_bias_copy().start()
    rows = lax.broadcasted_iota(jnp.int32, (tokens, HD), 0)
    limit = jnp.full((tokens, HD), counts_ref[0], jnp.int32)
    for s in range(1, tiles):
        limit = jnp.where(rows >= s * tok, counts_ref[s], limit)
    qv_ref[...] = jnp.where(lax.rem(rows, tok) < limit, 1.0, 0.0)

    lanes = lax.broadcasted_iota(jnp.int32, (share, 128), 1)
    tstat[...] = jnp.zeros_like(tstat)
    pair_slot = 3 - lax.rem(row, 2)

    def sibling_arrived(c):
        for d, condition in ((3, even), (2, odd)):
            @pl.when(condition)
            def _(d=d):
                direct(d, 0, c).wait_recv()
                direct(d, 1, c).wait_recv()

    for copy in loads[:3]:
        copy.wait()

    def text_part(j, _):
        c = first + j
        sibling_arrived(c)
        for h in range(PER):
            cols = pl.ds(pl.multiple_of(c * WIDTH + h * HD, HD), HD)
            here = slice(h * HD, (h + 1) * HD)
            to = pl.ds(pl.multiple_of(j * WIDTH + h * HD, HD), HD)
            q = tq_ref[:, cols]
            s0 = lax.dot_general(q, k_ref[:, cols], NT, preferred_element_type=jnp.float32)
            s1 = lax.dot_general(
                q, near[pair_slot, 0, c, :, here], NT, preferred_element_type=jnp.float32
            )
            s0 = s0 + own_ref[0:1, :]
            s1 = s1 + near_bias[pair_slot, 0:1, :]
            top = jnp.max(jnp.maximum(s0, s1), axis=1, keepdims=True)
            p0 = jnp.exp2((s0 - top) * LOG2E_SCALE)
            p1 = jnp.exp2((s1 - top) * LOG2E_SCALE)
            total = jnp.sum(p0 + p1, axis=1, keepdims=True)
            num = None
            for p, value in ((p0, v_ref[:, cols]), (p1, near[pair_slot, 1, c, :, here])):
                wide = p * 65537.0
                high = wide - (wide - p)
                for part in (high, p - high):
                    term = jnp.dot(
                        part.astype(jnp.bfloat16), value, preferred_element_type=jnp.float32
                    )
                    num = term if num is None else num + term
            head = j * PER + h
            for b in range(n):
                y, k = (b // 2) % 2, (b // 4) * 2 + b % 2
                part = slice(b * share, (b + 1) * share)
                tnum[y, k, :, to] = num[part]
                stat = jnp.where(lanes == head, top[part], tstat[y, k])
                tstat[y, k] = jnp.where(lanes == head + 64, total[part], stat)

        if fold:
            @pl.when(lax.rem(j, 2) == 1)
            def _():
                pass_pair(lax.div(j, 2))
        return 0

    lax.fori_loop(0, text_chunks, text_part, 0)

    partner = at(2 - 4 * line)

    def y_copies(there):
        return (
            remote(tnum.at[there], ynum, ysend_sem.at[0], yrecv_sem.at[0], partner),
            remote(tstat.at[there], ystat, ysend_sem.at[1], yrecv_sem.at[1], partner),
        )

    for copy in y_copies(1 - line):
        copy.start()
    start_pairs(handed, handed_ahead, pairs)
    start_pairs(calm, 0, min(1, pairs))
    start_pairs(late, 0, 1)

    peers = n // 2
    my_peer = lax.div(me, 4) * 2 + core
    heads = snum.shape[2] // HD

    def z_copies(i, there, here):
        k = lax.rem(my_peer + i, peers)
        to = lax.div(k, 2) * 4 + 2 * line + lax.rem(k, 2)
        source = k if there is None else there
        target = my_peer if here is None else here
        return (
            remote(snum.at[source], rnum.at[target], zsend_sem.at[0, i], zrecv_sem.at[0, i], to),
            remote(sstat.at[source], rstat.at[target], zsend_sem.at[1, i], zrecv_sem.at[1, i], to),
        )

    def whole_copy():
        return remote(
            ynum.at[my_peer + 1 - 2 * core], fnum, ysend_sem.at[2], yrecv_sem.at[2], at(1 - 2 * core)
        )

    def text_exchange():
        for copy in y_copies(1 - line):
            copy.wait_recv()

        def combine(k, _):
            mine, theirs = tstat[line, k], ystat[k]
            top = jnp.maximum(mine, theirs)
            one = jnp.exp2((mine - top) * LOG2E_SCALE)
            two = jnp.exp2((theirs - top) * LOG2E_SCALE)
            den = one * jnp.roll(mine, 64, axis=1) + two * jnp.roll(theirs, 64, axis=1)
            sstat[k] = jnp.where(lanes < 64, top, jnp.roll(den, 64, axis=1))
            for h in range(heads):
                cols = slice(h * HD, (h + 1) * HD)
                num = tnum[line, k, :, cols] * one[:, h:h + 1] + ynum[k, :, cols] * two[:, h:h + 1]
                ynum[k, :, cols] = num
                snum[k, :, cols] = num.astype(jnp.bfloat16)
            return 0

        lax.fori_loop(0, peers, combine, 0)

        def start_z(i, _):
            for copy in z_copies(i, None, None):
                copy.start()
            return 0

        whole_copy().start()
        lax.fori_loop(1, peers, start_z, 0)
        start_pairs(leading, min(ahead + 1, pairs), pairs)
        start_pairs(early, ahead, pairs)
        rnum[my_peer] = snum[my_peer]
        rstat[my_peer] = sstat[my_peer]

    row_ids = me * share + lax.broadcasted_iota(jnp.int32, (share, HD), 0)
    row_valid = row_ids < jnp.full((share, HD), tcount_ref[0], jnp.int32)

    def value(i, e, cols):
        sent = rnum[2 * i + e, :, cols].astype(jnp.float32)
        own = jnp.where(core == e, ynum[my_peer, :, cols], fnum[:, cols])
        return jnp.where(i == lax.div(me, 4), own, sent)

    def text_finish():
        def arrived(i, _):
            for copy in z_copies(i, None, None):
                copy.wait_send()
                copy.wait_recv()
            return 0

        lax.fori_loop(1, peers, arrived, 0)
        whole_copy().wait_send()
        whole_copy().wait_recv()
        for e in range(2):
            top = lax.fori_loop(
                1, peers // 2, lambda i, m: jnp.maximum(m, rstat[2 * i + e]), rstat[e]
            )

            def add(i, carry):
                den, nums = carry
                stat = rstat[2 * i + e]
                scale = jnp.exp2((stat - top) * LOG2E_SCALE)
                den = den + scale * jnp.roll(stat, 64, axis=1)
                nums = tuple(
                    nums[j] + value(i, e, slice(j * HD, (j + 1) * HD)) * scale[:, j:j + 1]
                    for j in range(heads)
                )
                return den, nums

            zeros = jnp.zeros((share, HD), jnp.float32)
            den, nums = lax.fori_loop(0, peers // 2, add, (zeros, (zeros,) * heads))
            for j in range(heads):
                result = jnp.where(row_valid, nums[j] / den[:, j:j + 1], 0.0)
                at_head = (e * heads + j) * HD
                tout_ref[:, at_head:at_head + HD] = result.astype(jnp.bfloat16)
        text_stored.start()

    def rest_arrived(i, _):
        sibling_arrived(lax.rem(first + text_chunks + i, chunks))
        return 0

    lax.fori_loop(0, chunks - text_chunks, rest_arrived, 0)
    for copy in loads[3:]:
        copy.wait()

    def stored(c):
        return pltpu.make_async_copy(
            out_ref.at[:, columns(c)], out_hbm.at[:, columns(c)], store_sem.at[c]
        )

    text_stored = pltpu.make_async_copy(tout_ref, tout_hbm, store_sem.at[chunks])

    hands0, hands1 = forwards[0][1], forwards[1][1]
    if fold:
        hands1 = hands1 | is_d

    def arrive(j, o):
        c = 2 * j + o
        for d, condition in forwards:
            @pl.when(condition)
            def _(d=d):
                for kv in range(2):
                    direct(d, kv, c).wait_recv()
                    forward(d, kv, c).start()
        if fold:
            @pl.when(is_d)
            def _():
                for kv in range(2):
                    direct(1, kv, c).wait_recv()

                    @pl.when(moved[o](j))
                    def _(kv=kv):
                        beside(kv, j + o).start()

            @pl.when(is_e)
            def _():
                for kv in range(2):
                    direct(3, kv, c).wait_recv()
                    after(kv, c).start()

    def attend(j, o):
        c = 2 * j + o
        if fold:
            @pl.when(is_e & moved[o](j))
            def _(i=j + o):
                @pl.when(i == 0)
                def _():
                    far_bias_copy().wait_recv()

                q_direct(i).wait_recv()
                for kv in range(2):
                    beside(kv, i).wait_recv()
                    before(kv, i).wait_recv()
                for h in range(PER):
                    cols = pl.ds(pl.multiple_of(c * WIDTH + h * HD, HD), HD)
                    here = slice(h * HD, (h + 1) * HD)
                    blocks = [
                        (near[3, 0, c, :, here], near[3, 1, c, :, here], far_bias.at[0]),
                        (side[1, 0, i, :, here], side[1, 1, i, :, here], far_bias.at[1]),
                        (k_ref[:, cols], v_ref[:, cols], far_bias.at[3]),
                        (side[0, 0, i, :, here], side[0, 1, i, :, here], far_bias.at[4]),
                        (tk_ref[:, cols], tv_ref[:, cols], far_bias.at[5]),
                    ]
                    result = softmax_block(far_q[i, :, here], blocks, half)
                    far_out[i, :, here] = result.astype(jnp.bfloat16)
                out_copy(i).start()

        skip = is_a & moved[o](j) if fold else None
        awaited = [
            (0, has[0] & off(hands0)), (1, has[1] & off(hands1)),
            (2, has[2] & even), (3, has[3] & odd & off(is_e) if fold else has[3] & odd),
        ]
        for d, condition in awaited:
            @pl.when(condition if skip is None or d % 2 else condition & off(skip))
            def _(d=d):
                direct(d, 0, c).wait_recv()
                direct(d, 1, c).wait_recv()

        def mine():
            for h in range(PER):
                cols = pl.ds(pl.multiple_of(c * WIDTH + h * HD, HD), HD)
                here = slice(h * HD, (h + 1) * HD)
                blocks = [(k_ref[:, cols], v_ref[:, cols], bias_ref.at[0])]
                for d in range(4):
                    blocks.append((near[d, 0, c, :, here], near[d, 1, c, :, here], bias_ref.at[d + 1]))
                blocks.append((tk_ref[:, cols], tv_ref[:, cols], bias_ref.at[5]))
                result = softmax_block(q_ref[:, cols], blocks, half)
                out_ref[:, cols] = jnp.where(qv_ref[...] > 0, result, 0.0).astype(jnp.bfloat16)
            stored(c).start()

        if skip is None:
            mine()
        else:
            pl.when(off(skip))(mine)

    def take(j):
        @pl.when(is_a)
        def _():
            out_copy(j).wait_recv()
            for h in range(PER):
                cols = pl.ds(pl.multiple_of(moved_chunk(j) * WIDTH + h * HD, HD), HD)
                result = back[j, :, h * HD:(h + 1) * HD].astype(jnp.float32)
                out_ref[:, cols] = jnp.where(qv_ref[...] > 0, result, 0.0).astype(jnp.bfloat16)
            stored(moved_chunk(j)).start()

    def finish(j):
        for sends in (leading, early, calm, far, handed, slow, late):
            send_pair(sends, j, wait_send)
        send_pair(onward, j, wait_send)
        for o in range(2):
            c = 2 * j + o
            for d, condition in ((2, even), (3, odd)):
                @pl.when(condition)
                def _(d=d, c=c):
                    direct(d, 0, c).wait_send()
                    direct(d, 1, c).wait_send()
            for d, condition in forwards:
                @pl.when(condition)
                def _(d=d, c=c):
                    forward(d, 0, c).wait_send()
                    forward(d, 1, c).wait_send()
        if fold:
            @pl.when((me == 2) & (lax.rem(j, 2) == 0))
            def _():
                q_from_relay(j).wait_send()

            @pl.when(is_e)
            def _():
                out_copy(j).wait_send()
                for o in range(2):
                    after(0, 2 * j + o).wait_send()
                    after(1, 2 * j + o).wait_send()

            @pl.when(is_d)
            def _():
                beside(0, j).wait_send()
                beside(1, j).wait_send()

    def step(j, _):
        if fold:
            @pl.when(j + far_ahead < pairs)
            def _():
                send_pair(far, j + far_ahead, start)

        @pl.when(j + 1 < pairs)
        def _():
            send_pair(calm, j + 1, start)

        @pl.when(j + 1 < pairs)
        def _():
            send_pair(late, j + 1, start)

        arrive(j, 1)
        attend(j, 0)

        @pl.when(j + 1 < pairs)
        def _():
            arrive(j + 1, 0)

        @pl.when(j > 1)
        def _():
            finish(j - 2)

        @pl.when(j == pairs - 1)
        def _():
            finish(pairs - 2)

        attend(j, 1)

        if fold:
            pass_pair(j + passed)

            @pl.when(j == 1)
            def _():
                take(0)

            @pl.when(j > 0)
            def _():
                take(j)

        @pl.when(j == min(1, pairs - 1))
        def _():
            text_exchange()

        @pl.when(j == pairs - 2)
        def _():
            text_finish()
        return 0

    arrive(jnp.int32(0), 0)
    lax.fori_loop(0, pairs, step, 0)

    def stores(c, _):
        stored(c).wait()
        return 0

    lax.fori_loop(0, chunks, stores, 0)
    text_stored.wait()

    for d in range(4):
        @pl.when(bias_sends[d])
        def _(d=d):
            bias_copy(d).wait_send()
    for copy in y_copies(1 - line):
        copy.wait_send()

    def finish_rest(j, _):
        finish(j)
        return 0

    lax.fori_loop(pairs - 1, pairs, finish_rest, 0)
    if fold:
        @pl.when(is_a)
        def _():
            far_bias_copy().wait_send()


def hand_over(video_ref, text_ref, video_out, text_out, video_part, text_part, sem):
    rows = video_ref.shape[0] // PARTS
    parts = [pl.ds(i * rows, rows) for i in range(PARTS)]
    into = [pltpu.make_async_copy(video_ref.at[p], video_part.at[p], sem.at[0, i]) for i, p in enumerate(parts)]
    onto = [pltpu.make_async_copy(video_part.at[p], video_out.at[p], sem.at[1, i]) for i, p in enumerate(parts)]
    into.append(pltpu.make_async_copy(text_ref, text_part, sem.at[0, PARTS]))
    onto.append(pltpu.make_async_copy(text_part, text_out, sem.at[1, PARTS]))
    for copy in into:
        copy.start()
    for first, second in zip(into, onto):
        first.wait()
        second.start()
    for copy in onto:
        copy.wait()


def per_device(video_q, video_k, video_v, text_q, text_k, text_v, window, counts, text_count):
    n = lax.axis_size("tiles")
    tokens, width = video_q.shape
    text = text_q.shape[0]
    share = text // n
    chunks = width // WIDTH
    pairs = chunks // 2
    peers = n // 2
    fold = n // 2 + NR + NR // 2 == n - 2
    smem = pl.BlockSpec(memory_space=pltpu.SMEM)
    hbm = pl.BlockSpec(memory_space=pl.ANY)
    dma = pltpu.SemaphoreType.DMA
    bf16, f32 = jnp.bfloat16, jnp.float32
    block = (tokens, WIDTH)
    video_out, text_out = pl.pallas_call(
        functools.partial(main_kernel, n, fold),
        out_shape=(
            jax.ShapeDtypeStruct((tokens, width), bf16),
            jax.ShapeDtypeStruct((share, width), bf16),
        ),
        in_specs=[hbm] * 6 + [smem] * 3,
        out_specs=(hbm, hbm),
        scratch_shapes=[
            pltpu.VMEM((tokens, width), bf16),
            pltpu.VMEM((share, width), bf16),
            *[pltpu.VMEM((tokens, width), bf16)] * 3,
            *[pltpu.VMEM((text, width), bf16)] * 3,
            pltpu.VMEM((8, tokens), f32),
            pltpu.VMEM((6, 8, tokens), f32),
            pltpu.VMEM((tokens, HD), f32),
            pltpu.VMEM((4, 2, chunks, *block), bf16),
            pltpu.VMEM((4, 8, tokens), f32),
            pltpu.VMEM((3, chunks, *block), bf16),
            pltpu.VMEM((6, 8, tokens), f32),
            pltpu.VMEM((pairs, *block), bf16),
            pltpu.VMEM((2, 2, pairs, *block), bf16),
            pltpu.VMEM((pairs, *block), bf16),
            pltpu.VMEM((pairs, *block), bf16),
            pltpu.VMEM((2, peers, share, width // 2), f32),
            pltpu.VMEM((2, peers, share, 128), f32),
            pltpu.VMEM((peers, share, width // 2), f32),
            pltpu.VMEM((peers, share, 128), f32),
            pltpu.VMEM((peers, share, width // 2), bf16),
            pltpu.VMEM((peers, share, 128), f32),
            pltpu.VMEM((peers, share, width // 2), bf16),
            pltpu.VMEM((peers, share, 128), f32),
            pltpu.VMEM((share, width // 2), f32),
            dma((6,)),
            dma((4, 2, chunks)),
            dma((4, 2, chunks)),
            dma((5,)),
            dma((5,)),
            dma((2, chunks)),
            dma((2, chunks)),
            dma((3, chunks)),
            dma((3, chunks)),
            dma((pairs,)),
            dma((pairs,)),
            dma((2, pairs)),
            dma((2, 2, pairs)),
            dma((pairs,)),
            dma((pairs,)),
            dma((3,)),
            dma((3,)),
            dma((2, peers)),
            dma((2, peers)),
            dma((chunks + 1,)),
        ],
        compiler_params=pltpu.CompilerParams(
            collective_id=0, has_side_effects=True, vmem_limit_bytes=56 * 1024 * 1024
        ),
    )(video_q, video_k, video_v, text_q, text_k, text_v, window, counts, text_count)
    return pl.pallas_call(
        hand_over,
        out_shape=(
            jax.ShapeDtypeStruct((tokens, width), bf16),
            jax.ShapeDtypeStruct((share, width), bf16),
        ),
        in_specs=[hbm] * 2,
        out_specs=(hbm, hbm),
        scratch_shapes=[
            pltpu.VMEM((tokens, width), bf16),
            pltpu.VMEM((share, width), bf16),
            dma((2, PARTS + 1)),
        ],
    )(video_out, text_out)


def solution(mesh):
    return jax.shard_map(
        per_device,
        mesh=mesh,
        in_specs=(
            P(("groups", "tiles"), None),
            P(("groups", "tiles"), None),
            P(("groups", "tiles"), None),
            P("groups", None),
            P("groups", None),
            P("groups", None),
            P("tiles", None),
            P(("groups", "tiles")),
            P("groups"),
        ),
        out_specs=(P(("groups", "tiles"), None), P(("groups", "tiles"), None)),
        check_vma=False,
    )
```
